32 devices in a mesh: tower: 4 (over y, x), dp: 8 (over z, core).
Axes of the slice: x: 2, y: 2, z: 4, core: 2. Of those that a mesh axis runs over, the one named last changes fastest.
Arguments:
- query_hidden: bfloat16 [1536, 2304], P('dp'), may hold values from -6 to 6
- passage_hidden: bfloat16 [1536, 3072], P(('tower', 'dp')), may hold values from -6 to 6
- pool_hidden: bfloat16 [16384, 3072], P(('tower', 'dp')), may hold values from -6 to 6
- query_proj: bfloat16 [2304, 768], replicated, may hold values from -0.125 to 0.125
- passage_proj: bfloat16 [3072, 768], replicated, may hold values from -0.109375 to 0.109375
- negative_ids: int32 [1536, 8], P('dp'), may hold values from 0 to 16383, as said below
Outputs:
- query_grad: bfloat16 [1536, 768], P(('dp', 'tower'))
- passage_grad: bfloat16 [1536, 768], P(('tower', 'dp'))
- negative_grad: bfloat16 [16384, 768], P(('tower', 'dp'))
The draws below stay inside these ranges and needn't reach their ends.
Inputs may be any that keep to these rules, and one draw needn't show every extreme that they name: `negative_ids`: the owner of pool row r is the device with index r // 512 along tower+dp. Among the 1536 ids of one index of dp, at most 96 have one owner, and in every draw some owner gets exactly 96 of them; ids may repeat.
All inputs are finite; a program needn't handle non-finite values.
Results may differ from the reference program's by a relative error of at most 0.015.
Values may be sent and summed in bfloat16 or wider, within the bound.
No kernel may reach another device: no remote copies, remote signals or barrier semaphores. Data moves between devices by JAX's collectives and lax.ppermute only.
A program may use at most 128 MiB of HBM per device.

```python
import jax
import jax.numpy as jnp
from jax import lax

D_QUERY = 2304
D_PASSAGE = 3072
EMB = 768
NEG = 8
Q_DEV = 192
POOL_DEV = 512
QUERIES = 1536
POOL = 16384
CAP = 96
N_TOWER = 4
N_DP = 8


def draw_negative_ids(key, part):
    owner_total = N_TOWER * N_DP
    slot_total = owner_total * CAP
    entry_total = Q_DEV * NEG

    def receiver_ids(receiver):
        folded = jax.random.fold_in(jax.random.fold_in(key, 7321), receiver)
        split_keys = jax.random.split(folded, 4)
        chosen = jax.random.randint(split_keys[0], (), 0, owner_total)
        places = jnp.arange(slot_total, dtype=jnp.int32)
        slot_owner = places // CAP
        jitter = jax.random.randint(split_keys[1], (slot_total,), 0, 65536)
        ranking = jnp.where(slot_owner == chosen, places, (jitter + 1) * slot_total + places)
        ordering = jnp.argsort(ranking, stable=True)[:entry_total]
        picked = slot_owner[ordering]
        picked = picked[jax.random.permutation(split_keys[2], entry_total)]
        pool_rows = jax.random.randint(split_keys[3], (entry_total,), 0, POOL_DEV)
        return (picked * POOL_DEV + pool_rows).astype(jnp.int32).reshape(Q_DEV, NEG)
    all_ids = jax.vmap(receiver_ids)(jnp.arange(N_DP, dtype=jnp.int32))
    return all_ids.reshape(Q_DEV * N_DP, NEG)


def level_of(rng, dims, cuts, least, largest):
    gain, own = 1.0, jax.random.fold_in(rng, 6)
    for axis_at, parts in cuts:
        steps = jnp.exp(jax.random.uniform(jax.random.fold_in(own, axis_at), (parts,), jnp.float32, least / len(cuts), largest / len(cuts)))
        gain = gain * jnp.repeat(steps, dims[axis_at] // parts).reshape([-1 if axis == axis_at else 1 for axis in range(len(dims))])
    return gain


def scatter_about(key, dims, scale, limit, cuts=(), kind=jnp.bfloat16):
    drawn = scale * jax.random.normal(key, dims, jnp.float32)
    if cuts:
        drawn = drawn * level_of(key, dims, cuts, -0.22, 0.18)
    return jnp.clip(drawn, -limit, limit).astype(kind)


def setup_inputs(seed: int = 0) -> dict:
    seeds = jax.random.split(jax.random.key(seed), 7)
    return {
        "query_hidden": scatter_about(seeds[0], (QUERIES, D_QUERY), 1.0, 6.0, ((0, 8),)),
        "passage_hidden": scatter_about(seeds[1], (QUERIES, D_PASSAGE), 1.0, 6.0, ((0, 32),)),
        "pool_hidden": scatter_about(seeds[2], (POOL, D_PASSAGE), 1.0, 6.0, ((0, 32),)),
        "query_proj": scatter_about(seeds[3], (D_QUERY, EMB), D_QUERY ** -0.5, 0.125),
        "passage_proj": scatter_about(seeds[4], (D_PASSAGE, EMB), D_PASSAGE ** -0.5, 0.109375),
        "negative_ids": draw_negative_ids(jax.random.fold_in(seeds[6], 71), 0),
    }


logit_scale = 50.0

def unit_rows(hidden, weight):
    projected = jnp.dot(hidden, weight, preferred_element_type=jnp.float32)
    length = jnp.sqrt(lax.optimization_barrier(jnp.sum(projected * projected, axis=1, keepdims=True)) + 1e-06)
    return (projected / length).astype(jnp.bfloat16)

def reference(query_hidden, passage_hidden, pool_hidden, query_proj, passage_proj, negative_ids):
    query_unit = unit_rows(query_hidden, query_proj)
    passage_unit = unit_rows(passage_hidden, passage_proj)
    pool_unit = unit_rows(pool_hidden, passage_proj)
    emb_width = query_unit.shape[1]
    query_blocks = query_unit.reshape(N_DP, Q_DEV, emb_width)
    id_blocks = negative_ids.reshape(N_DP, Q_DEV, NEG)

    def score_block(totals, inputs):
        passage_acc, pool_acc = totals
        block_index, queries, named_ids = inputs
        first_row = (block_index * Q_DEV).astype(jnp.int32)
        scores = logit_scale * lax.dot_general(queries, passage_unit, (((1,), (1,)), ((), ())), preferred_element_type=jnp.float32)
        exp_scores = jnp.exp(scores)
        weights = (exp_scores / lax.optimization_barrier(jnp.sum(exp_scores, axis=1, keepdims=True))).astype(jnp.bfloat16)
        positives = lax.dynamic_slice_in_dim(passage_unit, first_row, Q_DEV, 0)
        query_wide = queries.astype(jnp.float32)
        pos_score = logit_scale * lax.optimization_barrier(jnp.sum(query_wide * positives.astype(jnp.float32), axis=1))
        fetched = pool_unit[named_ids]
        fetched_wide = fetched.astype(jnp.float32)
        neg_score = logit_scale * jnp.einsum('qe,qke->qk', query_wide, fetched_wide)
        pos_exp = jnp.exp(pos_score)
        neg_exp = jnp.exp(neg_score)
        hard_total = pos_exp + lax.optimization_barrier(jnp.sum(neg_exp, axis=1))
        pos_weight = pos_exp / hard_total
        hard_weight = neg_exp / hard_total[:, None]
        query_grad = logit_scale * (jnp.dot(weights, passage_unit, preferred_element_type=jnp.float32) + (pos_weight - 2.0)[:, None] * positives.astype(jnp.float32) + jnp.einsum('qk,qke->qe', hard_weight, fetched_wide))
        batch_term = lax.dot_general(weights, queries, (((0,), (0,)), ((), ())), preferred_element_type=jnp.float32)
        passage_acc = passage_acc + logit_scale * batch_term
        own_part = lax.dynamic_slice_in_dim(passage_acc, first_row, Q_DEV, 0)
        own_part = own_part + logit_scale * (pos_weight - 2.0)[:, None] * query_wide
        passage_acc = lax.dynamic_update_slice_in_dim(passage_acc, own_part, first_row, 0)
        entry_grad = (logit_scale * hard_weight[:, :, None] * query_wide[:, None, :]).reshape(Q_DEV * NEG, emb_width)
        pool_acc = pool_acc.at[named_ids.reshape(-1)].add(entry_grad)
        return ((passage_acc, pool_acc), query_grad.astype(jnp.bfloat16))
    start_totals = (jnp.zeros((Q_DEV * N_DP, emb_width), jnp.float32), jnp.zeros((pool_unit.shape[0], emb_width), jnp.float32))
    block_ids = jnp.arange(N_DP, dtype=jnp.int32)
    (passage_acc, pool_acc), query_grads = lax.scan(score_block, start_totals, (block_ids, query_blocks, id_blocks))
    return (query_grads.reshape(Q_DEV * N_DP, emb_width), passage_acc.astype(jnp.bfloat16), pool_acc.astype(jnp.bfloat16))
```

```python
import jax
import jax.numpy as jnp
from jax import lax
from jax.sharding import PartitionSpec as P

logit_scale = 50.0
axes = ("tower", "dp")


def unit_rows(hidden, weight):
    projected = jnp.dot(hidden, weight, preferred_element_type=jnp.float32)
    length = jnp.sqrt(jnp.sum(projected * projected, axis=1, keepdims=True) + 1e-06)
    return (projected / length).astype(jnp.bfloat16)


def shards(query_hidden, passage_hidden, pool_hidden, query_proj, passage_proj, negative_ids):
    f32 = jnp.float32
    bf16 = jnp.bfloat16
    tower_count = lax.axis_size("tower")
    dp_size = lax.axis_size("dp")
    chips = dp_size // 2
    tower = lax.axis_index("tower")
    dp = lax.axis_index("dp")
    core = dp % 2
    place = dp // 2
    query_rows = query_hidden.shape[0]
    part_rows = query_rows // tower_count
    neg_count = negative_ids.shape[1]
    pool_rows = pool_hidden.shape[0]
    own_rows = passage_hidden.shape[0]
    width = query_proj.shape[1]

    def moved(x, tower_step=0, place_step=0, core_step=0):
        pairs = []
        for source in range(tower_count * dp_size):
            t, d = divmod(source, dp_size)
            target = ((d // 2) ^ place_step) * 2 + ((d % 2) ^ core_step)
            pairs.append((source, (t ^ tower_step) * dp_size + target))
        return lax.ppermute(x, axes, pairs)

    turned = tower ^ jnp.arange(tower_count)
    id_blocks = jnp.stack(
        [negative_ids] + [moved(negative_ids, place_step=s) for s in range(1, chips)]
    ).reshape(chips, tower_count, part_rows, neg_count)
    named = jnp.take(id_blocks, turned, axis=1).reshape(-1, neg_count)

    query_unit = unit_rows(query_hidden, query_proj)
    parts = jnp.take(query_unit.reshape(tower_count, part_rows, width), turned, axis=0)
    far = [moved(parts[0], place_step=s) for s in range(1, chips)]
    far = jnp.stack(far)
    spread = jnp.stack([far] + [moved(far, tower_step=s) for s in range(1, tower_count)], axis=1)
    queries = jnp.concatenate([parts[None], spread], axis=0).reshape(-1, width)

    passage_unit = unit_rows(passage_hidden, passage_proj)
    pool_unit = unit_rows(pool_hidden, passage_proj)
    items_own = jnp.concatenate([pool_unit, passage_unit], axis=0)
    items_other = moved(items_own, core_step=1)
    pool_all = jnp.concatenate([pool_unit, items_other[:pool_rows]], axis=0)
    passage_all = jnp.concatenate([passage_unit, items_other[pool_rows:]], axis=0)

    own_block = tower * dp_size + dp
    other_block = tower * dp_size + (dp ^ 1)
    pool_index = jnp.concatenate(
        [own_block * pool_rows + jnp.arange(pool_rows), other_block * pool_rows + jnp.arange(pool_rows)]
    )
    passage_index = jnp.concatenate(
        [own_block * own_rows + jnp.arange(own_rows), other_block * own_rows + jnp.arange(own_rows)]
    )
    query_index = (
        (((place ^ jnp.arange(chips)) * 2 + core) * query_rows)[:, None, None]
        + (turned * part_rows)[None, :, None]
        + jnp.arange(part_rows)[None, None, :]
    ).reshape(-1)
    count = jnp.sum((named[:, :, None] == pool_index[None, None, :]).astype(f32), axis=1)
    is_pos = query_index[:, None] == passage_index[None, :]

    contract = (((1,), (1,)), ((), ()))
    pool_exp = count * jnp.exp(
        logit_scale * lax.dot_general(queries, pool_all, contract, preferred_element_type=f32)
    )
    batch_exp = jnp.exp(
        logit_scale * lax.dot_general(queries, passage_all, contract, preferred_element_type=f32)
    )
    pos_exp = jnp.where(is_pos, batch_exp, 0.0)
    totals = jnp.stack(
        [jnp.sum(batch_exp, axis=1), jnp.sum(pool_exp, axis=1) + jnp.sum(pos_exp, axis=1)]
    )
    totals = totals.reshape(2, chips, tower_count, part_rows)
    line = totals
    for s in range(1, chips):
        line = line + moved(totals, place_step=s)[:, [k ^ s for k in range(chips)]]
    whole = line
    for s in range(1, tower_count):
        whole = whole + moved(line, tower_step=s)[:, :, [k ^ s for k in range(tower_count)]]
    batch_total = whole[0].reshape(-1, 1)
    hard_total = whole[1].reshape(-1, 1)
    pool_weight = (pool_exp / hard_total).astype(bf16)
    batch_weight = (
        batch_exp / batch_total + jnp.where(is_pos, pos_exp / hard_total - 2.0, 0.0)
    ).astype(bf16)
    query_term = logit_scale * (
        jnp.dot(pool_weight, pool_all, preferred_element_type=f32)
        + jnp.dot(batch_weight, passage_all, preferred_element_type=f32)
    )
    blocks = query_term.astype(bf16).reshape(chips, tower_count, part_rows, width)
    line_sum = blocks[:, 0].astype(f32)
    for s in range(1, tower_count):
        line_sum = line_sum + moved(blocks[:, s], tower_step=s).astype(f32)
    line_sum = line_sum.astype(bf16)
    query_grad = line_sum[0].astype(f32)
    for s in range(1, chips):
        query_grad = query_grad + moved(line_sum[s], place_step=s).astype(f32)

    across = (((0,), (0,)), ((), ()))
    pool_grad = logit_scale * lax.dot_general(pool_weight, queries, across, preferred_element_type=f32)
    passage_grad = logit_scale * lax.dot_general(
        batch_weight, queries, across, preferred_element_type=f32
    )
    given = jnp.concatenate([pool_grad[pool_rows:], passage_grad[own_rows:]], axis=0).astype(bf16)
    taken = moved(given, core_step=1).astype(f32)
    pool_grad = pool_grad[:pool_rows] + taken[:pool_rows]
    passage_grad = passage_grad[:own_rows] + taken[pool_rows:]
    return (query_grad.astype(bf16), passage_grad.astype(bf16), pool_grad.astype(bf16))


def solution(mesh):
    placed = (
        P("dp", None),
        P(("tower", "dp"), None),
        P(("tower", "dp"), None),
        P(),
        P(),
        P("dp", None),
    )
    return jax.shard_map(
        shards,
        mesh=mesh,
        in_specs=placed,
        out_specs=(P(("dp", "tower"), None), P(("tower", "dp"), None), P(("tower", "dp"), None)),
        check_vma=False,
    )
```

```python
import functools

import jax
import jax.numpy as jnp
from jax import lax
from jax.experimental import pallas as pl
from jax.experimental.pallas import tpu as pltpu
from jax.sharding import PartitionSpec as P

logit_scale = 50.0
axes = ("tower", "dp")
group = 4
f32 = jnp.float32
bf16 = jnp.bfloat16
last_last = (((1,), (1,)), ((), ()))
first_first = (((0,), (0,)), ((), ()))


def params(mib):
    return pltpu.CompilerParams(vmem_limit_bytes=mib * 2**20)


def normalized(projected):
    squares = jnp.sum(projected * projected, axis=1, keepdims=True)
    return (projected * lax.rsqrt(squares + 1e-06)).astype(bf16)


def query_kernel(steps, part_rows, hidden_ref, weight_ref, unit_ref, part_ref, total):
    step = pl.program_id(0)
    product = jnp.dot(hidden_ref[...], weight_ref[...], preferred_element_type=f32)

    @pl.when(step == 0)
    def _():
        total[...] = product

    @pl.when(step > 0)
    def _():
        total[...] += product

    @pl.when(step == steps - 1)
    def _():
        unit_ref[...] = normalized(total[...])
        start = pl.multiple_of(lax.axis_index("tower") * part_rows, 16)
        part_ref[...] = unit_ref[pl.ds(start, part_rows), :]


def project_queries(hidden, weight, part_rows):
    rows, depth = hidden.shape
    width = weight.shape[1]
    steps = 6
    chunk = depth // steps
    return pl.pallas_call(
        functools.partial(query_kernel, steps, part_rows),
        grid=(steps,),
        in_specs=[
            pl.BlockSpec((rows, chunk), lambda k: (0, k)),
            pl.BlockSpec((chunk, width), lambda k: (k, 0)),
        ],
        out_specs=[
            pl.BlockSpec((rows, width), lambda k: (0, 0)),
            pl.BlockSpec((part_rows, width), lambda k: (0, 0)),
        ],
        out_shape=[
            jax.ShapeDtypeStruct((rows, width), bf16),
            jax.ShapeDtypeStruct((part_rows, width), bf16),
        ],
        scratch_shapes=[pltpu.VMEM((rows, width), f32)],
        compiler_params=params(24),
        cost_estimate=pl.CostEstimate(
            flops=2 * rows * depth * width,
            bytes_accessed=2 * depth * (rows + width),
            transcendentals=0,
        ),
        name="query_units",
    )(hidden, weight)


def item_kernel(steps, pool_ref, passage_ref, weight_ref, unit_ref, total):
    step = pl.program_id(0)
    hidden = jnp.concatenate([pool_ref[...], passage_ref[...]], axis=0)
    product = jnp.dot(hidden, weight_ref[...], preferred_element_type=f32)

    @pl.when(step == 0)
    def _():
        total[...] = product

    @pl.when(step > 0)
    def _():
        total[...] += product

    @pl.when(step == steps - 1)
    def _():
        unit_ref[...] = normalized(total[...])


def project_items(pool, passage, weight):
    depth, width = weight.shape
    rows = pool.shape[0] + passage.shape[0]
    steps = 6
    chunk = depth // steps
    return pl.pallas_call(
        functools.partial(item_kernel, steps),
        grid=(steps,),
        in_specs=[
            pl.BlockSpec((pool.shape[0], chunk), lambda k: (0, k)),
            pl.BlockSpec((passage.shape[0], chunk), lambda k: (0, k)),
            pl.BlockSpec((chunk, width), lambda k: (k, 0)),
        ],
        out_specs=pl.BlockSpec((rows, width), lambda k: (0, 0)),
        out_shape=jax.ShapeDtypeStruct((rows, width), bf16),
        scratch_shapes=[pltpu.VMEM((rows, width), f32)],
        compiler_params=params(24),
        cost_estimate=pl.CostEstimate(
            flops=2 * rows * depth * width,
            bytes_accessed=2 * depth * (rows + width),
            transcendentals=0,
        ),
        name="item_units",
    )(pool, passage, weight)


def count_kernel(pool_rows, ids_ref, count_ref):
    own = lax.axis_index("tower") * lax.axis_size("dp") + lax.axis_index("dp")
    ids = ids_ref[...]
    neg_count, queries = ids.shape
    chunk = 64

    for half in range(2):
        base = (own ^ half) * pool_rows
        local = ids - base

        @pl.loop(0, pool_rows // chunk)
        def _(step):
            rows = lax.broadcasted_iota(jnp.int32, (chunk, queries), 0) + step * chunk
            count = jnp.zeros((chunk, queries), f32)
            for k in range(neg_count):
                count += jnp.where(rows == local[k : k + 1, :], 1.0, 0.0)
            start = pl.multiple_of(half * pool_rows + step * chunk, chunk)
            count_ref[pl.ds(start, chunk), :] = count.astype(bf16)


def count_names(ids, pool_rows, block):
    neg_count, queries = ids.shape
    return pl.pallas_call(
        functools.partial(count_kernel, pool_rows),
        grid=(queries // block,),
        in_specs=[pl.BlockSpec((neg_count, block), lambda g: (0, g))],
        out_specs=pl.BlockSpec((2 * pool_rows, block), lambda g: (0, g)),
        out_shape=jax.ShapeDtypeStruct((2 * pool_rows, queries), bf16),
        compiler_params=params(16),
        cost_estimate=pl.CostEstimate(
            flops=6 * queries * neg_count * pool_rows,
            bytes_accessed=4 * pool_rows * queries,
            transcendentals=0,
        ),
        name="name_counts",
    )(ids)


def positive_mask(query_rows, own_rows, half):
    block = group * query_rows
    dp_size = lax.axis_size("dp")
    tower, dp = lax.axis_index("tower"), lax.axis_index("dp")
    lane = lax.broadcasted_iota(jnp.int32, (1, block), 1)
    query = jnp.zeros((1, block), jnp.int32)
    for k in range(group):
        step = pl.program_id(0) * group + k
        start = (((dp // 2) ^ step) * 2 + dp % 2) * query_rows
        query = jnp.where(
            (lane >= k * query_rows) & (lane < (k + 1) * query_rows),
            start + lane - k * query_rows,
            query,
        )
    first = (tower * dp_size + (dp ^ half)) * own_rows
    passage = lax.broadcasted_iota(jnp.int32, (own_rows, block), 0) + first
    return passage == query


def placed_totals(totals, query_rows):
    place = (lax.axis_index("dp") // 2) % group
    out = totals
    for k in range(1, group):
        turned = jnp.concatenate(
            [
                totals[:, (j ^ k) * query_rows : ((j ^ k) + 1) * query_rows]
                for j in range(group)
            ],
            axis=1,
        )
        out = jnp.where(place == k, turned, out)
    return out


def score_kernel(joined, copies, query_rows, pool_rows, own_rows, part_rows, towers, *refs):
    if joined:
        queries_ref, *refs = refs
    else:
        unit_ref, *refs = refs
        far_refs, refs = refs[:towers], refs[towers:]
    own_ref, other_ref, count_ref, exp_ref, totals_ref, *refs = refs
    if not joined:
        (queries_ref,) = refs
        tower = lax.axis_index("tower")
        queries_ref[:query_rows, :] = unit_ref[...]
        for d in range(towers):
            for s in range(1, group):
                start = pl.multiple_of(s * query_rows + (tower ^ d) * part_rows, 16)
                queries_ref[pl.ds(start, part_rows), :] = far_refs[d][
                    (s - 1) * part_rows : s * part_rows, :
                ]
    queries = queries_ref[...]
    block = queries.shape[0]
    hard = jnp.zeros((1, block), f32)
    batch = jnp.zeros((1, block), f32)
    passage_start = 2 * pool_rows
    chunk = 128
    for half, items_ref in enumerate((own_ref, other_ref)):
        for start in range(0, pool_rows, chunk):
            scores = lax.dot_general(
                items_ref[start : start + chunk, :], queries, last_last, preferred_element_type=f32
            )
            row = half * pool_rows + start
            exps = jnp.exp(logit_scale * scores) * count_ref[row : row + chunk, :].astype(f32)
            hard += jnp.sum(exps, axis=0, keepdims=True)
            exp_ref[row : row + chunk, :] = exps.astype(bf16)
        scores = lax.dot_general(
            items_ref[pool_rows:, :], queries, last_last, preferred_element_type=f32
        )
        exps = jnp.exp(logit_scale * scores)
        batch += jnp.sum(exps, axis=0, keepdims=True)
        mask = positive_mask(query_rows, own_rows, half)
        hard += jnp.sum(jnp.where(mask, exps, 0.0), axis=0, keepdims=True)
        row = passage_start + half * own_rows
        exp_ref[row : row + own_rows, :] = exps.astype(bf16)
    totals = placed_totals(jnp.concatenate([batch, hard], axis=0), query_rows)
    for k in range(copies):
        totals_ref[k] = totals


def score_items(pieces, items, other, count, query_rows, pool_rows, part_rows, towers, copies):
    joined = len(pieces) == 1
    queries = count.shape[1]
    block = group * query_rows
    rows, width = items.shape
    own_rows = rows - pool_rows
    whole = lambda x: pl.BlockSpec(x.shape, lambda g: (0, 0))
    if joined:
        piece_specs = [pl.BlockSpec((block, width), lambda g: (g, 0))]
    else:
        piece_specs = [whole(x) for x in pieces]
    out_specs = [
        pl.BlockSpec((2 * rows, block), lambda g: (0, g)),
        pl.BlockSpec((copies, 2, block), lambda g: (0, 0, g)),
    ]
    out_shape = [
        jax.ShapeDtypeStruct((2 * rows, queries), bf16),
        jax.ShapeDtypeStruct((copies, 2, queries), f32),
    ]
    if not joined:
        out_specs.append(pl.BlockSpec((block, width), lambda g: (g, 0)))
        out_shape.append(jax.ShapeDtypeStruct((queries, width), bf16))
    out = pl.pallas_call(
        functools.partial(
            score_kernel, joined, copies, query_rows, pool_rows, own_rows, part_rows, towers
        ),
        grid=(queries // block,),
        in_specs=piece_specs
        + [whole(items), whole(other), pl.BlockSpec((2 * pool_rows, block), lambda g: (0, g))],
        out_specs=out_specs,
        out_shape=out_shape,
        compiler_params=params(40),
        cost_estimate=pl.CostEstimate(
            flops=4 * rows * queries * width,
            bytes_accessed=8 * rows * queries,
            transcendentals=2 * rows * queries,
        ),
        name="scores",
    )(*pieces, items, other, count)
    return out if not joined else (*out, pieces[0])


def weight_kernel(query_rows, pool_rows, own_rows, part_rows, towers, *refs):
    totals_ref, exp_ref, own_ref, other_ref, weight_ref, *send_refs = refs
    totals = placed_totals(jnp.sum(totals_ref[...], axis=0), query_rows)
    scale = 1.0 / totals
    batch, hard = scale[0:1, :], scale[1:2, :]
    pools = 2 * pool_rows
    weight_ref[:pools, :] = (exp_ref[:pools, :].astype(f32) * hard).astype(bf16)
    for half in range(2):
        row = pools + half * own_rows
        exps = exp_ref[row : row + own_rows, :].astype(f32)
        mask = positive_mask(query_rows, own_rows, half)
        weight_ref[row : row + own_rows, :] = (
            exps * batch + jnp.where(mask, exps * hard - 2.0, 0.0)
        ).astype(bf16)
    tower = lax.axis_index("tower")
    items = jnp.concatenate(
        [
            own_ref[:pool_rows, :],
            other_ref[:pool_rows, :],
            own_ref[pool_rows:, :],
            other_ref[pool_rows:, :],
        ],
        axis=0,
    )
    grad = logit_scale * lax.dot_general(
        weight_ref[...], items, first_first, preferred_element_type=f32
    )
    width = grad.shape[1]
    grad = grad.astype(bf16).reshape(group, towers, part_rows, width)
    for t in range(towers):
        for d in range(towers):

            @pl.when((tower ^ d) == t)
            def _(t=t, d=d):
                send_refs[d][...] = grad[:, t]


def weigh(totals, exps, items, other, query_rows, pool_rows, part_rows, towers):
    rows, width = items.shape
    queries = exps.shape[1]
    block = group * query_rows
    whole = lambda x: pl.BlockSpec(x.shape, lambda g: (0, 0))
    tall = pl.BlockSpec((2 * rows, block), lambda g: (0, g))
    sent = (queries // query_rows, part_rows, width)
    return pl.pallas_call(
        functools.partial(
            weight_kernel, query_rows, pool_rows, rows - pool_rows, part_rows, towers
        ),
        grid=(queries // block,),
        in_specs=[
            pl.BlockSpec((totals.shape[0], 2, block), lambda g: (0, 0, g)),
            tall,
            whole(items),
            whole(other),
        ],
        out_specs=[tall]
        + [pl.BlockSpec((group, part_rows, width), lambda g: (g, 0, 0))] * towers,
        out_shape=[jax.ShapeDtypeStruct((2 * rows, queries), bf16)]
        + [jax.ShapeDtypeStruct(sent, bf16)] * towers,
        compiler_params=params(40),
        cost_estimate=pl.CostEstimate(
            flops=4 * rows * queries * width,
            bytes_accessed=8 * rows * queries,
            transcendentals=0,
        ),
        name="weights",
    )(totals, exps, items, other)


def gradient_kernel(steps, pool_rows, own_rows, weight_ref, queries_ref, own_ref, sent_ref, total):
    step = pl.program_id(0)
    product = jnp.dot(weight_ref[...], queries_ref[...], preferred_element_type=f32)

    @pl.when(step == 0)
    def _():
        total[...] = product

    @pl.when(step > 0)
    def _():
        total[...] += product

    @pl.when(step == steps - 1)
    def _():
        pools = 2 * pool_rows
        own_ref[:pool_rows, :] = logit_scale * total[:pool_rows, :]
        own_ref[pool_rows:, :] = logit_scale * total[pools : pools + own_rows, :]
        sent_ref[:pool_rows, :] = (logit_scale * total[pool_rows:pools, :]).astype(bf16)
        sent_ref[pool_rows:, :] = (logit_scale * total[pools + own_rows :, :]).astype(bf16)


def item_gradients(weights, queries, query_rows, pool_rows):
    rows = weights.shape[0]
    half = rows // 2
    total, width = queries.shape
    block = group * query_rows
    fixed = pl.BlockSpec((half, width), lambda g: (0, 0))
    return pl.pallas_call(
        functools.partial(gradient_kernel, total // block, pool_rows, half - pool_rows),
        grid=(total // block,),
        in_specs=[
            pl.BlockSpec((rows, block), lambda g: (0, g)),
            pl.BlockSpec((block, width), lambda g: (g, 0)),
        ],
        out_specs=[fixed, fixed],
        out_shape=[
            jax.ShapeDtypeStruct((half, width), f32),
            jax.ShapeDtypeStruct((half, width), bf16),
        ],
        scratch_shapes=[pltpu.VMEM((rows, width), f32)],
        compiler_params=params(40),
        cost_estimate=pl.CostEstimate(
            flops=2 * rows * total * width, bytes_accessed=6 * rows * width, transcendentals=0
        ),
        name="item_gradients",
    )(weights, queries)


def shards(query_hidden, passage_hidden, pool_hidden, query_proj, passage_proj, negative_ids):
    towers = lax.axis_size("tower")
    dp_size = lax.axis_size("dp")
    chips = dp_size // 2
    query_rows = query_hidden.shape[0]
    part_rows = query_rows // towers
    pool_rows = pool_hidden.shape[0]
    width = query_proj.shape[1]

    def moved(x, tower_step=0, place_step=0, core_step=0):
        pairs = []
        for source in range(towers * dp_size):
            t, d = divmod(source, dp_size)
            target = ((d // 2) ^ place_step) * 2 + ((d % 2) ^ core_step)
            pairs.append((source, (t ^ tower_step) * dp_size + target))
        return lax.ppermute(x, axes, pairs)

    query_unit, part = project_queries(query_hidden, query_proj, part_rows)
    far = jnp.concatenate([moved(part, place_step=s) for s in range(1, chips)], axis=0)
    ids = jnp.transpose(negative_ids)
    ids = jnp.concatenate([ids] + [moved(ids, place_step=s) for s in range(1, chips)], axis=1)
    spread = [far] + [moved(far, tower_step=d) for d in range(1, towers)]
    items = project_items(pool_hidden, passage_hidden, passage_proj)
    other = moved(items, core_step=1)
    count = count_names(ids, pool_rows, group * query_rows)

    if chips == group:
        pieces = [query_unit] + spread
    else:
        tower = lax.axis_index("tower")
        near = query_unit.reshape(1, towers, part_rows, width)
        blocks = jnp.stack([x.reshape(chips - 1, part_rows, width) for x in spread], axis=1)
        blocks = jnp.take(blocks, tower ^ jnp.arange(towers), axis=1)
        pieces = [jnp.concatenate([near, blocks], axis=0).reshape(-1, width)]
    copies = towers * chips
    exps, totals, queries = score_items(
        pieces, items, other, count, query_rows, pool_rows, part_rows, towers, copies
    )
    if chips != group:
        shift = lax.axis_index("dp") // 2 // group
        turned = shift ^ jnp.arange(chips // group)
        totals = totals.reshape(copies, 2, chips // group, -1)
        totals = jnp.take(totals, turned, axis=2).reshape(copies, 2, -1)
    same_core = [
        [t * dp_size + 2 * z + c for t in range(towers) for z in range(chips)] for c in range(2)
    ]
    totals = lax.all_to_all(totals, axes, 0, 0, axis_index_groups=same_core)
    if chips != group:
        totals = totals.reshape(copies, 2, chips // group, -1)
        totals = jnp.take(totals, turned, axis=2).reshape(copies, 2, -1)
    weights, *sends = weigh(
        totals, exps, items, other, query_rows, pool_rows, part_rows, towers
    )
    line = sends[0].astype(f32)
    for d in range(1, towers):
        line = line + moved(sends[d], tower_step=d).astype(f32)
    line = line.astype(bf16)
    query_grad = line[0].astype(f32)
    for s in range(1, chips):
        query_grad = query_grad + moved(line[s], place_step=s).astype(f32)

    own_grad, sent_grad = item_gradients(weights, queries, query_rows, pool_rows)
    own_grad = own_grad + moved(sent_grad, core_step=1).astype(f32)
    pool_grad = own_grad[:pool_rows].astype(bf16)
    passage_grad = own_grad[pool_rows:].astype(bf16)
    return (query_grad.astype(bf16), passage_grad, pool_grad)


def solution(mesh):
    placed = (
        P("dp", None),
        P(("tower", "dp"), None),
        P(("tower", "dp"), None),
        P(),
        P(),
        P("dp", None),
    )
    return jax.shard_map(
        shards,
        mesh=mesh,
        in_specs=placed,
        out_specs=(P(("dp", "tower"), None), P(("tower", "dp"), None), P(("tower", "dp"), None)),
        check_vma=False,
    )
```

```python
import functools

import jax
import jax.numpy as jnp
from jax import lax
from jax.experimental import pallas as pl
from jax.experimental.pallas import tpu as pltpu
from jax.sharding import PartitionSpec as P

logit_scale = 50.0
axes = ("tower", "dp")
group = 4
f32 = jnp.float32
bf16 = jnp.bfloat16
last_last = (((1,), (1,)), ((), ()))
first_first = (((0,), (0,)), ((), ()))


def params(mib):
    return pltpu.CompilerParams(vmem_limit_bytes=int(mib * 2**20))


def normalized(projected):
    squares = jnp.sum(projected * projected, axis=1, keepdims=True)
    return (projected * lax.rsqrt(squares + 1e-06)).astype(bf16)


def query_kernel(steps, part_rows, hidden_ref, weight_ref, ids_ref, unit_ref, part_ref, digits_ref, hidden, weight, ids_near, sems, ids_sem):
    depth = weight.shape[0] // steps
    copies = []
    for k in range(steps):
        span = pl.ds(k * depth, depth)
        copies.append(
            (
                pltpu.make_async_copy(hidden_ref.at[:, span], hidden.at[:, span], sems.at[0, k]),
                pltpu.make_async_copy(weight_ref.at[span, :], weight.at[span, :], sems.at[1, k]),
            )
        )
    ids_copy = pltpu.make_async_copy(ids_ref, ids_near, ids_sem)
    ids_copy.start()
    for pair in copies:
        for copy in pair:
            copy.start()
    ids_copy.wait()
    ids = ids_near[...]
    neg_count, rows = ids.shape
    width = weight.shape[1]
    room = -(-rows // 128) * 128
    gap = jnp.zeros((neg_count, room - rows), f32)
    digits = jnp.concatenate(
        [
            ((ids >> 8) - 256).astype(f32),
            gap,
            (ids & 255).astype(f32),
            gap,
            jnp.zeros((neg_count, width - 2 * room), f32),
        ],
        axis=1,
    )
    extra = part_ref.shape[0] - part_rows
    digits = jnp.concatenate([digits, jnp.zeros((extra - neg_count, width), f32)], axis=0)
    digits = digits.astype(bf16)
    part_ref[part_rows:, :] = digits
    digits_ref[...] = digits
    total = None
    for k, pair in enumerate(copies):
        for copy in pair:
            copy.wait()
        span = slice(k * depth, (k + 1) * depth)
        product = jnp.dot(hidden[:, span], weight[span, :], preferred_element_type=f32)
        total = product if total is None else total + product
    unit_ref[...] = normalized(total)
    start = pl.multiple_of(lax.axis_index("tower") * part_rows, 16)
    part_ref[:part_rows, :] = unit_ref[pl.ds(start, part_rows), :]


def project_queries(hidden, weight, ids, part_rows):
    rows, depth = hidden.shape
    width = weight.shape[1]
    steps = 3
    extra = -(-ids.shape[0] // 16) * 16
    far = pl.BlockSpec(memory_space=pltpu.HBM)
    near = pl.BlockSpec(memory_space=pltpu.VMEM)
    return pl.pallas_call(
        functools.partial(query_kernel, steps, part_rows),
        in_specs=[far, far, far],
        out_specs=[near, near, near],
        out_shape=[
            jax.ShapeDtypeStruct((rows, width), bf16),
            jax.ShapeDtypeStruct((part_rows + extra, width), bf16),
            jax.ShapeDtypeStruct((extra, width), bf16),
        ],
        scratch_shapes=[
            pltpu.VMEM((rows, depth), bf16),
            pltpu.VMEM((depth, width), bf16),
            pltpu.VMEM(ids.shape, jnp.int32),
            pltpu.SemaphoreType.DMA((2, steps)),
            pltpu.SemaphoreType.DMA,
        ],
        compiler_params=params(62),
        cost_estimate=pl.CostEstimate(
            flops=2 * rows * depth * width,
            bytes_accessed=2 * depth * (rows + width),
            transcendentals=0,
        ),
        name="query_units",
    )(hidden, weight, ids)


def item_kernel(steps, pool_ref, passage_ref, weight_ref, unit_ref, hidden, weight, sems):
    depth = weight.shape[0] // steps
    pool_rows = pool_ref.shape[0]
    copies = []
    for k in range(steps):
        span = pl.ds(k * depth, depth)
        copies.append(
            (
                pltpu.make_async_copy(
                    pool_ref.at[:, span], hidden.at[pl.ds(0, pool_rows), span], sems.at[0, k]
                ),
                pltpu.make_async_copy(
                    passage_ref.at[:, span],
                    hidden.at[pl.ds(pool_rows, passage_ref.shape[0]), span],
                    sems.at[1, k],
                ),
                pltpu.make_async_copy(weight_ref.at[span, :], weight.at[span, :], sems.at[2, k]),
            )
        )
    for batch in copies:
        for copy in batch:
            copy.start()
    total = None
    for k, batch in enumerate(copies):
        for copy in batch:
            copy.wait()
        span = slice(k * depth, (k + 1) * depth)
        product = jnp.dot(hidden[:, span], weight[span, :], preferred_element_type=f32)
        total = product if total is None else total + product
    unit_ref[...] = normalized(total)


def project_items(pool, passage, weight):
    depth, width = weight.shape
    rows = pool.shape[0] + passage.shape[0]
    steps = 4
    far = pl.BlockSpec(memory_space=pltpu.HBM)
    return pl.pallas_call(
        functools.partial(item_kernel, steps),
        in_specs=[far, far, far],
        out_specs=pl.BlockSpec(memory_space=pltpu.VMEM),
        out_shape=jax.ShapeDtypeStruct((rows, width), bf16),
        scratch_shapes=[
            pltpu.VMEM((rows, depth), bf16),
            pltpu.VMEM((depth, width), bf16),
            pltpu.SemaphoreType.DMA((3, steps)),
        ],
        compiler_params=params(60),
        cost_estimate=pl.CostEstimate(
            flops=2 * rows * depth * width,
            bytes_accessed=2 * depth * (rows + width),
            transcendentals=0,
        ),
        name="item_units",
    )(pool, passage, weight)


def count_kernel(pool_rows, extra, *refs):
    ids_ref, *digit_refs, count_ref = refs
    own = lax.axis_index("tower") * lax.axis_size("dp") + lax.axis_index("dp")
    ids = [ids_ref[...]]
    for ref in digit_refs:
        digits = ref[-extra:, :].astype(f32).astype(jnp.int32)[: ids[0].shape[0]]
        rows = ids[0].shape[1]
        room = -(-rows // 128) * 128
        ids.append(((digits[:, :rows] + 256) << 8) + digits[:, room : room + rows])
    ids = jnp.concatenate(ids, axis=1)
    neg_count, queries = ids.shape
    chunk = 64

    for half in range(2):
        base = (own ^ half) * pool_rows
        local = ids - base

        @pl.loop(0, pool_rows // chunk)
        def _(step):
            rows = lax.broadcasted_iota(jnp.int32, (chunk, queries), 0) + step * chunk
            count = jnp.zeros((chunk, queries), f32)
            for k in range(neg_count):
                count += jnp.where(rows == local[k : k + 1, :], 1.0, 0.0)
            start = pl.multiple_of(half * pool_rows + step * chunk, chunk)
            count_ref[pl.ds(start, chunk), :] = count.astype(bf16)


def count_names(pieces, pool_rows, block):
    neg_count, queries = pieces[0].shape
    if len(pieces) == 1:
        specs = [pl.BlockSpec((neg_count, block), lambda g: (0, g))]
    else:
        queries *= len(pieces)
        specs = [pl.BlockSpec(x.shape, lambda g: (0, 0)) for x in pieces]
    return pl.pallas_call(
        functools.partial(count_kernel, pool_rows, -(-neg_count // 16) * 16),
        grid=(queries // block,),
        in_specs=specs,
        out_specs=pl.BlockSpec((2 * pool_rows, block), lambda g: (0, g)),
        out_shape=jax.ShapeDtypeStruct((2 * pool_rows, queries), bf16),
        compiler_params=params(16),
        cost_estimate=pl.CostEstimate(
            flops=6 * queries * neg_count * pool_rows,
            bytes_accessed=4 * pool_rows * queries,
            transcendentals=0,
        ),
        name="name_counts",
    )(*pieces)


def positive_mask(query_rows, own_rows, half, first_lane, block):
    dp_size = lax.axis_size("dp")
    tower, dp = lax.axis_index("tower"), lax.axis_index("dp")
    lane = lax.broadcasted_iota(jnp.int32, (1, block), 1) + first_lane
    query = jnp.zeros((1, block), jnp.int32)
    for k in range(group):
        step = pl.program_id(0) * group + k
        start = (((dp // 2) ^ step) * 2 + dp % 2) * query_rows
        query = jnp.where(
            (lane >= k * query_rows) & (lane < (k + 1) * query_rows),
            start + lane - k * query_rows,
            query,
        )
    first = (tower * dp_size + (dp ^ half)) * own_rows
    passage = lax.broadcasted_iota(jnp.int32, (own_rows, block), 0) + first
    return passage == query


def placed_totals(totals, query_rows):
    place = (lax.axis_index("dp") // 2) % group
    out = totals
    for k in range(1, group):
        turned = jnp.concatenate(
            [
                totals[:, (j ^ k) * query_rows : ((j ^ k) + 1) * query_rows]
                for j in range(group)
            ],
            axis=1,
        )
        out = jnp.where(place == k, turned, out)
    return out


def score_tile(items_refs, queries, count_ref, exp_ref, start, offset, query_rows, pool_rows):
    chunk = queries.shape[0]
    own_rows = items_refs[0].shape[0] - pool_rows
    lanes = slice(start, start + chunk)
    hard = jnp.zeros((1, chunk), f32)
    batch = jnp.zeros((1, chunk), f32)
    for half, items_ref in enumerate(items_refs):
        scores = lax.dot_general(items_ref[...], queries, last_last, preferred_element_type=f32)
        exps = jnp.exp(logit_scale * scores)
        rows = slice(half * pool_rows, (half + 1) * pool_rows)
        named = exps[:pool_rows] * count_ref[
            rows, offset + start : offset + start + chunk
        ].astype(f32)
        hard += jnp.sum(named, axis=0, keepdims=True)
        exp_ref[rows, lanes] = named.astype(bf16)
        mask = positive_mask(query_rows, own_rows, half, offset + start, chunk)
        hard += jnp.sum(jnp.where(mask, exps[pool_rows:], 0.0), axis=0, keepdims=True)
        batch += jnp.sum(exps[pool_rows:], axis=0, keepdims=True)
        row = 2 * pool_rows + half * own_rows
        exp_ref[row : row + own_rows, lanes] = exps[pool_rows:].astype(bf16)
    return jnp.concatenate([batch, hard], axis=0)


def score_tiles(items_refs, queries_ref, count_ref, exp_ref, offset, query_rows, pool_rows):
    block = queries_ref.shape[0]
    chunk = 256 if block % 256 == 0 else 128
    sums = []
    for start in range(0, block, chunk):
        queries = queries_ref[start : start + chunk, :]
        sums.append(
            score_tile(
                items_refs, queries, count_ref, exp_ref, start, offset, query_rows, pool_rows
            )
        )
    return jnp.concatenate(sums, axis=1)


def joined_kernel(copies, query_rows, pool_rows, queries_ref, own_ref, other_ref, count_ref, *outs):
    exp_ref, totals_ref = outs
    totals = score_tiles(
        (own_ref, other_ref), queries_ref, count_ref, exp_ref, 0, query_rows, pool_rows
    )
    totals = placed_totals(totals, query_rows)
    for k in range(copies):
        totals_ref[k] = totals


def pieces_kernel(copies, query_rows, pool_rows, part_rows, towers, *refs):
    unit_ref, next_ref, *refs = refs
    far_refs, refs = refs[:towers], refs[towers:]
    own_ref, other_ref, count_ref, exp_ref, totals_ref, queries_ref = refs
    tower = lax.axis_index("tower")
    queries_ref[:query_rows, :] = unit_ref[...]
    queries_ref[query_rows : 2 * query_rows, :] = next_ref[...]
    for d in range(towers):
        for s in range(2, group):
            start = pl.multiple_of(s * query_rows + (tower ^ d) * part_rows, 16)
            queries_ref[pl.ds(start, part_rows), :] = far_refs[d][
                (s - 2) * part_rows : (s - 1) * part_rows, :
            ]
    totals = score_tiles(
        (own_ref, other_ref), queries_ref, count_ref, exp_ref, 0, query_rows, pool_rows
    )
    totals = placed_totals(totals, query_rows)
    for k in range(copies):
        totals_ref[k] = totals


def score_cost(rows, queries, width):
    return pl.CostEstimate(
        flops=2 * rows * queries * width,
        bytes_accessed=4 * rows * queries,
        transcendentals=rows * queries,
    )


def score_joined(queries, items, other, count, query_rows, pool_rows, copies):
    total, width = queries.shape
    block = group * query_rows
    rows = 2 * items.shape[0]
    whole = lambda x: pl.BlockSpec(x.shape, lambda g: (0, 0))
    return pl.pallas_call(
        functools.partial(joined_kernel, copies, query_rows, pool_rows),
        grid=(total // block,),
        in_specs=[
            pl.BlockSpec((block, width), lambda g: (g, 0)),
            whole(items),
            whole(other),
            pl.BlockSpec((2 * pool_rows, block), lambda g: (0, g)),
        ],
        out_specs=[
            pl.BlockSpec((rows, block), lambda g: (0, g)),
            pl.BlockSpec((copies, 2, block), lambda g: (0, 0, g)),
        ],
        out_shape=[
            jax.ShapeDtypeStruct((rows, total), bf16),
            jax.ShapeDtypeStruct((copies, 2, total), f32),
        ],
        compiler_params=params(40),
        cost_estimate=score_cost(rows, total, width),
        name="scores",
    )(queries, items, other, count)


def score_pieces(pieces, items, other, count, query_rows, pool_rows, part_rows, copies):
    rows, width = 2 * items.shape[0], items.shape[1]
    queries = group * query_rows
    towers = len(pieces) - 2
    return pl.pallas_call(
        functools.partial(pieces_kernel, copies, query_rows, pool_rows, part_rows, towers),
        grid=(1,),
        out_shape=[
            jax.ShapeDtypeStruct((rows, queries), bf16),
            jax.ShapeDtypeStruct((copies, 2, queries), f32),
            jax.ShapeDtypeStruct((queries, width), bf16),
        ],
        compiler_params=params(32),
        cost_estimate=score_cost(rows, queries, width),
        name="scores",
    )(*pieces, items, other, count)


def weight_kernel(near_far, query_rows, pool_rows, own_rows, part_rows, towers, *refs):
    totals_ref, exp_ref, own_ref, other_ref, weight_ref, *grad_refs = refs
    totals = placed_totals(jnp.sum(totals_ref[...], axis=0), query_rows)
    scale = 1.0 / totals
    pools = 2 * pool_rows
    batch, hard = scale[0:1, :], scale[1:2, :]
    weight_ref[:pools, :] = (exp_ref[:pools, :].astype(f32) * hard).astype(bf16)
    for half in range(2):
        row = pools + half * own_rows
        exps = exp_ref[row : row + own_rows, :].astype(f32)
        mask = positive_mask(query_rows, own_rows, half, 0, exp_ref.shape[1])
        weight_ref[row : row + own_rows, :] = (
            exps * batch + jnp.where(mask, exps * hard - 2.0, 0.0)
        ).astype(bf16)
    tower = lax.axis_index("tower")
    items = jnp.concatenate(
        [
            own_ref[:pool_rows, :],
            other_ref[:pool_rows, :],
            own_ref[pool_rows:, :],
            other_ref[pool_rows:, :],
        ],
        axis=0,
    )
    grad = logit_scale * lax.dot_general(
        weight_ref[...], items, first_first, preferred_element_type=f32
    )
    grad = grad.astype(bf16)
    if near_far:
        near_ref, next_ref, *grad_refs = grad_refs
        near_ref[...] = grad[:query_rows]
        next_ref[...] = grad[query_rows : 2 * query_rows]
        grad = grad[2 * query_rows :]
    grad = grad.reshape(-1, towers, part_rows, grad.shape[1])
    for t in range(towers):
        for d in range(towers):

            @pl.when((tower ^ d) == t)
            def _(t=t, d=d):
                grad_refs[d][...] = grad[:, t]


def weigh(near_far, totals, exps, items, other, query_rows, pool_rows, part_rows, towers):
    rows, width = items.shape
    queries = exps.shape[1]
    block = group * query_rows
    whole = lambda x: pl.BlockSpec(x.shape, lambda g: (0, 0))
    tall = pl.BlockSpec((2 * rows, block), lambda g: (0, g))
    near = pl.BlockSpec((query_rows, width), lambda g: (0, 0))
    if not near_far:
        out_specs, out_shape, sent = [], [], group
    else:
        out_specs = [near, near]
        out_shape = [jax.ShapeDtypeStruct((query_rows, width), bf16)] * 2
        sent = group - 2
    blocks = queries // block
    return pl.pallas_call(
        functools.partial(
            weight_kernel, near_far, query_rows, pool_rows, rows - pool_rows, part_rows, towers
        ),
        grid=(blocks,),
        in_specs=[
            pl.BlockSpec((totals.shape[0], 2, block), lambda g: (0, 0, g)),
            tall,
            whole(items),
            whole(other),
        ],
        out_specs=[tall]
        + out_specs
        + [pl.BlockSpec((sent, part_rows, width), lambda g: (g, 0, 0))] * towers,
        out_shape=[jax.ShapeDtypeStruct((2 * rows, queries), bf16)]
        + out_shape
        + [jax.ShapeDtypeStruct((sent * blocks, part_rows, width), bf16)] * towers,
        compiler_params=params(40),
        cost_estimate=pl.CostEstimate(
            flops=4 * rows * queries * width,
            bytes_accessed=8 * rows * queries,
            transcendentals=0,
        ),
        name="weights",
    )(totals, exps, items, other)


def gradient_kernel(steps, pool_rows, own_rows, weight_ref, queries_ref, own_ref, sent_ref, total):
    step = pl.program_id(0)
    product = jnp.dot(weight_ref[...], queries_ref[...], preferred_element_type=f32)

    @pl.when(step == 0)
    def _():
        total[...] = product

    @pl.when(step > 0)
    def _():
        total[...] += product

    @pl.when(step == steps - 1)
    def _():
        pools = 2 * pool_rows
        own_ref[:pool_rows, :] = logit_scale * total[:pool_rows, :]
        own_ref[pool_rows:, :] = logit_scale * total[pools : pools + own_rows, :]
        sent_ref[:pool_rows, :] = (logit_scale * total[pool_rows:pools, :]).astype(bf16)
        sent_ref[pool_rows:, :] = (logit_scale * total[pools + own_rows :, :]).astype(bf16)


def item_gradients(weights, queries, query_rows, pool_rows):
    rows, total = weights.shape
    half = rows // 2
    width = queries.shape[1]
    block = group * query_rows
    fixed = pl.BlockSpec((half, width), lambda g: (0, 0))
    return pl.pallas_call(
        functools.partial(gradient_kernel, total // block, pool_rows, half - pool_rows),
        grid=(total // block,),
        in_specs=[
            pl.BlockSpec((rows, block), lambda g: (0, g)),
            pl.BlockSpec((block, width), lambda g: (g, 0)),
        ],
        out_specs=[fixed, fixed],
        out_shape=[
            jax.ShapeDtypeStruct((half, width), f32),
            jax.ShapeDtypeStruct((half, width), bf16),
        ],
        scratch_shapes=[pltpu.VMEM((rows, width), f32)],
        compiler_params=params(40),
        cost_estimate=pl.CostEstimate(
            flops=2 * rows * total * width, bytes_accessed=6 * rows * width, transcendentals=0
        ),
        name="item_gradients",
    )(weights, queries)


def join_kernel(pool_rows, own_ref, taken_ref, pool_ref, passage_ref):
    grad = (own_ref[...] + taken_ref[...].astype(f32)).astype(bf16)
    pool_ref[...] = grad[:pool_rows]
    passage_ref[...] = grad[pool_rows:]


def join_gradients(own, taken, pool_rows):
    rows, width = own.shape
    return pl.pallas_call(
        functools.partial(join_kernel, pool_rows),
        out_shape=[
            jax.ShapeDtypeStruct((pool_rows, width), bf16),
            jax.ShapeDtypeStruct((rows - pool_rows, width), bf16),
        ],
        compiler_params=params(16),
        cost_estimate=pl.CostEstimate(
            flops=rows * width, bytes_accessed=8 * rows * width, transcendentals=0
        ),
        name="join_item_gradients",
    )(own, taken)


def line_kernel(towers, part_rows, near_far, *refs):
    ins, refs = refs[:towers], refs[towers:]
    if near_far:
        near_ref, arrived_ref, *refs = refs
        plane_refs, refs = refs[:towers], refs[towers:]
        tower = lax.axis_index("tower")
        for d, out_ref in enumerate(plane_refs):
            rows = pl.ds(pl.multiple_of((tower ^ d) * part_rows, 16), part_rows)
            total = near_ref[rows, :].astype(f32) + arrived_ref[rows, :].astype(f32)
            out_ref[...] = total.astype(bf16)
    for s, out_ref in enumerate(refs):
        total = ins[0][s].astype(f32)
        for ref in ins[1:]:
            total += ref[s].astype(f32)
        out_ref[...] = total.astype(bf16)


def sum_lines(pieces, near=()):
    chips, rows, width = pieces[0].shape
    towers = len(pieces)
    outs = chips + (towers if near else 0)
    out = pl.pallas_call(
        functools.partial(line_kernel, towers, rows, len(near) > 0),
        out_shape=[jax.ShapeDtypeStruct((rows, width), bf16)] * outs,
        compiler_params=params(32),
        cost_estimate=pl.CostEstimate(
            flops=4 * outs * rows * width,
            bytes_accessed=10 * outs * rows * width,
            transcendentals=0,
        ),
        name="partial_sums",
    )(*pieces, *near)
    return (out[:towers], out[towers:]) if near else out


def shards(query_hidden, passage_hidden, pool_hidden, query_proj, passage_proj, negative_ids):
    towers = lax.axis_size("tower")
    dp_size = lax.axis_size("dp")
    chips = dp_size // 2
    query_rows = query_hidden.shape[0]
    part_rows = query_rows // towers
    pool_rows = pool_hidden.shape[0]
    width = query_proj.shape[1]

    def moved(x, tower_step=0, place_step=0, core_step=0):
        pairs = []
        for source in range(towers * dp_size):
            t, d = divmod(source, dp_size)
            target = ((d // 2) ^ place_step) * 2 + ((d % 2) ^ core_step)
            pairs.append((source, (t ^ tower_step) * dp_size + target))
        return lax.ppermute(x, axes, pairs)

    ids = jnp.transpose(negative_ids)
    near_far = chips == group
    copies = towers * chips
    query_unit, part, digits = project_queries(query_hidden, query_proj, ids, part_rows)
    parts = [moved(part, place_step=s) for s in range(2 if near_far else 1, chips)]
    far = jnp.concatenate([x[:part_rows] for x in parts], axis=0)
    if near_far:
        next_digits = moved(digits, place_step=1)
        far, next_digits = lax.optimization_barrier((far, next_digits))
    spread = [far] + [moved(far, tower_step=d) for d in range(1, towers)]
    pool_hidden, part = lax.optimization_barrier((pool_hidden, part))
    items = project_items(pool_hidden, passage_hidden, passage_proj)
    sent_items, _ = lax.optimization_barrier((items, far))
    other = moved(sent_items, core_step=1)
    if near_far:
        sent_unit, _ = lax.optimization_barrier((query_unit, far))
        next_unit = moved(sent_unit, place_step=1)
        count = count_names([ids, next_digits] + parts, pool_rows, group * query_rows)
        exps, totals, queries = score_pieces(
            [query_unit, next_unit] + spread,
            items,
            other,
            count,
            query_rows,
            pool_rows,
            part_rows,
            copies,
        )
    else:
        neg_count = ids.shape[0]
        room = -(-query_rows // 128) * 128
        ids = [ids]
        for x in parts:
            digits = x[part_rows : part_rows + neg_count].astype(f32).astype(jnp.int32)
            ids.append(
                ((digits[:, :query_rows] + 256) << 8) + digits[:, room : room + query_rows]
            )
        count = count_names([jnp.concatenate(ids, axis=1)], pool_rows, group * query_rows)
        tower = lax.axis_index("tower")
        near = query_unit.reshape(1, towers, part_rows, width)
        blocks = jnp.stack([x.reshape(chips - 1, part_rows, width) for x in spread], axis=1)
        blocks = jnp.take(blocks, tower ^ jnp.arange(towers), axis=1)
        queries = jnp.concatenate([near, blocks], axis=0).reshape(-1, width)
        exps, totals = score_joined(
            queries, items, other, count, query_rows, pool_rows, copies
        )
        shift = lax.axis_index("dp") // 2 // group
        turned = shift ^ jnp.arange(chips // group)
        totals = totals.reshape(copies, 2, chips // group, -1)
        totals = jnp.take(totals, turned, axis=2).reshape(copies, 2, -1)
    same_core = [
        [t * dp_size + 2 * z + c for t in range(towers) for z in range(chips)] for c in range(2)
    ]
    totals = lax.all_to_all(totals, axes, 0, 0, axis_index_groups=same_core)
    if not near_far:
        totals = totals.reshape(copies, 2, chips // group, -1)
        totals = jnp.take(totals, turned, axis=2).reshape(copies, 2, -1)
    weights, *grads = weigh(
        near_far, totals, exps, items, other, query_rows, pool_rows, part_rows, towers
    )
    own_grad, sent_grad = item_gradients(weights, queries, query_rows, pool_rows)
    if near_far:
        near_grad, next_grad, *grads = grads
    sums = [grads[0]] + [moved(grads[d], tower_step=d) for d in range(1, towers)]
    if near_far:
        plane, line = sum_lines(sums, (near_grad, moved(next_grad, place_step=1)))
        arrived = [moved(line[s - 2], place_step=s) for s in range(2, chips)]
        arrived += [moved(plane[d], tower_step=d) for d in range(1, towers)]
        own_line = plane[0]
    else:
        line = sum_lines(sums)
        arrived = [moved(line[s], place_step=s) for s in range(1, chips)]
        own_line = line[0]
    sent_grad, own_line = lax.optimization_barrier((sent_grad, own_line))
    taken_grad = moved(sent_grad, core_step=1)
    pool_grad, passage_grad = join_gradients(own_grad, taken_grad, pool_rows)
    own_line, pool_grad = lax.optimization_barrier((own_line, pool_grad))
    query_grad = own_line.astype(f32)
    for x in arrived:
        query_grad = query_grad + x.astype(f32)
    return (query_grad.astype(bf16), passage_grad, pool_grad)


def solution(mesh):
    placed = (
        P("dp", None),
        P(("tower", "dp"), None),
        P(("tower", "dp"), None),
        P(),
        P(),
        P("dp", None),
    )
    return jax.shard_map(
        shards,
        mesh=mesh,
        in_specs=placed,
        out_specs=(P(("dp", "tower"), None), P(("tower", "dp"), None), P(("tower", "dp"), None)),
        check_vma=False,
    )
```

```python
import functools

import jax
import jax.numpy as jnp
from jax import lax
from jax.experimental import pallas as pl
from jax.experimental.pallas import tpu as pltpu
from jax.sharding import PartitionSpec as P

logit_scale = 50.0
axes = ("tower", "dp")
group = 4
f32 = jnp.float32
bf16 = jnp.bfloat16
last_last = (((1,), (1,)), ((), ()))
first_first = (((0,), (0,)), ((), ()))


def params(mib):
    return pltpu.CompilerParams(vmem_limit_bytes=int(mib * 2**20))


def normalized(projected):
    squares = jnp.sum(projected * projected, axis=1, keepdims=True)
    return (projected * lax.rsqrt(squares + 1e-06)).astype(bf16)


def query_kernel(steps, part_rows, hidden_ref, weight_ref, ids_ref, unit_ref, part_ref, digits_ref, hidden, weight, ids_near, sems, ids_sem):
    depth = weight.shape[0] // steps
    copies = []
    for k in range(steps):
        span = pl.ds(k * depth, depth)
        copies.append(
            (
                pltpu.make_async_copy(hidden_ref.at[:, span], hidden.at[:, span], sems.at[0, k]),
                pltpu.make_async_copy(weight_ref.at[span, :], weight.at[span, :], sems.at[1, k]),
            )
        )
    ids_copy = pltpu.make_async_copy(ids_ref, ids_near, ids_sem)
    ids_copy.start()
    for pair in copies:
        for copy in pair:
            copy.start()
    ids_copy.wait()
    ids = ids_near[...]
    neg_count, rows = ids.shape
    width = weight.shape[1]
    room = -(-rows // 128) * 128
    gap = jnp.zeros((neg_count, room - rows), f32)
    digits = jnp.concatenate(
        [
            ((ids >> 8) - 256).astype(f32),
            gap,
            (ids & 255).astype(f32),
            gap,
            jnp.zeros((neg_count, width - 2 * room), f32),
        ],
        axis=1,
    )
    digits = digits.astype(bf16)
    part_ref[part_rows:, :] = digits
    digits_ref[...] = digits
    total = None
    for k, pair in enumerate(copies):
        for copy in pair:
            copy.wait()
        span = slice(k * depth, (k + 1) * depth)
        product = jnp.dot(hidden[:, span], weight[span, :], preferred_element_type=f32)
        total = product if total is None else total + product
    unit_ref[...] = normalized(total)
    start = pl.multiple_of(lax.axis_index("tower") * part_rows, 16)
    part_ref[:part_rows, :] = unit_ref[pl.ds(start, part_rows), :]


def project_queries(hidden, weight, ids, part_rows):
    rows, depth = hidden.shape
    width = weight.shape[1]
    steps = 3
    extra = ids.shape[0]
    far = pl.BlockSpec(memory_space=pltpu.HBM)
    near = pl.BlockSpec(memory_space=pltpu.VMEM)
    return pl.pallas_call(
        functools.partial(query_kernel, steps, part_rows),
        in_specs=[far, far, far],
        out_specs=[near, near, near],
        out_shape=[
            jax.ShapeDtypeStruct((rows, width), bf16),
            jax.ShapeDtypeStruct((part_rows + extra, width), bf16),
            jax.ShapeDtypeStruct((extra, width), bf16),
        ],
        scratch_shapes=[
            pltpu.VMEM((rows, depth), bf16),
            pltpu.VMEM((depth, width), bf16),
            pltpu.VMEM(ids.shape, jnp.int32),
            pltpu.SemaphoreType.DMA((2, steps)),
            pltpu.SemaphoreType.DMA,
        ],
        compiler_params=params(24),
        cost_estimate=pl.CostEstimate(
            flops=2 * rows * depth * width,
            bytes_accessed=2 * depth * (rows + width),
            transcendentals=0,
        ),
        name="query_units",
    )(
        pltpu.with_memory_space_constraint(hidden, pltpu.HBM),
        pltpu.with_memory_space_constraint(weight, pltpu.HBM),
        pltpu.with_memory_space_constraint(ids, pltpu.HBM),
    )


def item_kernel(pool_ref, passage_ref, weight_ref, unit_ref):
    hidden = jnp.concatenate([pool_ref[...], passage_ref[...]], axis=0)
    unit_ref[...] = normalized(
        jnp.dot(hidden, weight_ref[...], preferred_element_type=f32)
    )


def project_items(pool, passage, weight):
    depth, width = weight.shape
    rows = pool.shape[0] + passage.shape[0]
    return pl.pallas_call(
        item_kernel,
        out_shape=jax.ShapeDtypeStruct((rows, width), bf16),
        compiler_params=params(24),
        cost_estimate=pl.CostEstimate(
            flops=2 * rows * depth * width,
            bytes_accessed=2 * depth * (rows + width),
            transcendentals=0,
        ),
        name="item_units",
    )(pool, passage, weight)


def count_kernel(pool_rows, extra, *refs):
    ids_ref, *digit_refs, count_ref = refs
    own = lax.axis_index("tower") * lax.axis_size("dp") + lax.axis_index("dp")
    ids = [ids_ref[...]]
    for ref in digit_refs:
        digits = ref[-extra:, :].astype(f32).astype(jnp.int32)[: ids[0].shape[0]]
        rows = ids[0].shape[1]
        room = -(-rows // 128) * 128
        ids.append(((digits[:, :rows] + 256) << 8) + digits[:, room : room + rows])
    ids = jnp.concatenate(ids, axis=1)
    neg_count, queries = ids.shape
    chunk = 64

    for half in range(2):
        base = (own ^ half) * pool_rows
        local = ids - base

        @pl.loop(0, pool_rows // chunk)
        def _(step):
            rows = lax.broadcasted_iota(jnp.int32, (chunk, queries), 0) + step * chunk
            count = jnp.zeros((chunk, queries), f32)
            for k in range(neg_count):
                count += jnp.where(rows == local[k : k + 1, :], 1.0, 0.0)
            start = pl.multiple_of(half * pool_rows + step * chunk, chunk)
            count_ref[pl.ds(start, chunk), :] = count.astype(bf16)


def count_names(pieces, pool_rows, block):
    neg_count, queries = pieces[0].shape
    if len(pieces) == 1:
        specs = [pl.BlockSpec((neg_count, block), lambda g: (0, g))]
    else:
        queries *= len(pieces)
        specs = [pl.BlockSpec(x.shape, lambda g: (0, 0)) for x in pieces]
    return pl.pallas_call(
        functools.partial(count_kernel, pool_rows, neg_count),
        grid=(queries // block,),
        in_specs=specs,
        out_specs=pl.BlockSpec((2 * pool_rows, block), lambda g: (0, g)),
        out_shape=jax.ShapeDtypeStruct((2 * pool_rows, queries), bf16),
        compiler_params=params(16),
        cost_estimate=pl.CostEstimate(
            flops=6 * queries * neg_count * pool_rows,
            bytes_accessed=4 * pool_rows * queries,
            transcendentals=0,
        ),
        name="name_counts",
    )(*pieces)


def positive_mask(query_rows, own_rows, half, first_lane, block):
    dp_size = lax.axis_size("dp")
    tower, dp = lax.axis_index("tower"), lax.axis_index("dp")
    lane = lax.broadcasted_iota(jnp.int32, (1, block), 1) + first_lane
    query = jnp.zeros((1, block), jnp.int32)
    for k in range(group):
        step = pl.program_id(0) * group + k
        start = (((dp // 2) ^ step) * 2 + dp % 2) * query_rows
        query = jnp.where(
            (lane >= k * query_rows) & (lane < (k + 1) * query_rows),
            start + lane - k * query_rows,
            query,
        )
    first = (tower * dp_size + (dp ^ half)) * own_rows
    passage = lax.broadcasted_iota(jnp.int32, (own_rows, block), 0) + first
    return passage == query


def placed_totals(totals, query_rows):
    place = (lax.axis_index("dp") // 2) % group
    out = totals
    for k in range(1, group):
        turned = jnp.concatenate(
            [
                totals[:, (j ^ k) * query_rows : ((j ^ k) + 1) * query_rows]
                for j in range(group)
            ],
            axis=1,
        )
        out = jnp.where(place == k, turned, out)
    return out


def score_tile(items_refs, queries, count_ref, exp_ref, start, offset, query_rows, pool_rows):
    chunk = queries.shape[0]
    own_rows = items_refs[0].shape[0] - pool_rows
    lanes = slice(start, start + chunk)
    hard = jnp.zeros((1, chunk), f32)
    batch = jnp.zeros((1, chunk), f32)
    for half, items_ref in enumerate(items_refs):
        scores = lax.dot_general(items_ref[...], queries, last_last, preferred_element_type=f32)
        exps = jnp.exp(logit_scale * scores)
        rows = slice(half * pool_rows, (half + 1) * pool_rows)
        named = exps[:pool_rows] * count_ref[
            rows, offset + start : offset + start + chunk
        ].astype(f32)
        hard += jnp.sum(named, axis=0, keepdims=True)
        exp_ref[rows, lanes] = named.astype(bf16)
        mask = positive_mask(query_rows, own_rows, half, offset + start, chunk)
        hard += jnp.sum(jnp.where(mask, exps[pool_rows:], 0.0), axis=0, keepdims=True)
        batch += jnp.sum(exps[pool_rows:], axis=0, keepdims=True)
        row = 2 * pool_rows + half * own_rows
        exp_ref[row : row + own_rows, lanes] = exps[pool_rows:].astype(bf16)
    return jnp.concatenate([batch, hard], axis=0)


def score_tiles(items_refs, queries_ref, count_ref, exp_ref, offset, query_rows, pool_rows):
    block = queries_ref.shape[0]
    chunk = 256 if block % 256 == 0 else 128
    sums = []
    for start in range(0, block, chunk):
        queries = queries_ref[start : start + chunk, :]
        sums.append(
            score_tile(
                items_refs, queries, count_ref, exp_ref, start, offset, query_rows, pool_rows
            )
        )
    return jnp.concatenate(sums, axis=1)


def joined_kernel(copies, query_rows, pool_rows, queries_ref, own_ref, other_ref, count_ref, *outs):
    exp_ref, totals_ref = outs
    totals = score_tiles(
        (own_ref, other_ref), queries_ref, count_ref, exp_ref, 0, query_rows, pool_rows
    )
    totals = placed_totals(totals, query_rows)
    for k in range(copies):
        totals_ref[k] = totals


def pieces_kernel(copies, query_rows, pool_rows, part_rows, towers, *refs):
    unit_ref, next_ref, *refs = refs
    far_refs, refs = refs[:towers], refs[towers:]
    own_ref, other_ref, count_ref, exp_ref, totals_ref, queries_ref = refs
    tower = lax.axis_index("tower")
    queries_ref[:query_rows, :] = unit_ref[...]
    queries_ref[query_rows : 2 * query_rows, :] = next_ref[...]
    for d in range(towers):
        for s in range(2, group):
            start = pl.multiple_of(s * query_rows + (tower ^ d) * part_rows, 16)
            queries_ref[pl.ds(start, part_rows), :] = far_refs[d][
                (s - 2) * part_rows : (s - 1) * part_rows, :
            ]
    totals = score_tiles(
        (own_ref, other_ref), queries_ref, count_ref, exp_ref, 0, query_rows, pool_rows
    )
    totals = placed_totals(totals, query_rows)
    for k in range(copies):
        totals_ref[k] = totals


def score_cost(rows, queries, width):
    return pl.CostEstimate(
        flops=2 * rows * queries * width,
        bytes_accessed=4 * rows * queries,
        transcendentals=rows * queries,
    )


def score_joined(queries, items, other, count, query_rows, pool_rows, copies):
    total, width = queries.shape
    block = group * query_rows
    rows = 2 * items.shape[0]
    whole = lambda x: pl.BlockSpec(x.shape, lambda g: (0, 0))
    return pl.pallas_call(
        functools.partial(joined_kernel, copies, query_rows, pool_rows),
        grid=(total // block,),
        in_specs=[
            pl.BlockSpec((block, width), lambda g: (g, 0)),
            whole(items),
            whole(other),
            pl.BlockSpec((2 * pool_rows, block), lambda g: (0, g)),
        ],
        out_specs=[
            pl.BlockSpec((rows, block), lambda g: (0, g)),
            pl.BlockSpec((copies, 2, block), lambda g: (0, 0, g)),
        ],
        out_shape=[
            jax.ShapeDtypeStruct((rows, total), bf16),
            jax.ShapeDtypeStruct((copies, 2, total), f32),
        ],
        compiler_params=params(40),
        cost_estimate=score_cost(rows, total, width),
        name="scores",
    )(queries, items, other, count)


def score_pieces(pieces, items, other, count, query_rows, pool_rows, part_rows, copies):
    rows, width = 2 * items.shape[0], items.shape[1]
    queries = group * query_rows
    towers = len(pieces) - 2
    return pl.pallas_call(
        functools.partial(pieces_kernel, copies, query_rows, pool_rows, part_rows, towers),
        grid=(1,),
        out_shape=[
            jax.ShapeDtypeStruct((rows, queries), bf16),
            jax.ShapeDtypeStruct((copies, 2, queries), f32),
            jax.ShapeDtypeStruct((queries, width), bf16),
        ],
        compiler_params=params(32),
        cost_estimate=score_cost(rows, queries, width),
        name="scores",
    )(*pieces, items, other, count)


def weight_kernel(near_far, query_rows, pool_rows, own_rows, part_rows, towers, *refs):
    totals_ref, exp_ref, own_ref, other_ref, weight_ref, *grad_refs = refs
    totals = placed_totals(jnp.sum(totals_ref[...], axis=0), query_rows)
    scale = 1.0 / totals
    pools = 2 * pool_rows
    batch, hard = scale[0:1, :], scale[1:2, :]
    weight_ref[:pools, :] = (exp_ref[:pools, :].astype(f32) * hard).astype(bf16)
    for half in range(2):
        row = pools + half * own_rows
        exps = exp_ref[row : row + own_rows, :].astype(f32)
        mask = positive_mask(query_rows, own_rows, half, 0, exp_ref.shape[1])
        weight_ref[row : row + own_rows, :] = (
            exps * batch + jnp.where(mask, exps * hard - 2.0, 0.0)
        ).astype(bf16)
    tower = lax.axis_index("tower")
    items = jnp.concatenate(
        [
            own_ref[:pool_rows, :],
            other_ref[:pool_rows, :],
            own_ref[pool_rows:, :],
            other_ref[pool_rows:, :],
        ],
        axis=0,
    )
    grad = logit_scale * lax.dot_general(
        weight_ref[...], items, first_first, preferred_element_type=f32
    )
    grad = grad.astype(bf16)
    if near_far:
        near_ref, next_ref, *grad_refs = grad_refs
        near_ref[...] = grad[:query_rows]
        next_ref[...] = grad[query_rows : 2 * query_rows]
        grad = grad[2 * query_rows :]
    grad = grad.reshape(-1, towers, part_rows, grad.shape[1])
    for t in range(towers):
        for d in range(towers):

            @pl.when((tower ^ d) == t)
            def _(t=t, d=d):
                grad_refs[d][...] = grad[:, t]


def weigh(near_far, totals, exps, items, other, query_rows, pool_rows, part_rows, towers):
    rows, width = items.shape
    queries = exps.shape[1]
    block = group * query_rows
    whole = lambda x: pl.BlockSpec(x.shape, lambda g: (0, 0))
    tall = pl.BlockSpec((2 * rows, block), lambda g: (0, g))
    near = pl.BlockSpec((query_rows, width), lambda g: (0, 0))
    if not near_far:
        out_specs, out_shape, sent = [], [], group
    else:
        out_specs = [near, near]
        out_shape = [jax.ShapeDtypeStruct((query_rows, width), bf16)] * 2
        sent = group - 2
    blocks = queries // block
    return pl.pallas_call(
        functools.partial(
            weight_kernel, near_far, query_rows, pool_rows, rows - pool_rows, part_rows, towers
        ),
        grid=(blocks,),
        in_specs=[
            pl.BlockSpec((totals.shape[0], 2, block), lambda g: (0, 0, g)),
            tall,
            whole(items),
            whole(other),
        ],
        out_specs=[tall]
        + out_specs
        + [pl.BlockSpec((sent, part_rows, width), lambda g: (g, 0, 0))] * towers,
        out_shape=[jax.ShapeDtypeStruct((2 * rows, queries), bf16)]
        + out_shape
        + [jax.ShapeDtypeStruct((sent * blocks, part_rows, width), bf16)] * towers,
        compiler_params=params(40),
        cost_estimate=pl.CostEstimate(
            flops=4 * rows * queries * width,
            bytes_accessed=8 * rows * queries,
            transcendentals=0,
        ),
        name="weights",
    )(totals, exps, items, other)


def gradient_kernel(steps, pool_rows, own_rows, weight_ref, queries_ref, own_ref, sent_ref, total):
    step = pl.program_id(0)
    product = jnp.dot(weight_ref[...], queries_ref[...], preferred_element_type=f32)

    @pl.when(step == 0)
    def _():
        total[...] = product

    @pl.when(step > 0)
    def _():
        total[...] += product

    @pl.when(step == steps - 1)
    def _():
        pools = 2 * pool_rows
        own_ref[:pool_rows, :] = logit_scale * total[:pool_rows, :]
        own_ref[pool_rows:, :] = logit_scale * total[pools : pools + own_rows, :]
        sent_ref[:pool_rows, :] = (logit_scale * total[pool_rows:pools, :]).astype(bf16)
        sent_ref[pool_rows:, :] = (logit_scale * total[pools + own_rows :, :]).astype(bf16)


def item_gradients(weights, queries, query_rows, pool_rows):
    rows, total = weights.shape
    half = rows // 2
    width = queries.shape[1]
    block = group * query_rows
    fixed = pl.BlockSpec((half, width), lambda g: (0, 0))
    return pl.pallas_call(
        functools.partial(gradient_kernel, total // block, pool_rows, half - pool_rows),
        grid=(total // block,),
        in_specs=[
            pl.BlockSpec((rows, block), lambda g: (0, g)),
            pl.BlockSpec((block, width), lambda g: (g, 0)),
        ],
        out_specs=[fixed, fixed],
        out_shape=[
            jax.ShapeDtypeStruct((half, width), f32),
            jax.ShapeDtypeStruct((half, width), bf16),
        ],
        scratch_shapes=[pltpu.VMEM((rows, width), f32)],
        compiler_params=params(40),
        cost_estimate=pl.CostEstimate(
            flops=2 * rows * total * width, bytes_accessed=6 * rows * width, transcendentals=0
        ),
        name="item_gradients",
    )(weights, queries)


def join_kernel(pool_rows, own_ref, taken_ref, pool_ref, passage_ref):
    grad = (own_ref[...] + taken_ref[...].astype(f32)).astype(bf16)
    pool_ref[...] = grad[:pool_rows]
    passage_ref[...] = grad[pool_rows:]


def join_gradients(own, taken, pool_rows):
    rows, width = own.shape
    return pl.pallas_call(
        functools.partial(join_kernel, pool_rows),
        out_shape=[
            jax.ShapeDtypeStruct((pool_rows, width), bf16),
            jax.ShapeDtypeStruct((rows - pool_rows, width), bf16),
        ],
        compiler_params=params(16),
        cost_estimate=pl.CostEstimate(
            flops=rows * width, bytes_accessed=8 * rows * width, transcendentals=0
        ),
        name="join_item_gradients",
    )(own, taken)


def line_kernel(towers, part_rows, near_far, *refs):
    ins, refs = refs[:towers], refs[towers:]
    if near_far:
        near_ref, arrived_ref, *refs = refs
        plane_refs, refs = refs[:towers], refs[towers:]
        tower = lax.axis_index("tower")
        for d, out_ref in enumerate(plane_refs):
            rows = pl.ds(pl.multiple_of((tower ^ d) * part_rows, 16), part_rows)
            total = near_ref[rows, :].astype(f32) + arrived_ref[rows, :].astype(f32)
            out_ref[...] = total.astype(bf16)
    for s, out_ref in enumerate(refs):
        total = ins[0][s].astype(f32)
        for ref in ins[1:]:
            total += ref[s].astype(f32)
        out_ref[...] = total.astype(bf16)


def sum_lines(pieces, near=()):
    chips, rows, width = pieces[0].shape
    towers = len(pieces)
    outs = chips + (towers if near else 0)
    out = pl.pallas_call(
        functools.partial(line_kernel, towers, rows, len(near) > 0),
        out_shape=[jax.ShapeDtypeStruct((rows, width), bf16)] * outs,
        compiler_params=params(32),
        cost_estimate=pl.CostEstimate(
            flops=4 * outs * rows * width,
            bytes_accessed=10 * outs * rows * width,
            transcendentals=0,
        ),
        name="partial_sums",
    )(*pieces, *near)
    return (out[:towers], out[towers:]) if near else out


def shards(query_hidden, passage_hidden, pool_hidden, query_proj, passage_proj, negative_ids):
    towers = lax.axis_size("tower")
    dp_size = lax.axis_size("dp")
    chips = dp_size // 2
    query_rows = query_hidden.shape[0]
    part_rows = query_rows // towers
    pool_rows = pool_hidden.shape[0]
    width = query_proj.shape[1]

    def moved(x, tower_step=0, place_step=0, core_step=0):
        pairs = []
        for source in range(towers * dp_size):
            t, d = divmod(source, dp_size)
            target = ((d // 2) ^ place_step) * 2 + ((d % 2) ^ core_step)
            pairs.append((source, (t ^ tower_step) * dp_size + target))
        return lax.ppermute(x, axes, pairs)

    ids = jnp.transpose(negative_ids)
    near_far = chips == group
    copies = towers * chips
    query_unit, part, digits = project_queries(query_hidden, query_proj, ids, part_rows)
    parts = [moved(part, place_step=s) for s in range(2 if near_far else 1, chips)]
    far = jnp.concatenate([x[:part_rows] for x in parts], axis=0)
    if near_far:
        next_digits = moved(digits, place_step=1)
        far, next_digits = lax.optimization_barrier((far, next_digits))
    spread = [far] + [moved(far, tower_step=d) for d in range(1, towers)]
    pool_hidden, part = lax.optimization_barrier((pool_hidden, part))
    items = project_items(pool_hidden, passage_hidden, passage_proj)
    sent_items, _ = lax.optimization_barrier((items, far))
    other = moved(sent_items, core_step=1)
    if near_far:
        sent_unit, _ = lax.optimization_barrier((query_unit, far))
        next_unit = moved(sent_unit, place_step=1)
        count = count_names([ids, next_digits] + parts, pool_rows, group * query_rows)
        exps, totals, queries = score_pieces(
            [query_unit, next_unit] + spread,
            items,
            other,
            count,
            query_rows,
            pool_rows,
            part_rows,
            copies,
        )
    else:
        neg_count = ids.shape[0]
        room = -(-query_rows // 128) * 128
        ids = [ids]
        for x in parts:
            digits = x[part_rows : part_rows + neg_count].astype(f32).astype(jnp.int32)
            ids.append(
                ((digits[:, :query_rows] + 256) << 8) + digits[:, room : room + query_rows]
            )
        count = count_names([jnp.concatenate(ids, axis=1)], pool_rows, group * query_rows)
        tower = lax.axis_index("tower")
        near = query_unit.reshape(1, towers, part_rows, width)
        blocks = jnp.stack([x.reshape(chips - 1, part_rows, width) for x in spread], axis=1)
        blocks = jnp.take(blocks, tower ^ jnp.arange(towers), axis=1)
        queries = jnp.concatenate([near, blocks], axis=0).reshape(-1, width)
        exps, totals = score_joined(
            queries, items, other, count, query_rows, pool_rows, copies
        )
        shift = lax.axis_index("dp") // 2 // group
        turned = shift ^ jnp.arange(chips // group)
        totals = totals.reshape(copies, 2, chips // group, -1)
        totals = jnp.take(totals, turned, axis=2).reshape(copies, 2, -1)
    same_core = [
        [t * dp_size + 2 * z + c for t in range(towers) for z in range(chips)] for c in range(2)
    ]
    totals = lax.all_to_all(totals, axes, 0, 0, axis_index_groups=same_core)
    if not near_far:
        totals = totals.reshape(copies, 2, chips // group, -1)
        totals = jnp.take(totals, turned, axis=2).reshape(copies, 2, -1)
    weights, *grads = weigh(
        near_far, totals, exps, items, other, query_rows, pool_rows, part_rows, towers
    )
    own_grad, sent_grad = item_gradients(weights, queries, query_rows, pool_rows)
    if near_far:
        near_grad, next_grad, *grads = grads
    sums = [grads[0]] + [moved(grads[d], tower_step=d) for d in range(1, towers)]
    if near_far:
        plane, line = sum_lines(sums, (near_grad, moved(next_grad, place_step=1)))
        arrived = [moved(line[s - 2], place_step=s) for s in range(2, chips)]
        arrived += [moved(plane[d], tower_step=d) for d in range(1, towers)]
        own_line = plane[0]
    else:
        line = sum_lines(sums)
        arrived = [moved(line[s], place_step=s) for s in range(1, chips)]
        own_line = line[0]
    sent_grad, own_line = lax.optimization_barrier((sent_grad, own_line))
    taken_grad = moved(sent_grad, core_step=1)
    pool_grad, passage_grad = join_gradients(own_grad, taken_grad, pool_rows)
    own_line, pool_grad = lax.optimization_barrier((own_line, pool_grad))
    query_grad = own_line.astype(f32)
    for x in arrived:
        query_grad = query_grad + x.astype(f32)
    return (query_grad.astype(bf16), passage_grad, pool_grad)


def solution(mesh):
    placed = (
        P("dp", None),
        P(("tower", "dp"), None),
        P(("tower", "dp"), None),
        P(),
        P(),
        P("dp", None),
    )
    return jax.shard_map(
        shards,
        mesh=mesh,
        in_specs=placed,
        out_specs=(P(("dp", "tower"), None), P(("tower", "dp"), None), P(("tower", "dp"), None)),
        check_vma=False,
    )
```

```python
import functools

import jax
import jax.numpy as jnp
from jax import lax
from jax.experimental import pallas as pl
from jax.experimental.pallas import tpu as pltpu
from jax.sharding import PartitionSpec as P

logit_scale = 50.0
axes = ("tower", "dp")
group = 4
f32 = jnp.float32
bf16 = jnp.bfloat16
last_last = (((1,), (1,)), ((), ()))
first_first = (((0,), (0,)), ((), ()))


def block_step(blocks):
    return pl.program_id(0) if blocks > 1 else 0


def grid_of(blocks, in_specs, out_specs):
    if blocks == 1:
        return {}
    return {"grid": (blocks,), "in_specs": in_specs, "out_specs": out_specs}


def params(mib):
    return pltpu.CompilerParams(vmem_limit_bytes=int(mib * 2**20))


def normalized(projected):
    squares = jnp.sum(projected * projected, axis=1, keepdims=True)
    return (projected * lax.rsqrt(squares + 1e-06)).astype(bf16)


def digits_of(ids):
    rows = ids.shape[1]
    full = rows // 128 * 128
    assert rows - full == 64 and full == 128
    high = ((ids >> 8) - 256).astype(f32)
    low = (ids & 255).astype(f32)
    last = jnp.concatenate([high[:, full:], low[:, full:]], axis=1)
    return jnp.concatenate([high[:, :full], low[:, :full], last], axis=0).astype(bf16)


def ids_of(digits):
    digits = digits.astype(f32).astype(jnp.int32)
    count = digits.shape[0] // 3
    last = digits[2 * count :]
    high = jnp.concatenate([digits[:count], last[:, :64]], axis=1)
    low = jnp.concatenate([digits[count : 2 * count], last[:, 64:]], axis=1)
    return ((high + 256) << 8) + low


def query_kernel(steps, part_rows, hidden_ref, weight_ref, ids_ref, unit_ref, part_ref, digits_ref, hidden, weight, ids_near, sems, ids_sem):
    depth = weight.shape[0] // steps
    copies = []
    for k in range(steps):
        span = pl.ds(k * depth, depth)
        copies.append(
            (
                pltpu.make_async_copy(hidden_ref.at[:, span], hidden.at[:, span], sems.at[0, k]),
                pltpu.make_async_copy(weight_ref.at[span, :], weight.at[span, :], sems.at[1, k]),
            )
        )
    ids_copy = pltpu.make_async_copy(ids_ref, ids_near, ids_sem)
    ids_copy.start()
    for pair in copies:
        for copy in pair:
            copy.start()
    ids_copy.wait()
    digits = digits_of(ids_near[...])
    slabs = weight.shape[1] // 128
    part_ref[slabs * part_rows :, :] = digits
    digits_ref[...] = digits
    total = None
    for k, pair in enumerate(copies):
        for copy in pair:
            copy.wait()
        span = slice(k * depth, (k + 1) * depth)
        product = jnp.dot(hidden[:, span], weight[span, :], preferred_element_type=f32)
        total = product if total is None else total + product
    unit_ref[...] = normalized(total)
    start = pl.multiple_of(lax.axis_index("tower") * part_rows, 16)
    for k in range(slabs):
        part_ref[k * part_rows : (k + 1) * part_rows, :] = unit_ref[
            pl.ds(start, part_rows), k * 128 : (k + 1) * 128
        ]


def project_queries(hidden, weight, ids, part_rows):
    rows, depth = hidden.shape
    width = weight.shape[1]
    steps = 3
    extra = 3 * ids.shape[0]
    far = pl.BlockSpec(memory_space=pltpu.HBM)
    near = pl.BlockSpec(memory_space=pltpu.VMEM)
    return pl.pallas_call(
        functools.partial(query_kernel, steps, part_rows),
        in_specs=[far, far, far],
        out_specs=[near, near, near],
        out_shape=[
            jax.ShapeDtypeStruct((rows, width), bf16),
            jax.ShapeDtypeStruct((part_rows * width // 128 + extra, 128), bf16),
            jax.ShapeDtypeStruct((extra, 128), bf16),
        ],
        scratch_shapes=[
            pltpu.VMEM((rows, depth), bf16),
            pltpu.VMEM((depth, width), bf16),
            pltpu.VMEM(ids.shape, jnp.int32),
            pltpu.SemaphoreType.DMA((2, steps)),
            pltpu.SemaphoreType.DMA,
        ],
        compiler_params=params(24),
        cost_estimate=pl.CostEstimate(
            flops=16 * rows * depth * width,
            bytes_accessed=12 * depth * (rows + width),
            transcendentals=0,
        ),
        name="query_units",
    )(
        pltpu.with_memory_space_constraint(hidden, pltpu.HBM),
        pltpu.with_memory_space_constraint(weight, pltpu.HBM),
        pltpu.with_memory_space_constraint(ids, pltpu.HBM),
    )


def item_kernel(pool_ref, passage_ref, weight_ref, unit_ref):
    hidden = jnp.concatenate([pool_ref[...], passage_ref[...]], axis=0)
    unit_ref[...] = normalized(
        jnp.dot(hidden, weight_ref[...], preferred_element_type=f32)
    )


def project_items(pool, passage, weight):
    depth, width = weight.shape
    rows = pool.shape[0] + passage.shape[0]
    return pl.pallas_call(
        item_kernel,
        out_shape=jax.ShapeDtypeStruct((rows, width), bf16),
        compiler_params=params(24),
        cost_estimate=pl.CostEstimate(
            flops=2 * rows * depth * width,
            bytes_accessed=2 * depth * (rows + width),
            transcendentals=0,
        ),
        name="item_units",
    )(pool, passage, weight)


def count_kernel(pool_rows, extra, *refs):
    ids_ref, *digit_refs, count_ref = refs
    own = lax.axis_index("tower") * lax.axis_size("dp") + lax.axis_index("dp")
    ids = [ids_ref[...]]
    for ref in digit_refs:
        ids.append(ids_of(ref[-extra:, :]))
    ids = jnp.concatenate(ids, axis=1)
    neg_count, queries = ids.shape
    chunk = 64

    for half in range(2):
        base = (own ^ half) * pool_rows
        local = ids - base

        @pl.loop(0, pool_rows // chunk)
        def _(step):
            rows = lax.broadcasted_iota(jnp.int32, (chunk, queries), 0) + step * chunk
            count = jnp.zeros((chunk, queries), f32)
            for k in range(neg_count):
                count += jnp.where(rows == local[k : k + 1, :], 1.0, 0.0)
            start = pl.multiple_of(half * pool_rows + step * chunk, chunk)
            count_ref[pl.ds(start, chunk), :] = count.astype(bf16)


def count_names(pieces, pool_rows, block):
    neg_count, queries = pieces[0].shape
    if len(pieces) == 1:
        specs = [pl.BlockSpec((neg_count, block), lambda g: (0, g))]
    else:
        queries *= len(pieces)
        specs = [pl.BlockSpec(x.shape, lambda g: (0, 0)) for x in pieces]
    return pl.pallas_call(
        functools.partial(count_kernel, pool_rows, 3 * neg_count),
        out_shape=jax.ShapeDtypeStruct((2 * pool_rows, queries), bf16),
        **grid_of(
            queries // block, specs, pl.BlockSpec((2 * pool_rows, block), lambda g: (0, g))
        ),
        compiler_params=params(16),
        cost_estimate=pl.CostEstimate(
            flops=6 * queries * neg_count * pool_rows,
            bytes_accessed=4 * pool_rows * queries,
            transcendentals=0,
        ),
        name="name_counts",
    )(*pieces)


def positive_mask(query_rows, own_rows, half, first_lane, block, blocks):
    dp_size = lax.axis_size("dp")
    tower, dp = lax.axis_index("tower"), lax.axis_index("dp")
    lane = lax.broadcasted_iota(jnp.int32, (1, block), 1) + first_lane
    query = jnp.zeros((1, block), jnp.int32)
    for k in range(group):
        step = block_step(blocks) * group + k
        start = (((dp // 2) ^ step) * 2 + dp % 2) * query_rows
        query = jnp.where(
            (lane >= k * query_rows) & (lane < (k + 1) * query_rows),
            start + lane - k * query_rows,
            query,
        )
    first = (tower * dp_size + (dp ^ half)) * own_rows
    passage = lax.broadcasted_iota(jnp.int32, (own_rows, block), 0) + first
    return passage == query


def placed_totals(totals, query_rows):
    place = (lax.axis_index("dp") // 2) % group
    out = totals
    for k in range(1, group):
        turned = jnp.concatenate(
            [
                totals[:, (j ^ k) * query_rows : ((j ^ k) + 1) * query_rows]
                for j in range(group)
            ],
            axis=1,
        )
        out = jnp.where(place == k, turned, out)
    return out


def score_tile(
    items_refs, queries, count_ref, exp_ref, start, offset, query_rows, pool_rows, blocks
):
    chunk = queries.shape[0]
    own_rows = items_refs[0].shape[0] - pool_rows
    lanes = slice(start, start + chunk)
    hard = jnp.zeros((1, chunk), f32)
    batch = jnp.zeros((1, chunk), f32)
    for half, items_ref in enumerate(items_refs):
        scores = lax.dot_general(items_ref[...], queries, last_last, preferred_element_type=f32)
        exps = jnp.exp(logit_scale * scores)
        rows = slice(half * pool_rows, (half + 1) * pool_rows)
        named = exps[:pool_rows] * count_ref[
            rows, offset + start : offset + start + chunk
        ].astype(f32)
        hard += jnp.sum(named, axis=0, keepdims=True)
        exp_ref[rows, lanes] = named.astype(bf16)
        mask = positive_mask(query_rows, own_rows, half, offset + start, chunk, blocks)
        hard += jnp.sum(jnp.where(mask, exps[pool_rows:], 0.0), axis=0, keepdims=True)
        batch += jnp.sum(exps[pool_rows:], axis=0, keepdims=True)
        row = 2 * pool_rows + half * own_rows
        exp_ref[row : row + own_rows, lanes] = exps[pool_rows:].astype(bf16)
    return jnp.concatenate([batch, hard], axis=0)


def score_tiles(
    items_refs, queries_ref, count_ref, exp_ref, offset, query_rows, pool_rows, blocks
):
    block = queries_ref.shape[0]
    chunk = 256 if block % 256 == 0 else block
    sums = []
    for start in range(0, block, chunk):
        queries = queries_ref[start : start + chunk, :]
        sums.append(
            score_tile(
                items_refs,
                queries,
                count_ref,
                exp_ref,
                start,
                offset,
                query_rows,
                pool_rows,
                blocks,
            )
        )
    return jnp.concatenate(sums, axis=1)


def joined_kernel(blocks, copies, query_rows, pool_rows, queries_ref, own_ref, other_ref, count_ref, *outs):
    exp_ref, totals_ref = outs
    totals = score_tiles(
        (own_ref, other_ref), queries_ref, count_ref, exp_ref, 0, query_rows, pool_rows, blocks
    )
    totals = placed_totals(totals, query_rows)
    for k in range(copies):
        totals_ref[k] = totals


def far_kernel(copies, query_rows, pool_rows, part_rows, towers, *refs):
    far_refs, refs = refs[:towers], refs[towers:]
    own_ref, other_ref, count_ref, near_ref, exp_ref, totals_ref, queries_ref = refs
    tower = lax.axis_index("tower")
    slabs = queries_ref.shape[1] // 128
    for d in range(towers):
        for s in range(queries_ref.shape[0] // query_rows):
            start = pl.multiple_of(s * query_rows + (tower ^ d) * part_rows, 16)
            for k in range(slabs):
                queries_ref[pl.ds(start, part_rows), k * 128 : (k + 1) * 128] = far_refs[d][
                    (s * slabs + k) * part_rows : (s * slabs + k + 1) * part_rows, :
                ]
    items = (own_ref, other_ref)
    totals = score_tiles(
        items, queries_ref, count_ref, exp_ref, 2 * query_rows, query_rows, pool_rows, 1
    )
    totals = placed_totals(jnp.concatenate([near_ref[...], totals], axis=1), query_rows)
    for k in range(copies):
        totals_ref[k] = totals


def near_kernel(query_rows, pool_rows, *refs):
    unit_ref, next_ref, own_ref, other_ref, count_ref, exp_ref, totals_ref, queries = refs
    queries[:query_rows, :] = unit_ref[...]
    queries[query_rows:, :] = next_ref[...]
    totals_ref[...] = score_tiles(
        (own_ref, other_ref), queries, count_ref, exp_ref, 0, query_rows, pool_rows, 1
    )


def score_cost(rows, queries, width):
    return pl.CostEstimate(
        flops=2 * rows * queries * width,
        bytes_accessed=4 * rows * queries,
        transcendentals=rows * queries,
    )


def score_joined(queries, items, other, count, query_rows, pool_rows, copies):
    total, width = queries.shape
    block = group * query_rows
    rows = 2 * items.shape[0]
    whole = lambda x: pl.BlockSpec(x.shape, lambda g: (0, 0))
    return pl.pallas_call(
        functools.partial(joined_kernel, total // block, copies, query_rows, pool_rows),
        grid=(total // block,),
        in_specs=[
            pl.BlockSpec((block, width), lambda g: (g, 0)),
            whole(items),
            whole(other),
            pl.BlockSpec((2 * pool_rows, block), lambda g: (0, g)),
        ],
        out_specs=[
            pl.BlockSpec((rows, block), lambda g: (0, g)),
            pl.BlockSpec((copies, 2, block), lambda g: (0, 0, g)),
        ],
        out_shape=[
            jax.ShapeDtypeStruct((rows, total), bf16),
            jax.ShapeDtypeStruct((copies, 2, total), f32),
        ],
        compiler_params=params(40),
        cost_estimate=score_cost(rows, total, width),
        name="scores",
    )(queries, items, other, count)


def score_far(spread, items, other, count, near, query_rows, pool_rows, part_rows, copies):
    rows, width = 2 * items.shape[0], items.shape[1]
    queries = (group - 2) * query_rows
    return pl.pallas_call(
        functools.partial(far_kernel, copies, query_rows, pool_rows, part_rows, len(spread)),
        out_shape=[
            jax.ShapeDtypeStruct((rows, queries), bf16),
            jax.ShapeDtypeStruct((copies, 2, group * query_rows), f32),
            jax.ShapeDtypeStruct((queries, width), bf16),
        ],
        compiler_params=params(32),
        cost_estimate=score_cost(rows, queries, width),
        name="far_scores",
    )(*spread, items, other, count, near)


def score_near(unit, next_unit, items, other, count, query_rows, pool_rows):
    rows, width = 2 * items.shape[0], items.shape[1]
    queries = 2 * query_rows
    return pl.pallas_call(
        functools.partial(near_kernel, query_rows, pool_rows),
        out_shape=[
            jax.ShapeDtypeStruct((rows, queries), bf16),
            jax.ShapeDtypeStruct((2, queries), f32),
        ],
        scratch_shapes=[pltpu.VMEM((queries, width), bf16)],
        compiler_params=params(32),
        cost_estimate=score_cost(rows, queries, width),
        name="near_scores",
    )(unit, next_unit, items, other, count)


def weight_kernel(blocks, exp_count, query_rows, pool_rows, own_rows, part_rows, towers, *refs):
    totals_ref, refs = refs[0], refs[1:]
    exp_refs, refs = refs[:exp_count], refs[exp_count:]
    own_ref, other_ref, weight_ref, *grad_refs = refs
    totals = placed_totals(jnp.sum(totals_ref[...], axis=0), query_rows)
    scale = 1.0 / totals
    pools = 2 * pool_rows
    first = 0
    for exp_ref in exp_refs:
        block = exp_ref.shape[1]
        lanes = slice(first, first + block)
        batch, hard = scale[0:1, lanes], scale[1:2, lanes]
        weight_ref[:pools, lanes] = (exp_ref[:pools, :].astype(f32) * hard).astype(bf16)
        for half in range(2):
            row = pools + half * own_rows
            exps = exp_ref[row : row + own_rows, :].astype(f32)
            mask = positive_mask(query_rows, own_rows, half, first, block, blocks)
            weight_ref[row : row + own_rows, lanes] = (
                exps * batch + jnp.where(mask, exps * hard - 2.0, 0.0)
            ).astype(bf16)
        first += block
    tower = lax.axis_index("tower")
    items = jnp.concatenate(
        [
            own_ref[:pool_rows, :],
            other_ref[:pool_rows, :],
            own_ref[pool_rows:, :],
            other_ref[pool_rows:, :],
        ],
        axis=0,
    )
    grad = logit_scale * lax.dot_general(
        weight_ref[...], items, first_first, preferred_element_type=f32
    )
    grad = grad.astype(bf16)
    if exp_count == 2:
        near_ref, next_ref, *grad_refs = grad_refs
        near_ref[...] = grad[:query_rows]
        next_ref[...] = grad[query_rows : 2 * query_rows]
        grad = grad[2 * query_rows :]
    grad = grad.reshape(-1, towers, part_rows, grad.shape[1])
    for t in range(towers):
        for d in range(towers):

            @pl.when((tower ^ d) == t)
            def _(t=t, d=d):
                grad_refs[d][...] = grad[:, t]


def weigh(totals, exps, items, other, query_rows, pool_rows, part_rows, towers):
    rows, width = items.shape
    queries = sum(x.shape[1] for x in exps)
    block = group * query_rows
    whole = lambda x: pl.BlockSpec(x.shape, lambda g: (0, 0))
    tall = pl.BlockSpec((2 * rows, block), lambda g: (0, g))
    near = pl.BlockSpec((query_rows, width), lambda g: (0, 0))
    if len(exps) == 1:
        exp_specs, out_specs, out_shape, sent = [tall], [], [], group
    else:
        exp_specs = [whole(x) for x in exps]
        out_specs = [near, near]
        out_shape = [jax.ShapeDtypeStruct((query_rows, width), bf16)] * 2
        sent = group - 2
    blocks = queries // block
    return pl.pallas_call(
        functools.partial(
            weight_kernel,
            blocks,
            len(exps),
            query_rows,
            pool_rows,
            rows - pool_rows,
            part_rows,
            towers,
        ),
        **grid_of(
            blocks,
            [pl.BlockSpec((totals.shape[0], 2, block), lambda g: (0, 0, g))]
            + exp_specs
            + [whole(items), whole(other)],
            [tall]
            + out_specs
            + [pl.BlockSpec((sent, part_rows, width), lambda g: (g, 0, 0))] * towers,
        ),
        out_shape=[jax.ShapeDtypeStruct((2 * rows, queries), bf16)]
        + out_shape
        + [jax.ShapeDtypeStruct((sent * blocks, part_rows, width), bf16)] * towers,
        compiler_params=params(40),
        cost_estimate=pl.CostEstimate(
            flops=4 * rows * queries * width,
            bytes_accessed=8 * rows * queries,
            transcendentals=0,
        ),
        name="weights",
    )(totals, *exps, items, other)


def gradient_kernel(steps, query_count, pool_rows, own_rows, weight_ref, *refs):
    query_refs, refs = refs[:query_count], refs[query_count:]
    own_ref, sent_ref, *scratch = refs
    step = block_step(steps)
    if len(query_refs) == 1:
        queries = query_refs[0][...]
    else:
        unit_ref, next_ref, far_ref = query_refs
        queries = jnp.concatenate(
            [unit_ref[...], next_ref[...], far_ref[...]], axis=0
        )
    product = jnp.dot(weight_ref[...], queries, preferred_element_type=f32)

    def finish(total):
        pools = 2 * pool_rows
        own_ref[:pool_rows, :] = logit_scale * total[:pool_rows, :]
        own_ref[pool_rows:, :] = logit_scale * total[pools : pools + own_rows, :]
        sent_ref[:pool_rows, :] = (logit_scale * total[pool_rows:pools, :]).astype(bf16)
        sent_ref[pool_rows:, :] = (logit_scale * total[pools + own_rows :, :]).astype(bf16)

    if steps == 1:
        finish(product)
        return
    (total,) = scratch

    @pl.when(step == 0)
    def _():
        total[...] = product

    @pl.when(step > 0)
    def _():
        total[...] += product

    @pl.when(step == steps - 1)
    def _():
        finish(total[...])


def item_gradients(weights, queries, query_rows, pool_rows):
    rows, total = weights.shape
    half = rows // 2
    width = queries[0].shape[1]
    block = group * query_rows
    blocks = total // block
    fixed = pl.BlockSpec((half, width), lambda g: (0, 0))
    if len(queries) == 1:
        query_specs = [pl.BlockSpec((block, width), lambda g: (g, 0))]
    else:
        query_specs = [pl.BlockSpec(x.shape, lambda g: (0, 0)) for x in queries]
    return pl.pallas_call(
        functools.partial(
            gradient_kernel, blocks, len(queries), pool_rows, half - pool_rows
        ),
        **grid_of(
            blocks,
            [pl.BlockSpec((rows, block), lambda g: (0, g))] + query_specs,
            [fixed, fixed],
        ),
        out_shape=[
            jax.ShapeDtypeStruct((half, width), f32),
            jax.ShapeDtypeStruct((half, width), bf16),
        ],
        scratch_shapes=[pltpu.VMEM((rows, width), f32)] if blocks > 1 else [],
        compiler_params=params(40),
        cost_estimate=pl.CostEstimate(
            flops=2 * rows * total * width, bytes_accessed=6 * rows * width, transcendentals=0
        ),
        name="item_gradients",
    )(weights, *queries)


def join_kernel(pool_rows, own_ref, taken_ref, pool_ref, passage_ref):
    grad = (own_ref[...] + taken_ref[...].astype(f32)).astype(bf16)
    pool_ref[...] = grad[:pool_rows]
    passage_ref[...] = grad[pool_rows:]


def join_gradients(own, taken, pool_rows):
    rows, width = own.shape
    return pl.pallas_call(
        functools.partial(join_kernel, pool_rows),
        out_shape=[
            jax.ShapeDtypeStruct((pool_rows, width), bf16),
            jax.ShapeDtypeStruct((rows - pool_rows, width), bf16),
        ],
        compiler_params=params(16),
        cost_estimate=pl.CostEstimate(
            flops=rows * width, bytes_accessed=8 * rows * width, transcendentals=0
        ),
        name="join_item_gradients",
    )(own, taken)


def line_kernel(towers, part_rows, near_far, *refs):
    ins, refs = refs[:towers], refs[towers:]
    if near_far:
        near_ref, arrived_ref, *refs = refs
        plane_refs, refs = refs[:towers], refs[towers:]
        tower = lax.axis_index("tower")
        for d, out_ref in enumerate(plane_refs):
            rows = pl.ds(pl.multiple_of((tower ^ d) * part_rows, 16), part_rows)
            total = near_ref[rows, :].astype(f32) + arrived_ref[rows, :].astype(f32)
            out_ref[...] = total.astype(bf16)
    for s, out_ref in enumerate(refs):
        total = ins[0][s].astype(f32)
        for ref in ins[1:]:
            total += ref[s].astype(f32)
        out_ref[...] = total.astype(bf16)


def sum_lines(pieces, near=()):
    chips, rows, width = pieces[0].shape
    towers = len(pieces)
    outs = chips + (towers if near else 0)
    out = pl.pallas_call(
        functools.partial(line_kernel, towers, rows, len(near) > 0),
        out_shape=[jax.ShapeDtypeStruct((rows, width), bf16)] * outs,
        compiler_params=params(32),
        cost_estimate=pl.CostEstimate(
            flops=4 * outs * rows * width,
            bytes_accessed=10 * outs * rows * width,
            transcendentals=0,
        ),
        name="partial_sums",
    )(*pieces, *near)
    return (out[:towers], out[towers:]) if near else out


def shards(query_hidden, passage_hidden, pool_hidden, query_proj, passage_proj, negative_ids):
    towers = lax.axis_size("tower")
    dp_size = lax.axis_size("dp")
    chips = dp_size // 2
    query_rows = query_hidden.shape[0]
    part_rows = query_rows // towers
    pool_rows = pool_hidden.shape[0]
    width = query_proj.shape[1]

    def moved(x, tower_step=0, place_step=0, core_step=0):
        pairs = []
        for source in range(towers * dp_size):
            t, d = divmod(source, dp_size)
            target = ((d // 2) ^ place_step) * 2 + ((d % 2) ^ core_step)
            pairs.append((source, (t ^ tower_step) * dp_size + target))
        return lax.ppermute(x, axes, pairs)

    ids = jnp.transpose(negative_ids)
    near_far = chips == group
    copies = towers * chips
    query_unit, part, digits = project_queries(query_hidden, query_proj, ids, part_rows)
    parts = [moved(part, place_step=s) for s in range(2 if near_far else 1, chips)]
    slabs = width // 128
    far = jnp.concatenate([x[: slabs * part_rows] for x in parts], axis=0)
    if near_far:
        next_digits = moved(digits, place_step=1)
        far, next_digits = lax.optimization_barrier((far, next_digits))
    spread = [far] + [moved(far, tower_step=d) for d in range(1, towers)]
    pool_hidden, part = lax.optimization_barrier((pool_hidden, part))
    items = project_items(pool_hidden, passage_hidden, passage_proj)
    sent_items, _ = lax.optimization_barrier((items, far))
    other = moved(sent_items, core_step=1)
    if near_far:
        sent_unit, _ = lax.optimization_barrier((query_unit, far))
        next_unit = moved(sent_unit, place_step=1)
        count = count_names([ids, next_digits] + parts, pool_rows, group * query_rows)
        exps, near_totals = score_near(
            query_unit, next_unit, items, other, count, query_rows, pool_rows
        )
        far_exps, totals, far_queries = score_far(
            spread, items, other, count, near_totals, query_rows, pool_rows, part_rows, copies
        )
        exps = [exps, far_exps]
        queries = [query_unit, next_unit, far_queries]
    else:
        ids = [ids] + [ids_of(x[slabs * part_rows :]) for x in parts]
        count = count_names([jnp.concatenate(ids, axis=1)], pool_rows, group * query_rows)
        tower = lax.axis_index("tower")
        near = query_unit.reshape(1, towers, part_rows, width)
        blocks = jnp.stack(
            [
                jnp.moveaxis(x.reshape(chips - 1, slabs, part_rows, 128), 1, 2).reshape(
                    chips - 1, part_rows, width
                )
                for x in spread
            ],
            axis=1,
        )
        blocks = jnp.take(blocks, tower ^ jnp.arange(towers), axis=1)
        queries = jnp.concatenate([near, blocks], axis=0).reshape(-1, width)
        exps, totals = score_joined(
            queries, items, other, count, query_rows, pool_rows, copies
        )
        exps = [exps]
        queries = [queries]
        shift = lax.axis_index("dp") // 2 // group
        turned = shift ^ jnp.arange(chips // group)
        totals = totals.reshape(copies, 2, chips // group, -1)
        totals = jnp.take(totals, turned, axis=2).reshape(copies, 2, -1)
    same_core = [
        [t * dp_size + 2 * z + c for t in range(towers) for z in range(chips)] for c in range(2)
    ]
    totals = lax.all_to_all(totals, axes, 0, 0, axis_index_groups=same_core)
    if not near_far:
        totals = totals.reshape(copies, 2, chips // group, -1)
        totals = jnp.take(totals, turned, axis=2).reshape(copies, 2, -1)
    weights, *grads = weigh(
        totals, exps, items, other, query_rows, pool_rows, part_rows, towers
    )
    own_grad, sent_grad = item_gradients(weights, queries, query_rows, pool_rows)
    if near_far:
        near_grad, next_grad, *grads = grads
    sums = [grads[0]] + [moved(grads[d], tower_step=d) for d in range(1, towers)]
    if near_far:
        plane, line = sum_lines(sums, (near_grad, moved(next_grad, place_step=1)))
        arrived = [moved(line[s - 2], place_step=s) for s in range(2, chips)]
        arrived += [moved(plane[d], tower_step=d) for d in range(1, towers)]
        own_line = plane[0]
    else:
        line = sum_lines(sums)
        arrived = [moved(line[s], place_step=s) for s in range(1, chips)]
        own_line = line[0]
    sent_grad, own_line = lax.optimization_barrier((sent_grad, own_line))
    taken_grad = moved(sent_grad, core_step=1)
    pool_grad, passage_grad = join_gradients(own_grad, taken_grad, pool_rows)
    own_line, pool_grad = lax.optimization_barrier((own_line, pool_grad))
    query_grad = own_line.astype(f32)
    for x in arrived:
        query_grad = query_grad + x.astype(f32)
    return (query_grad.astype(bf16), passage_grad, pool_grad)


def solution(mesh):
    placed = (
        P("dp", None),
        P(("tower", "dp"), None),
        P(("tower", "dp"), None),
        P(),
        P(),
        P("dp", None),
    )
    return jax.shard_map(
        shards,
        mesh=mesh,
        in_specs=placed,
        out_specs=(P(("dp", "tower"), None), P(("tower", "dp"), None), P(("tower", "dp"), None)),
        check_vma=False,
    )
```

```python
import functools

import jax
import jax.numpy as jnp
from jax import lax
from jax.experimental import pallas as pl
from jax.experimental.pallas import tpu as pltpu
from jax.sharding import PartitionSpec as P

logit_scale = 50.0
axes = ("tower", "dp")
group = 4
f32 = jnp.float32
bf16 = jnp.bfloat16
last_last = (((1,), (1,)), ((), ()))
first_first = (((0,), (0,)), ((), ()))


def block_step(blocks):
    return pl.program_id(0) if blocks > 1 else 0


def grid_of(blocks, in_specs, out_specs):
    if blocks == 1:
        return {}
    return {"grid": (blocks,), "in_specs": in_specs, "out_specs": out_specs}


def params(mib):
    return pltpu.CompilerParams(vmem_limit_bytes=int(mib * 2**20))


def normalized(projected):
    squares = jnp.sum(projected * projected, axis=1, keepdims=True)
    return (projected * lax.rsqrt(squares + 1e-06)).astype(bf16)


def digits_of(ids):
    rows = ids.shape[1]
    full = rows // 128 * 128
    assert rows - full == 64 and full == 128
    high = ((ids >> 8) - 256).astype(f32)
    low = (ids & 255).astype(f32)
    last = jnp.concatenate([high[:, full:], low[:, full:]], axis=1)
    return jnp.concatenate([high[:, :full], low[:, :full], last], axis=0).astype(bf16)


def ids_of(digits):
    digits = digits.astype(f32).astype(jnp.int32)
    count = digits.shape[0] // 3
    last = digits[2 * count :]
    high = jnp.concatenate([digits[:count], last[:, :64]], axis=1)
    low = jnp.concatenate([digits[count : 2 * count], last[:, 64:]], axis=1)
    return ((high + 256) << 8) + low


def query_kernel(steps, part_rows, hidden_ref, weight_ref, ids_ref, unit_ref, part_ref, digits_ref, hidden, weight, ids_near, sems, ids_sem):
    depth = weight.shape[0] // steps
    copies = []
    for k in range(steps):
        span = pl.ds(k * depth, depth)
        copies.append(
            (
                pltpu.make_async_copy(hidden_ref.at[:, span], hidden.at[:, span], sems.at[0, k]),
                pltpu.make_async_copy(weight_ref.at[span, :], weight.at[span, :], sems.at[1, k]),
            )
        )
    ids_copy = pltpu.make_async_copy(ids_ref, ids_near, ids_sem)
    ids_copy.start()
    for pair in copies:
        for copy in pair:
            copy.start()
    ids_copy.wait()
    digits = digits_of(ids_near[...])
    slabs = weight.shape[1] // 128
    part_ref[slabs * part_rows :, :] = digits
    digits_ref[...] = digits
    total = None
    for k, pair in enumerate(copies):
        for copy in pair:
            copy.wait()
        span = slice(k * depth, (k + 1) * depth)
        product = jnp.dot(hidden[:, span], weight[span, :], preferred_element_type=f32)
        total = product if total is None else total + product
    unit_ref[...] = normalized(total)
    start = pl.multiple_of(lax.axis_index("tower") * part_rows, 16)
    for k in range(slabs):
        part_ref[k * part_rows : (k + 1) * part_rows, :] = unit_ref[
            pl.ds(start, part_rows), k * 128 : (k + 1) * 128
        ]


def project_queries(hidden, weight, ids, part_rows):
    rows, depth = hidden.shape
    width = weight.shape[1]
    steps = 3
    extra = 3 * ids.shape[0]
    far = pl.BlockSpec(memory_space=pltpu.HBM)
    near = pl.BlockSpec(memory_space=pltpu.VMEM)
    return pl.pallas_call(
        functools.partial(query_kernel, steps, part_rows),
        in_specs=[far, far, far],
        out_specs=[near, near, near],
        out_shape=[
            jax.ShapeDtypeStruct((rows, width), bf16),
            jax.ShapeDtypeStruct((part_rows * width // 128 + extra, 128), bf16),
            jax.ShapeDtypeStruct((extra, 128), bf16),
        ],
        scratch_shapes=[
            pltpu.VMEM((rows, depth), bf16),
            pltpu.VMEM((depth, width), bf16),
            pltpu.VMEM(ids.shape, jnp.int32),
            pltpu.SemaphoreType.DMA((2, steps)),
            pltpu.SemaphoreType.DMA,
        ],
        compiler_params=params(24),
        cost_estimate=pl.CostEstimate(
            flops=16 * rows * depth * width,
            bytes_accessed=12 * depth * (rows + width),
            transcendentals=0,
        ),
        name="query_units",
    )(
        pltpu.with_memory_space_constraint(hidden, pltpu.HBM),
        pltpu.with_memory_space_constraint(weight, pltpu.HBM),
        pltpu.with_memory_space_constraint(ids, pltpu.HBM),
    )


def item_kernel(pool_ref, passage_ref, weight_ref, unit_ref):
    hidden = jnp.concatenate([pool_ref[...], passage_ref[...]], axis=0)
    unit_ref[...] = normalized(
        jnp.dot(hidden, weight_ref[...], preferred_element_type=f32)
    )


def project_items(pool, passage, weight):
    depth, width = weight.shape
    rows = pool.shape[0] + passage.shape[0]
    return pl.pallas_call(
        item_kernel,
        out_shape=jax.ShapeDtypeStruct((rows, width), bf16),
        compiler_params=params(24),
        cost_estimate=pl.CostEstimate(
            flops=2 * rows * depth * width,
            bytes_accessed=2 * depth * (rows + width),
            transcendentals=0,
        ),
        name="item_units",
    )(pool, passage, weight)


def count_kernel(pool_rows, extra, *refs):
    ids_ref, *digit_refs, count_ref = refs
    own = lax.axis_index("tower") * lax.axis_size("dp") + lax.axis_index("dp")
    ids = [ids_ref[...]]
    for ref in digit_refs:
        ids.append(ids_of(ref[-extra:, :]))
    ids = jnp.concatenate(ids, axis=1)
    neg_count, queries = ids.shape
    chunk = 64

    for half in range(2):
        base = (own ^ half) * pool_rows
        local = ids - base

        @pl.loop(0, pool_rows // chunk)
        def _(step):
            rows = lax.broadcasted_iota(jnp.int32, (chunk, queries), 0) + step * chunk
            count = jnp.zeros((chunk, queries), f32)
            for k in range(neg_count):
                count += jnp.where(rows == local[k : k + 1, :], 1.0, 0.0)
            start = pl.multiple_of(half * pool_rows + step * chunk, chunk)
            count_ref[pl.ds(start, chunk), :] = count.astype(bf16)


def count_names(pieces, pool_rows, block):
    neg_count, queries = pieces[0].shape
    if len(pieces) == 1:
        specs = [pl.BlockSpec((neg_count, block), lambda g: (0, g))]
    else:
        queries *= len(pieces)
        specs = [pl.BlockSpec(x.shape, lambda g: (0, 0)) for x in pieces]
    return pl.pallas_call(
        functools.partial(count_kernel, pool_rows, 3 * neg_count),
        out_shape=jax.ShapeDtypeStruct((2 * pool_rows, queries), bf16),
        **grid_of(
            queries // block, specs, pl.BlockSpec((2 * pool_rows, block), lambda g: (0, g))
        ),
        compiler_params=params(16),
        cost_estimate=pl.CostEstimate(
            flops=6 * queries * neg_count * pool_rows,
            bytes_accessed=4 * pool_rows * queries,
            transcendentals=0,
        ),
        name="name_counts",
    )(*pieces)


def positive_mask(query_rows, own_rows, half, first_lane, block, blocks):
    dp_size = lax.axis_size("dp")
    tower, dp = lax.axis_index("tower"), lax.axis_index("dp")
    lane = lax.broadcasted_iota(jnp.int32, (1, block), 1) + first_lane
    query = jnp.zeros((1, block), jnp.int32)
    for k in range(group):
        step = block_step(blocks) * group + k
        start = (((dp // 2) ^ step) * 2 + dp % 2) * query_rows
        query = jnp.where(
            (lane >= k * query_rows) & (lane < (k + 1) * query_rows),
            start + lane - k * query_rows,
            query,
        )
    first = (tower * dp_size + (dp ^ half)) * own_rows
    passage = lax.broadcasted_iota(jnp.int32, (own_rows, block), 0) + first
    return passage == query


def placed_totals(totals, query_rows):
    place = (lax.axis_index("dp") // 2) % group
    out = totals
    for k in range(1, group):
        turned = jnp.concatenate(
            [
                totals[:, (j ^ k) * query_rows : ((j ^ k) + 1) * query_rows]
                for j in range(group)
            ],
            axis=1,
        )
        out = jnp.where(place == k, turned, out)
    return out


def score_tile(
    items_refs, queries, count_ref, exp_ref, start, offset, query_rows, pool_rows, blocks
):
    chunk = queries.shape[0]
    own_rows = items_refs[0].shape[0] - pool_rows
    lanes = slice(start, start + chunk)
    hard = jnp.zeros((1, chunk), f32)
    batch = jnp.zeros((1, chunk), f32)
    for half, items_ref in enumerate(items_refs):
        scores = lax.dot_general(items_ref[...], queries, last_last, preferred_element_type=f32)
        exps = jnp.exp(logit_scale * scores)
        rows = slice(half * pool_rows, (half + 1) * pool_rows)
        named = exps[:pool_rows] * count_ref[
            rows, offset + start : offset + start + chunk
        ].astype(f32)
        hard += jnp.sum(named, axis=0, keepdims=True)
        exp_ref[rows, lanes] = named.astype(bf16)
        mask = positive_mask(query_rows, own_rows, half, offset + start, chunk, blocks)
        hard += jnp.sum(jnp.where(mask, exps[pool_rows:], 0.0), axis=0, keepdims=True)
        batch += jnp.sum(exps[pool_rows:], axis=0, keepdims=True)
        row = 2 * pool_rows + half * own_rows
        exp_ref[row : row + own_rows, lanes] = exps[pool_rows:].astype(bf16)
    return jnp.concatenate([batch, hard], axis=0)


def score_tiles(
    items_refs, queries_ref, count_ref, exp_ref, offset, query_rows, pool_rows, blocks
):
    block = queries_ref.shape[0]
    chunk = 256 if block % 256 == 0 else block
    sums = []
    for start in range(0, block, chunk):
        queries = queries_ref[start : start + chunk, :]
        sums.append(
            score_tile(
                items_refs,
                queries,
                count_ref,
                exp_ref,
                start,
                offset,
                query_rows,
                pool_rows,
                blocks,
            )
        )
    return jnp.concatenate(sums, axis=1)


def joined_kernel(blocks, copies, query_rows, pool_rows, queries_ref, own_ref, other_ref, count_ref, *outs):
    exp_ref, totals_ref = outs
    totals = score_tiles(
        (own_ref, other_ref), queries_ref, count_ref, exp_ref, 0, query_rows, pool_rows, blocks
    )
    totals = placed_totals(totals, query_rows)
    for k in range(copies):
        totals_ref[k] = totals


def far_kernel(copies, query_rows, pool_rows, part_rows, towers, *refs):
    far_refs, refs = refs[:towers], refs[towers:]
    own_ref, other_ref, count_ref, near_ref, exp_ref, totals_ref, queries_ref = refs
    tower = lax.axis_index("tower")
    slabs = queries_ref.shape[1] // 128
    for d in range(towers):
        for s in range(queries_ref.shape[0] // query_rows):
            start = pl.multiple_of(s * query_rows + (tower ^ d) * part_rows, 16)
            for k in range(slabs):
                queries_ref[pl.ds(start, part_rows), k * 128 : (k + 1) * 128] = far_refs[d][
                    (s * slabs + k) * part_rows : (s * slabs + k + 1) * part_rows, :
                ]
    items = (own_ref, other_ref)
    totals = score_tiles(
        items, queries_ref, count_ref, exp_ref, 2 * query_rows, query_rows, pool_rows, 1
    )
    totals = placed_totals(jnp.concatenate([near_ref[...], totals], axis=1), query_rows)
    for k in range(copies):
        totals_ref[k] = totals


def near_kernel(query_rows, pool_rows, *refs):
    unit_ref, next_ref, own_ref, other_ref, count_ref, exp_ref, totals_ref, queries = refs
    queries[:query_rows, :] = unit_ref[...]
    queries[query_rows:, :] = next_ref[...]
    totals_ref[...] = score_tiles(
        (own_ref, other_ref), queries, count_ref, exp_ref, 0, query_rows, pool_rows, 1
    )


def score_cost(rows, queries, width):
    return pl.CostEstimate(
        flops=2 * rows * queries * width,
        bytes_accessed=4 * rows * queries,
        transcendentals=rows * queries,
    )


def score_joined(queries, items, other, count, query_rows, pool_rows, copies):
    total, width = queries.shape
    block = group * query_rows
    rows = 2 * items.shape[0]
    whole = lambda x: pl.BlockSpec(x.shape, lambda g: (0, 0))
    return pl.pallas_call(
        functools.partial(joined_kernel, total // block, copies, query_rows, pool_rows),
        grid=(total // block,),
        in_specs=[
            pl.BlockSpec((block, width), lambda g: (g, 0)),
            whole(items),
            whole(other),
            pl.BlockSpec((2 * pool_rows, block), lambda g: (0, g)),
        ],
        out_specs=[
            pl.BlockSpec((rows, block), lambda g: (0, g)),
            pl.BlockSpec((copies, 2, block), lambda g: (0, 0, g)),
        ],
        out_shape=[
            jax.ShapeDtypeStruct((rows, total), bf16),
            jax.ShapeDtypeStruct((copies, 2, total), f32),
        ],
        compiler_params=params(40),
        cost_estimate=score_cost(rows, total, width),
        name="scores",
    )(queries, items, other, count)


def score_far(spread, items, other, count, near, query_rows, pool_rows, part_rows, copies):
    rows, width = 2 * items.shape[0], items.shape[1]
    queries = (group - 2) * query_rows
    return pl.pallas_call(
        functools.partial(far_kernel, copies, query_rows, pool_rows, part_rows, len(spread)),
        out_shape=[
            jax.ShapeDtypeStruct((rows, queries), bf16),
            jax.ShapeDtypeStruct((copies, 2, group * query_rows), f32),
            jax.ShapeDtypeStruct((queries, width), bf16),
        ],
        compiler_params=params(32),
        cost_estimate=score_cost(rows, queries, width),
        name="far_scores",
    )(*spread, items, other, count, near)


def score_near(unit, next_unit, items, other, count, query_rows, pool_rows):
    rows, width = 2 * items.shape[0], items.shape[1]
    queries = 2 * query_rows
    return pl.pallas_call(
        functools.partial(near_kernel, query_rows, pool_rows),
        out_shape=[
            jax.ShapeDtypeStruct((rows, queries), bf16),
            jax.ShapeDtypeStruct((2, queries), f32),
        ],
        scratch_shapes=[pltpu.VMEM((queries, width), bf16)],
        compiler_params=params(32),
        cost_estimate=score_cost(rows, queries, width),
        name="near_scores",
    )(unit, next_unit, items, other, count)


def weight_kernel(blocks, exp_count, query_rows, pool_rows, own_rows, part_rows, towers, *refs):
    totals_ref, refs = refs[0], refs[1:]
    exp_refs, refs = refs[:exp_count], refs[exp_count:]
    own_ref, other_ref, weight_ref, *grad_refs = refs
    totals = placed_totals(jnp.sum(totals_ref[...], axis=0), query_rows)
    scale = 1.0 / totals
    pools = 2 * pool_rows
    first = 0
    for exp_ref in exp_refs:
        block = exp_ref.shape[1]
        lanes = slice(first, first + block)
        batch, hard = scale[0:1, lanes], scale[1:2, lanes]
        weight_ref[:pools, lanes] = (exp_ref[:pools, :].astype(f32) * hard).astype(bf16)
        for half in range(2):
            row = pools + half * own_rows
            exps = exp_ref[row : row + own_rows, :].astype(f32)
            mask = positive_mask(query_rows, own_rows, half, first, block, blocks)
            weight_ref[row : row + own_rows, lanes] = (
                exps * batch + jnp.where(mask, exps * hard - 2.0, 0.0)
            ).astype(bf16)
        first += block
    tower = lax.axis_index("tower")
    items = jnp.concatenate(
        [
            own_ref[:pool_rows, :],
            other_ref[:pool_rows, :],
            own_ref[pool_rows:, :],
            other_ref[pool_rows:, :],
        ],
        axis=0,
    )
    grad = logit_scale * lax.dot_general(
        weight_ref[...], items, first_first, preferred_element_type=f32
    )
    grad = grad.astype(bf16)
    if exp_count == 2:
        near_ref, next_ref, *grad_refs = grad_refs
        near_ref[...] = grad[:query_rows]
        next_ref[...] = grad[query_rows : 2 * query_rows]
        grad = grad[2 * query_rows :]
    grad = grad.reshape(-1, towers, part_rows, grad.shape[1])
    for t in range(towers):
        for d in range(towers):

            @pl.when((tower ^ d) == t)
            def _(t=t, d=d):
                grad_refs[d][...] = grad[:, t]


def weigh(totals, exps, items, other, query_rows, pool_rows, part_rows, towers):
    rows, width = items.shape
    queries = sum(x.shape[1] for x in exps)
    block = group * query_rows
    whole = lambda x: pl.BlockSpec(x.shape, lambda g: (0, 0))
    tall = pl.BlockSpec((2 * rows, block), lambda g: (0, g))
    near = pl.BlockSpec((query_rows, width), lambda g: (0, 0))
    if len(exps) == 1:
        exp_specs, out_specs, out_shape, sent = [tall], [], [], group
    else:
        exp_specs = [whole(x) for x in exps]
        out_specs = [near, near]
        out_shape = [jax.ShapeDtypeStruct((query_rows, width), bf16)] * 2
        sent = group - 2
    blocks = queries // block
    return pl.pallas_call(
        functools.partial(
            weight_kernel,
            blocks,
            len(exps),
            query_rows,
            pool_rows,
            rows - pool_rows,
            part_rows,
            towers,
        ),
        **grid_of(
            blocks,
            [pl.BlockSpec((totals.shape[0], 2, block), lambda g: (0, 0, g))]
            + exp_specs
            + [whole(items), whole(other)],
            [tall]
            + out_specs
            + [pl.BlockSpec((sent, part_rows, width), lambda g: (g, 0, 0))] * towers,
        ),
        out_shape=[jax.ShapeDtypeStruct((2 * rows, queries), bf16)]
        + out_shape
        + [jax.ShapeDtypeStruct((sent * blocks, part_rows, width), bf16)] * towers,
        compiler_params=params(40),
        cost_estimate=pl.CostEstimate(
            flops=4 * rows * queries * width,
            bytes_accessed=8 * rows * queries,
            transcendentals=0,
        ),
        name="weights",
    )(totals, *exps, items, other)


def gradient_kernel(steps, query_count, pool_rows, own_rows, weight_ref, *refs):
    query_refs, refs = refs[:query_count], refs[query_count:]
    own_ref, sent_ref, *scratch = refs
    step = block_step(steps)
    if len(query_refs) == 1:
        queries = query_refs[0][...]
    else:
        unit_ref, next_ref, far_ref = query_refs
        queries = jnp.concatenate(
            [unit_ref[...], next_ref[...], far_ref[...]], axis=0
        )
    product = jnp.dot(weight_ref[...], queries, preferred_element_type=f32)

    def finish(total):
        pools = 2 * pool_rows
        own_ref[:pool_rows, :] = logit_scale * total[:pool_rows, :]
        own_ref[pool_rows:, :] = logit_scale * total[pools : pools + own_rows, :]
        sent_ref[:pool_rows, :] = (logit_scale * total[pool_rows:pools, :]).astype(bf16)
        sent_ref[pool_rows:, :] = (logit_scale * total[pools + own_rows :, :]).astype(bf16)

    if steps == 1:
        finish(product)
        return
    (total,) = scratch

    @pl.when(step == 0)
    def _():
        total[...] = product

    @pl.when(step > 0)
    def _():
        total[...] += product

    @pl.when(step == steps - 1)
    def _():
        finish(total[...])


def item_gradients(weights, queries, query_rows, pool_rows):
    rows, total = weights.shape
    half = rows // 2
    width = queries[0].shape[1]
    block = group * query_rows
    blocks = total // block
    fixed = pl.BlockSpec((half, width), lambda g: (0, 0))
    if len(queries) == 1:
        query_specs = [pl.BlockSpec((block, width), lambda g: (g, 0))]
    else:
        query_specs = [pl.BlockSpec(x.shape, lambda g: (0, 0)) for x in queries]
    return pl.pallas_call(
        functools.partial(
            gradient_kernel, blocks, len(queries), pool_rows, half - pool_rows
        ),
        **grid_of(
            blocks,
            [pl.BlockSpec((rows, block), lambda g: (0, g))] + query_specs,
            [fixed, fixed],
        ),
        out_shape=[
            jax.ShapeDtypeStruct((half, width), f32),
            jax.ShapeDtypeStruct((half, width), bf16),
        ],
        scratch_shapes=[pltpu.VMEM((rows, width), f32)] if blocks > 1 else [],
        compiler_params=params(40),
        cost_estimate=pl.CostEstimate(
            flops=2 * rows * total * width, bytes_accessed=6 * rows * width, transcendentals=0
        ),
        name="item_gradients",
    )(weights, *queries)


def join_kernel(pool_rows, own_ref, taken_ref, pool_ref, passage_ref):
    grad = (own_ref[...] + taken_ref[...].astype(f32)).astype(bf16)
    pool_ref[...] = grad[:pool_rows]
    passage_ref[...] = grad[pool_rows:]


def join_gradients(own, taken, pool_rows):
    rows, width = own.shape
    return pl.pallas_call(
        functools.partial(join_kernel, pool_rows),
        out_shape=[
            jax.ShapeDtypeStruct((pool_rows, width), bf16),
            jax.ShapeDtypeStruct((rows - pool_rows, width), bf16),
        ],
        compiler_params=params(16),
        cost_estimate=pl.CostEstimate(
            flops=rows * width, bytes_accessed=8 * rows * width, transcendentals=0
        ),
        name="join_item_gradients",
    )(own, taken)


def line_kernel(towers, part_rows, near_far, *refs):
    ins, refs = refs[:towers], refs[towers:]
    if near_far:
        near_ref, arrived_ref, *refs = refs
        plane_refs, refs = refs[:towers], refs[towers:]
        tower = lax.axis_index("tower")
        for d, out_ref in enumerate(plane_refs):
            rows = pl.ds(pl.multiple_of((tower ^ d) * part_rows, 16), part_rows)
            total = near_ref[rows, :].astype(f32) + arrived_ref[rows, :].astype(f32)
            out_ref[...] = total.astype(bf16)
    for s, out_ref in enumerate(refs):
        total = ins[0][s].astype(f32)
        for ref in ins[1:]:
            total += ref[s].astype(f32)
        out_ref[...] = total.astype(bf16)


def sum_lines(pieces, near=()):
    chips, rows, width = pieces[0].shape
    towers = len(pieces)
    outs = chips + (towers if near else 0)
    out = pl.pallas_call(
        functools.partial(line_kernel, towers, rows, len(near) > 0),
        out_shape=[jax.ShapeDtypeStruct((rows, width), bf16)] * outs,
        compiler_params=params(32),
        cost_estimate=pl.CostEstimate(
            flops=4 * outs * rows * width,
            bytes_accessed=10 * outs * rows * width,
            transcendentals=0,
        ),
        name="partial_sums",
    )(*pieces, *near)
    return (out[:towers], out[towers:]) if near else out


def shards(query_hidden, passage_hidden, pool_hidden, query_proj, passage_proj, negative_ids):
    towers = lax.axis_size("tower")
    dp_size = lax.axis_size("dp")
    chips = dp_size // 2
    query_rows = query_hidden.shape[0]
    part_rows = query_rows // towers
    pool_rows = pool_hidden.shape[0]
    width = query_proj.shape[1]

    def moved(x, tower_step=0, place_step=0, core_step=0):
        pairs = []
        for source in range(towers * dp_size):
            t, d = divmod(source, dp_size)
            target = ((d // 2) ^ place_step) * 2 + ((d % 2) ^ core_step)
            pairs.append((source, (t ^ tower_step) * dp_size + target))
        return lax.ppermute(x, axes, pairs)

    ids = jnp.transpose(negative_ids)
    near_far = chips == group
    copies = towers * chips
    query_unit, part, digits = project_queries(query_hidden, query_proj, ids, part_rows)
    if near_far:
        parts = {s: moved(part, place_step=s) for s in [2, 3]}
        parts = [parts[s] for s in range(2, chips)]
    else:
        parts = [moved(part, place_step=s) for s in range(1, chips)]
    slabs = width // 128
    far = jnp.concatenate([x[: slabs * part_rows] for x in parts], axis=0)
    if near_far:
        next_digits = moved(digits, place_step=1)
        far, next_digits = lax.optimization_barrier((far, next_digits))
    spread = {d: moved(far, tower_step=d) for d in [1, 2, 3]}
    spread = [far] + [spread[d] for d in range(1, towers)]
    pool_hidden, part = lax.optimization_barrier((pool_hidden, part))
    items = project_items(pool_hidden, passage_hidden, passage_proj)
    sent_items, _ = lax.optimization_barrier((items, far))
    other = moved(sent_items, core_step=1)
    if near_far:
        sent_unit, _ = lax.optimization_barrier((query_unit, far))
        next_unit = moved(sent_unit, place_step=1)
        count = count_names([ids, next_digits] + parts, pool_rows, group * query_rows)
        exps, near_totals = score_near(
            query_unit, next_unit, items, other, count, query_rows, pool_rows
        )
        far_exps, totals, far_queries = score_far(
            spread, items, other, count, near_totals, query_rows, pool_rows, part_rows, copies
        )
        exps = [exps, far_exps]
        queries = [query_unit, next_unit, far_queries]
    else:
        ids = [ids] + [ids_of(x[slabs * part_rows :]) for x in parts]
        count = count_names([jnp.concatenate(ids, axis=1)], pool_rows, group * query_rows)
        tower = lax.axis_index("tower")
        near = query_unit.reshape(1, towers, part_rows, width)
        blocks = jnp.stack(
            [
                jnp.moveaxis(x.reshape(chips - 1, slabs, part_rows, 128), 1, 2).reshape(
                    chips - 1, part_rows, width
                )
                for x in spread
            ],
            axis=1,
        )
        blocks = jnp.take(blocks, tower ^ jnp.arange(towers), axis=1)
        queries = jnp.concatenate([near, blocks], axis=0).reshape(-1, width)
        exps, totals = score_joined(
            queries, items, other, count, query_rows, pool_rows, copies
        )
        exps = [exps]
        queries = [queries]
        shift = lax.axis_index("dp") // 2 // group
        turned = shift ^ jnp.arange(chips // group)
        totals = totals.reshape(copies, 2, chips // group, -1)
        totals = jnp.take(totals, turned, axis=2).reshape(copies, 2, -1)
    same_core = [
        [t * dp_size + 2 * z + c for t in range(towers) for z in range(chips)] for c in range(2)
    ]
    totals = lax.all_to_all(totals, axes, 0, 0, axis_index_groups=same_core)
    if not near_far:
        totals = totals.reshape(copies, 2, chips // group, -1)
        totals = jnp.take(totals, turned, axis=2).reshape(copies, 2, -1)
    weights, *grads = weigh(
        totals, exps, items, other, query_rows, pool_rows, part_rows, towers
    )
    own_grad, sent_grad = item_gradients(weights, queries, query_rows, pool_rows)
    if near_far:
        near_grad, next_grad, *grads = grads
    far_sums = [moved(grads[d], tower_step=d) for d in [3, 2, 1]]
    sums = [grads[0]] + far_sums
    if near_far:
        plane, line = sum_lines(sums, (near_grad, moved(next_grad, place_step=1)))
        arrived = [moved(line[s - 2], place_step=s) for s in [3, 2]]
        arrived += [moved(plane[d], tower_step=d) for d in [3, 2, 1]]
        own_line = plane[0]
    else:
        line = sum_lines(sums)
        arrived = [moved(line[s], place_step=s) for s in range(1, chips)]
        own_line = line[0]
    sent_grad, own_line = lax.optimization_barrier((sent_grad, own_line))
    taken_grad = moved(sent_grad, core_step=1)
    pool_grad, passage_grad = join_gradients(own_grad, taken_grad, pool_rows)
    own_line, pool_grad = lax.optimization_barrier((own_line, pool_grad))
    query_grad = own_line.astype(f32)
    for x in arrived:
        query_grad = query_grad + x.astype(f32)
    return (query_grad.astype(bf16), passage_grad, pool_grad)


def solution(mesh):
    placed = (
        P("dp", None),
        P(("tower", "dp"), None),
        P(("tower", "dp"), None),
        P(),
        P(),
        P("dp", None),
    )
    return jax.shard_map(
        shards,
        mesh=mesh,
        in_specs=placed,
        out_specs=(P(("dp", "tower"), None), P(("tower", "dp"), None), P(("tower", "dp"), None)),
        check_vma=False,
    )
```

```python
import functools

import jax
import jax.numpy as jnp
from jax import lax
from jax.experimental import pallas as pl
from jax.experimental.pallas import tpu as pltpu
from jax.sharding import PartitionSpec as P

logit_scale = 50.0
axes = ("tower", "dp")
group = 4
f32 = jnp.float32
bf16 = jnp.bfloat16
last_last = (((1,), (1,)), ((), ()))
first_first = (((0,), (0,)), ((), ()))


def block_step(blocks):
    return pl.program_id(0) if blocks > 1 else 0


def grid_of(blocks, in_specs, out_specs):
    if blocks == 1:
        return {}
    return {"grid": (blocks,), "in_specs": in_specs, "out_specs": out_specs}


def params(mib):
    return pltpu.CompilerParams(vmem_limit_bytes=int(mib * 2**20))


def normalized(projected):
    squares = jnp.sum(projected * projected, axis=1, keepdims=True)
    return (projected * lax.rsqrt(squares + 1e-06)).astype(bf16)


def digits_of(ids):
    rows = ids.shape[1]
    full = rows // 128 * 128
    assert rows - full == 64 and full == 128
    high = ((ids >> 8) - 256).astype(f32)
    low = (ids & 255).astype(f32)
    last = jnp.concatenate([high[:, full:], low[:, full:]], axis=1)
    return jnp.concatenate([high[:, :full], low[:, :full], last], axis=0).astype(bf16)


def ids_of(digits):
    digits = digits.astype(f32).astype(jnp.int32)
    count = digits.shape[0] // 3
    last = digits[2 * count :]
    high = jnp.concatenate([digits[:count], last[:, :64]], axis=1)
    low = jnp.concatenate([digits[count : 2 * count], last[:, 64:]], axis=1)
    return ((high + 256) << 8) + low


def query_kernel(steps, part_rows, hidden_ref, weight_ref, ids_ref, unit_ref, part_ref, head_ref, rest_ref, hidden, weight, ids_near, sems, ids_sem):
    depth = weight.shape[0] // steps
    copies = []
    for k in range(steps):
        span = pl.ds(k * depth, depth)
        copies.append(
            (
                pltpu.make_async_copy(hidden_ref.at[:, span], hidden.at[:, span], sems.at[0, k]),
                pltpu.make_async_copy(weight_ref.at[span, :], weight.at[span, :], sems.at[1, k]),
            )
        )
    ids_copy = pltpu.make_async_copy(ids_ref, ids_near, ids_sem)
    ids_copy.start()
    for pair in copies:
        for copy in pair:
            copy.start()
    ids_copy.wait()
    digits = digits_of(ids_near[...])
    slabs = weight.shape[1] // 128
    part_ref[slabs * part_rows :, :] = digits
    head_rows = unit_ref.shape[0] - rest_ref.shape[0]
    head_ref[slabs * head_rows :, :] = digits
    total = None
    for k, pair in enumerate(copies):
        for copy in pair:
            copy.wait()
        span = slice(k * depth, (k + 1) * depth)
        product = jnp.dot(hidden[:, span], weight[span, :], preferred_element_type=f32)
        total = product if total is None else total + product
    unit_ref[...] = normalized(total)
    start = pl.multiple_of(lax.axis_index("tower") * part_rows, 16)
    rest_ref[...] = unit_ref[head_rows:, :]
    for k in range(slabs):
        head_ref[k * head_rows : (k + 1) * head_rows, :] = unit_ref[
            :head_rows, k * 128 : (k + 1) * 128
        ]
        part_ref[k * part_rows : (k + 1) * part_rows, :] = unit_ref[
            pl.ds(start, part_rows), k * 128 : (k + 1) * 128
        ]


def project_queries(hidden, weight, ids, part_rows):
    rows, depth = hidden.shape
    width = weight.shape[1]
    steps = 3
    extra = 3 * ids.shape[0]
    head = 1 * part_rows
    far = pl.BlockSpec(memory_space=pltpu.HBM)
    near = pl.BlockSpec(memory_space=pltpu.VMEM)
    return pl.pallas_call(
        functools.partial(query_kernel, steps, part_rows),
        in_specs=[far, far, far],
        out_specs=[near, near, near, near],
        out_shape=[
            jax.ShapeDtypeStruct((rows, width), bf16),
            jax.ShapeDtypeStruct((part_rows * width // 128 + extra, 128), bf16),
            jax.ShapeDtypeStruct((head * width // 128 + extra, 128), bf16),
            jax.ShapeDtypeStruct((rows - head, width), bf16),
        ],
        scratch_shapes=[
            pltpu.VMEM((rows, depth), bf16),
            pltpu.VMEM((depth, width), bf16),
            pltpu.VMEM(ids.shape, jnp.int32),
            pltpu.SemaphoreType.DMA((2, steps)),
            pltpu.SemaphoreType.DMA,
        ],
        compiler_params=params(24),
        cost_estimate=pl.CostEstimate(
            flops=16 * rows * depth * width,
            bytes_accessed=12 * depth * (rows + width),
            transcendentals=0,
        ),
        name="query_units",
    )(
        pltpu.with_memory_space_constraint(hidden, pltpu.HBM),
        pltpu.with_memory_space_constraint(weight, pltpu.HBM),
        pltpu.with_memory_space_constraint(ids, pltpu.HBM),
    )


def item_kernel(pool_ref, passage_ref, weight_ref, unit_ref):
    hidden = jnp.concatenate([pool_ref[...], passage_ref[...]], axis=0)
    unit_ref[...] = normalized(
        jnp.dot(hidden, weight_ref[...], preferred_element_type=f32)
    )


def project_items(pool, passage, weight):
    depth, width = weight.shape
    rows = pool.shape[0] + passage.shape[0]
    return pl.pallas_call(
        item_kernel,
        out_shape=jax.ShapeDtypeStruct((rows, width), bf16),
        compiler_params=params(24),
        cost_estimate=pl.CostEstimate(
            flops=2 * rows * depth * width,
            bytes_accessed=2 * depth * (rows + width),
            transcendentals=0,
        ),
        name="item_units",
    )(pool, passage, weight)


def count_kernel(pool_rows, extra, *refs):
    ids_ref, *digit_refs, count_ref = refs
    own = lax.axis_index("tower") * lax.axis_size("dp") + lax.axis_index("dp")
    ids = [ids_ref[...]]
    for ref in digit_refs:
        ids.append(ids_of(ref[-extra:, :]))
    ids = jnp.concatenate(ids, axis=1)
    neg_count, queries = ids.shape
    chunk = 64

    for half in range(2):
        base = (own ^ half) * pool_rows
        local = ids - base

        @pl.loop(0, pool_rows // chunk)
        def _(step):
            rows = lax.broadcasted_iota(jnp.int32, (chunk, queries), 0) + step * chunk
            count = jnp.zeros((chunk, queries), f32)
            for k in range(neg_count):
                count += jnp.where(rows == local[k : k + 1, :], 1.0, 0.0)
            start = pl.multiple_of(half * pool_rows + step * chunk, chunk)
            count_ref[pl.ds(start, chunk), :] = count.astype(bf16)


def count_names(pieces, pool_rows, block):
    neg_count, queries = pieces[0].shape
    if len(pieces) == 1:
        specs = [pl.BlockSpec((neg_count, block), lambda g: (0, g))]
    else:
        queries *= len(pieces)
        specs = [pl.BlockSpec(x.shape, lambda g: (0, 0)) for x in pieces]
    return pl.pallas_call(
        functools.partial(count_kernel, pool_rows, 3 * neg_count),
        out_shape=jax.ShapeDtypeStruct((2 * pool_rows, queries), bf16),
        **grid_of(
            queries // block, specs, pl.BlockSpec((2 * pool_rows, block), lambda g: (0, g))
        ),
        compiler_params=params(16),
        cost_estimate=pl.CostEstimate(
            flops=6 * queries * neg_count * pool_rows,
            bytes_accessed=4 * pool_rows * queries,
            transcendentals=0,
        ),
        name="name_counts",
    )(*pieces)


def positive_mask(query_rows, own_rows, half, first_lane, block, blocks):
    dp_size = lax.axis_size("dp")
    tower, dp = lax.axis_index("tower"), lax.axis_index("dp")
    lane = lax.broadcasted_iota(jnp.int32, (1, block), 1) + first_lane
    query = jnp.zeros((1, block), jnp.int32)
    for k in range(group):
        step = block_step(blocks) * group + k
        start = (((dp // 2) ^ step) * 2 + dp % 2) * query_rows
        query = jnp.where(
            (lane >= k * query_rows) & (lane < (k + 1) * query_rows),
            start + lane - k * query_rows,
            query,
        )
    first = (tower * dp_size + (dp ^ half)) * own_rows
    passage = lax.broadcasted_iota(jnp.int32, (own_rows, block), 0) + first
    return passage == query


def placed_totals(totals, query_rows):
    place = (lax.axis_index("dp") // 2) % group
    out = totals
    for k in range(1, group):
        turned = jnp.concatenate(
            [
                totals[:, (j ^ k) * query_rows : ((j ^ k) + 1) * query_rows]
                for j in range(group)
            ],
            axis=1,
        )
        out = jnp.where(place == k, turned, out)
    return out


def score_tile(
    items_refs, queries, count_ref, exp_ref, start, offset, query_rows, pool_rows, blocks
):
    chunk = queries.shape[0]
    own_rows = items_refs[0].shape[0] - pool_rows
    lanes = slice(start, start + chunk)
    hard = jnp.zeros((1, chunk), f32)
    batch = jnp.zeros((1, chunk), f32)
    for half, items_ref in enumerate(items_refs):
        scores = lax.dot_general(items_ref[...], queries, last_last, preferred_element_type=f32)
        exps = jnp.exp(logit_scale * scores)
        rows = slice(half * pool_rows, (half + 1) * pool_rows)
        named = exps[:pool_rows] * count_ref[
            rows, offset + start : offset + start + chunk
        ].astype(f32)
        hard += jnp.sum(named, axis=0, keepdims=True)
        exp_ref[rows, lanes] = named.astype(bf16)
        mask = positive_mask(query_rows, own_rows, half, offset + start, chunk, blocks)
        hard += jnp.sum(jnp.where(mask, exps[pool_rows:], 0.0), axis=0, keepdims=True)
        batch += jnp.sum(exps[pool_rows:], axis=0, keepdims=True)
        row = 2 * pool_rows + half * own_rows
        exp_ref[row : row + own_rows, lanes] = exps[pool_rows:].astype(bf16)
    return jnp.concatenate([batch, hard], axis=0)


def score_tiles(
    items_refs, queries_ref, count_ref, exp_ref, offset, query_rows, pool_rows, blocks
):
    block = queries_ref.shape[0]
    chunk = 256 if block % 256 == 0 else block
    sums = []
    for start in range(0, block, chunk):
        queries = queries_ref[start : start + chunk, :]
        sums.append(
            score_tile(
                items_refs,
                queries,
                count_ref,
                exp_ref,
                start,
                offset,
                query_rows,
                pool_rows,
                blocks,
            )
        )
    return jnp.concatenate(sums, axis=1)


def joined_kernel(blocks, copies, query_rows, pool_rows, queries_ref, own_ref, other_ref, count_ref, *outs):
    exp_ref, totals_ref = outs
    totals = score_tiles(
        (own_ref, other_ref), queries_ref, count_ref, exp_ref, 0, query_rows, pool_rows, blocks
    )
    totals = placed_totals(totals, query_rows)
    for k in range(copies):
        totals_ref[k] = totals


def far_kernel(copies, query_rows, pool_rows, part_rows, towers, *refs):
    far_refs, refs = refs[:towers], refs[towers:]
    own_ref, other_ref, count_ref, near_ref, exp_ref, totals_ref, queries_ref = refs
    tower = lax.axis_index("tower")
    slabs = queries_ref.shape[1] // 128
    for d in range(towers):
        for s in range(queries_ref.shape[0] // query_rows):
            start = pl.multiple_of(s * query_rows + (tower ^ d) * part_rows, 16)
            for k in range(slabs):
                queries_ref[pl.ds(start, part_rows), k * 128 : (k + 1) * 128] = far_refs[d][
                    (s * slabs + k) * part_rows : (s * slabs + k + 1) * part_rows, :
                ]
    items = (own_ref, other_ref)
    totals = score_tiles(
        items, queries_ref, count_ref, exp_ref, 2 * query_rows, query_rows, pool_rows, 1
    )
    totals = placed_totals(jnp.concatenate([near_ref[...], totals], axis=1), query_rows)
    for k in range(copies):
        totals_ref[k] = totals


def near_kernel(query_rows, pool_rows, *refs):
    unit_ref, head_ref, rest_ref, own_ref, other_ref, count_ref, exp_ref, totals_ref, queries = refs
    queries[:query_rows, :] = unit_ref[...]
    head_rows = query_rows - rest_ref.shape[0]
    for k in range(queries.shape[1] // 128):
        queries[query_rows : query_rows + head_rows, k * 128 : (k + 1) * 128] = head_ref[
            k * head_rows : (k + 1) * head_rows, :
        ]
    queries[query_rows + head_rows :, :] = rest_ref[...]
    totals_ref[...] = score_tiles(
        (own_ref, other_ref), queries, count_ref, exp_ref, 0, query_rows, pool_rows, 1
    )


def score_cost(rows, queries, width):
    return pl.CostEstimate(
        flops=2 * rows * queries * width,
        bytes_accessed=4 * rows * queries,
        transcendentals=rows * queries,
    )


def score_joined(queries, items, other, count, query_rows, pool_rows, copies):
    total, width = queries.shape
    block = group * query_rows
    rows = 2 * items.shape[0]
    whole = lambda x: pl.BlockSpec(x.shape, lambda g: (0, 0))
    return pl.pallas_call(
        functools.partial(joined_kernel, total // block, copies, query_rows, pool_rows),
        grid=(total // block,),
        in_specs=[
            pl.BlockSpec((block, width), lambda g: (g, 0)),
            whole(items),
            whole(other),
            pl.BlockSpec((2 * pool_rows, block), lambda g: (0, g)),
        ],
        out_specs=[
            pl.BlockSpec((rows, block), lambda g: (0, g)),
            pl.BlockSpec((copies, 2, block), lambda g: (0, 0, g)),
        ],
        out_shape=[
            jax.ShapeDtypeStruct((rows, total), bf16),
            jax.ShapeDtypeStruct((copies, 2, total), f32),
        ],
        compiler_params=params(40),
        cost_estimate=score_cost(rows, total, width),
        name="scores",
    )(queries, items, other, count)


def score_far(spread, items, other, count, near, query_rows, pool_rows, part_rows, copies):
    rows, width = 2 * items.shape[0], items.shape[1]
    queries = (group - 2) * query_rows
    return pl.pallas_call(
        functools.partial(far_kernel, copies, query_rows, pool_rows, part_rows, len(spread)),
        out_shape=[
            jax.ShapeDtypeStruct((rows, queries), bf16),
            jax.ShapeDtypeStruct((copies, 2, group * query_rows), f32),
            jax.ShapeDtypeStruct((queries, width), bf16),
        ],
        compiler_params=params(32),
        cost_estimate=score_cost(rows, queries, width),
        name="far_scores",
    )(*spread, items, other, count, near)


def score_near(unit, head, rest, items, other, count, query_rows, pool_rows):
    rows, width = 2 * items.shape[0], items.shape[1]
    queries = 2 * query_rows
    return pl.pallas_call(
        functools.partial(near_kernel, query_rows, pool_rows),
        out_shape=[
            jax.ShapeDtypeStruct((rows, queries), bf16),
            jax.ShapeDtypeStruct((2, queries), f32),
            jax.ShapeDtypeStruct((queries, width), bf16),
        ],
        compiler_params=params(32),
        cost_estimate=score_cost(rows, queries, width),
        name="near_scores",
    )(unit, head, rest, items, other, count)


def weight_kernel(blocks, exp_count, query_rows, pool_rows, own_rows, part_rows, towers, *refs):
    totals_ref, refs = refs[0], refs[1:]
    exp_refs, refs = refs[:exp_count], refs[exp_count:]
    own_ref, other_ref, weight_ref, *grad_refs = refs
    totals = placed_totals(jnp.sum(totals_ref[...], axis=0), query_rows)
    scale = logit_scale / totals
    pools = 2 * pool_rows
    first = 0
    for exp_ref in exp_refs:
        block = exp_ref.shape[1]
        lanes = slice(first, first + block)
        batch, hard = scale[0:1, lanes], scale[1:2, lanes]
        weight_ref[:pools, lanes] = (exp_ref[:pools, :].astype(f32) * hard).astype(bf16)
        for half in range(2):
            row = pools + half * own_rows
            exps = exp_ref[row : row + own_rows, :].astype(f32)
            mask = positive_mask(query_rows, own_rows, half, first, block, blocks)
            weight_ref[row : row + own_rows, lanes] = (
                exps * batch + jnp.where(mask, exps * hard - 2.0 * logit_scale, 0.0)
            ).astype(bf16)
        first += block
    tower = lax.axis_index("tower")
    items = jnp.concatenate(
        [
            own_ref[:pool_rows, :],
            other_ref[:pool_rows, :],
            own_ref[pool_rows:, :],
            other_ref[pool_rows:, :],
        ],
        axis=0,
    )
    grad = lax.dot_general(
        weight_ref[...], items, first_first, preferred_element_type=f32
    ).astype(bf16)
    if exp_count == 2:
        near_ref, next_ref, *grad_refs = grad_refs
        near_ref[...] = grad[:query_rows]
        next_ref[...] = grad[query_rows : 2 * query_rows]
        grad = grad[2 * query_rows :]
    grad = grad.reshape(-1, towers, part_rows, grad.shape[1])
    for t in range(towers):
        for d in range(towers):

            @pl.when((tower ^ d) == t)
            def _(t=t, d=d):
                grad_refs[d][...] = grad[:, t]


def weigh(totals, exps, items, other, query_rows, pool_rows, part_rows, towers):
    rows, width = items.shape
    queries = sum(x.shape[1] for x in exps)
    block = group * query_rows
    whole = lambda x: pl.BlockSpec(x.shape, lambda g: (0, 0))
    tall = pl.BlockSpec((2 * rows, block), lambda g: (0, g))
    near = pl.BlockSpec((query_rows, width), lambda g: (0, 0))
    if len(exps) == 1:
        exp_specs, out_specs, out_shape, sent = [tall], [], [], group
    else:
        exp_specs = [whole(x) for x in exps]
        out_specs = [near, near]
        out_shape = [jax.ShapeDtypeStruct((query_rows, width), bf16)] * 2
        sent = group - 2
    blocks = queries // block
    return pl.pallas_call(
        functools.partial(
            weight_kernel,
            blocks,
            len(exps),
            query_rows,
            pool_rows,
            rows - pool_rows,
            part_rows,
            towers,
        ),
        **grid_of(
            blocks,
            [pl.BlockSpec((totals.shape[0], 2, block), lambda g: (0, 0, g))]
            + exp_specs
            + [whole(items), whole(other)],
            [tall]
            + out_specs
            + [pl.BlockSpec((sent, part_rows, width), lambda g: (g, 0, 0))] * towers,
        ),
        out_shape=[jax.ShapeDtypeStruct((2 * rows, queries), bf16)]
        + out_shape
        + [jax.ShapeDtypeStruct((sent * blocks, part_rows, width), bf16)] * towers,
        compiler_params=params(40),
        cost_estimate=pl.CostEstimate(
            flops=4 * rows * queries * width,
            bytes_accessed=8 * rows * queries,
            transcendentals=0,
        ),
        name="weights",
    )(totals, *exps, items, other)


def gradient_kernel(steps, query_count, pool_rows, own_rows, weight_ref, *refs):
    query_refs, refs = refs[:query_count], refs[query_count:]
    own_ref, sent_ref, *scratch = refs
    step = block_step(steps)
    if len(query_refs) == 1:
        queries = query_refs[0][...]
    else:
        queries = jnp.concatenate([ref[...] for ref in query_refs], axis=0)
    product = jnp.dot(weight_ref[...], queries, preferred_element_type=f32)

    def finish(total):
        pools = 2 * pool_rows
        own_ref[:pool_rows, :] = total[:pool_rows, :]
        own_ref[pool_rows:, :] = total[pools : pools + own_rows, :]
        sent_ref[:pool_rows, :] = total[pool_rows:pools, :].astype(bf16)
        sent_ref[pool_rows:, :] = total[pools + own_rows :, :].astype(bf16)

    if steps == 1:
        finish(product)
        return
    (total,) = scratch

    @pl.when(step == 0)
    def _():
        total[...] = product

    @pl.when(step > 0)
    def _():
        total[...] += product

    @pl.when(step == steps - 1)
    def _():
        finish(total[...])


def item_gradients(weights, queries, query_rows, pool_rows):
    rows, total = weights.shape
    half = rows // 2
    width = queries[0].shape[1]
    block = group * query_rows
    blocks = total // block
    fixed = pl.BlockSpec((half, width), lambda g: (0, 0))
    if len(queries) == 1:
        query_specs = [pl.BlockSpec((block, width), lambda g: (g, 0))]
    else:
        query_specs = [pl.BlockSpec(x.shape, lambda g: (0, 0)) for x in queries]
    return pl.pallas_call(
        functools.partial(
            gradient_kernel, blocks, len(queries), pool_rows, half - pool_rows
        ),
        **grid_of(
            blocks,
            [pl.BlockSpec((rows, block), lambda g: (0, g))] + query_specs,
            [fixed, fixed],
        ),
        out_shape=[
            jax.ShapeDtypeStruct((half, width), f32),
            jax.ShapeDtypeStruct((half, width), bf16),
        ],
        scratch_shapes=[pltpu.VMEM((rows, width), f32)] if blocks > 1 else [],
        compiler_params=params(40),
        cost_estimate=pl.CostEstimate(
            flops=2 * rows * total * width, bytes_accessed=6 * rows * width, transcendentals=0
        ),
        name="item_gradients",
    )(weights, *queries)


def join_kernel(pool_rows, own_ref, taken_ref, pool_ref, passage_ref):
    grad = (own_ref[...] + taken_ref[...].astype(f32)).astype(bf16)
    pool_ref[...] = grad[:pool_rows]
    passage_ref[...] = grad[pool_rows:]


def join_gradients(own, taken, pool_rows):
    rows, width = own.shape
    return pl.pallas_call(
        functools.partial(join_kernel, pool_rows),
        out_shape=[
            jax.ShapeDtypeStruct((pool_rows, width), bf16),
            jax.ShapeDtypeStruct((rows - pool_rows, width), bf16),
        ],
        compiler_params=params(16),
        cost_estimate=pl.CostEstimate(
            flops=rows * width, bytes_accessed=8 * rows * width, transcendentals=0
        ),
        name="join_item_gradients",
    )(own, taken)


def line_kernel(towers, part_rows, near_far, *refs):
    ins, refs = refs[:towers], refs[towers:]
    if near_far:
        near_ref, arrived_ref, *refs = refs
        plane_refs, refs = refs[:towers], refs[towers:]
        tower = lax.axis_index("tower")
        for d, out_ref in enumerate(plane_refs):
            rows = pl.ds(pl.multiple_of((tower ^ d) * part_rows, 16), part_rows)
            total = near_ref[rows, :].astype(f32) + arrived_ref[rows, :].astype(f32)
            out_ref[...] = total.astype(bf16)
    for s, out_ref in enumerate(refs):
        total = ins[0][s].astype(f32)
        for ref in ins[1:]:
            total += ref[s].astype(f32)
        out_ref[...] = total.astype(bf16)


def sum_lines(pieces, near=()):
    chips, rows, width = pieces[0].shape
    towers = len(pieces)
    outs = chips + (towers if near else 0)
    out = pl.pallas_call(
        functools.partial(line_kernel, towers, rows, len(near) > 0),
        out_shape=[jax.ShapeDtypeStruct((rows, width), bf16)] * outs,
        compiler_params=params(32),
        cost_estimate=pl.CostEstimate(
            flops=4 * outs * rows * width,
            bytes_accessed=10 * outs * rows * width,
            transcendentals=0,
        ),
        name="partial_sums",
    )(*pieces, *near)
    return (out[:towers], out[towers:]) if near else out


def shards(query_hidden, passage_hidden, pool_hidden, query_proj, passage_proj, negative_ids):
    towers = lax.axis_size("tower")
    dp_size = lax.axis_size("dp")
    chips = dp_size // 2
    query_rows = query_hidden.shape[0]
    part_rows = query_rows // towers
    pool_rows = pool_hidden.shape[0]
    width = query_proj.shape[1]

    def moved(x, tower_step=0, place_step=0, core_step=0):
        pairs = []
        for source in range(towers * dp_size):
            t, d = divmod(source, dp_size)
            target = ((d // 2) ^ place_step) * 2 + ((d % 2) ^ core_step)
            pairs.append((source, (t ^ tower_step) * dp_size + target))
        return lax.ppermute(x, axes, pairs)

    ids = jnp.transpose(negative_ids)
    near_far = chips == group
    copies = towers * chips
    query_unit, part, head, rest = project_queries(query_hidden, query_proj, ids, part_rows)
    if near_far:
        parts = {s: moved(part, place_step=s) for s in [2, 3]}
        parts = [parts[s] for s in range(2, chips)]
    else:
        parts = [moved(part, place_step=s) for s in range(1, chips)]
    slabs = width // 128
    far = jnp.concatenate([x[: slabs * part_rows] for x in parts], axis=0)
    if near_far:
        next_head = moved(head, place_step=1)
        far, next_head = lax.optimization_barrier((far, next_head))
    spread = {d: moved(far, tower_step=d) for d in [1, 2, 3]}
    spread = [far] + [spread[d] for d in range(1, towers)]
    pool_hidden, part = lax.optimization_barrier((pool_hidden, part))
    items = project_items(pool_hidden, passage_hidden, passage_proj)
    sent_items, _ = lax.optimization_barrier((items, far))
    other = moved(sent_items, core_step=1)
    if near_far:
        sent_rest, _ = lax.optimization_barrier((rest, far))
        next_rest = moved(sent_rest, place_step=1)
        count = count_names([ids, next_head] + parts, pool_rows, group * query_rows)
        exps, near_totals, near_queries = score_near(
            query_unit, next_head, next_rest, items, other, count, query_rows, pool_rows
        )
        far_exps, totals, far_queries = score_far(
            spread, items, other, count, near_totals, query_rows, pool_rows, part_rows, copies
        )
        exps = [exps, far_exps]
        queries = [near_queries, far_queries]
    else:
        ids = [ids] + [ids_of(x[slabs * part_rows :]) for x in parts]
        count = count_names([jnp.concatenate(ids, axis=1)], pool_rows, group * query_rows)
        tower = lax.axis_index("tower")
        near = query_unit.reshape(1, towers, part_rows, width)
        blocks = jnp.stack(
            [
                jnp.moveaxis(x.reshape(chips - 1, slabs, part_rows, 128), 1, 2).reshape(
                    chips - 1, part_rows, width
                )
                for x in spread
            ],
            axis=1,
        )
        blocks = jnp.take(blocks, tower ^ jnp.arange(towers), axis=1)
        queries = jnp.concatenate([near, blocks], axis=0).reshape(-1, width)
        exps, totals = score_joined(
            queries, items, other, count, query_rows, pool_rows, copies
        )
        exps = [exps]
        queries = [queries]
        shift = lax.axis_index("dp") // 2 // group
        turned = shift ^ jnp.arange(chips // group)
        totals = totals.reshape(copies, 2, chips // group, -1)
        totals = jnp.take(totals, turned, axis=2).reshape(copies, 2, -1)
    same_core = [
        [t * dp_size + 2 * z + c for t in range(towers) for z in range(chips)] for c in range(2)
    ]
    totals = lax.all_to_all(totals, axes, 0, 0, axis_index_groups=same_core)
    if not near_far:
        totals = totals.reshape(copies, 2, chips // group, -1)
        totals = jnp.take(totals, turned, axis=2).reshape(copies, 2, -1)
    weights, *grads = weigh(
        totals, exps, items, other, query_rows, pool_rows, part_rows, towers
    )
    own_grad, sent_grad = item_gradients(weights, queries, query_rows, pool_rows)
    if near_far:
        near_grad, next_grad, *grads = grads
    far_sums = [moved(grads[d], tower_step=d) for d in [3, 2, 1]]
    sums = [grads[0]] + far_sums
    if near_far:
        plane, line = sum_lines(sums, (near_grad, moved(next_grad, place_step=1)))
        arrived = [moved(line[s - 2], place_step=s) for s in [3, 2]]
        arrived += [moved(plane[d], tower_step=d) for d in [3, 2, 1]]
        own_line = plane[0]
    else:
        line = sum_lines(sums)
        arrived = [moved(line[s], place_step=s) for s in range(1, chips)]
        own_line = line[0]
    sent_grad, own_line = lax.optimization_barrier((sent_grad, own_line))
    taken_grad = moved(sent_grad, core_step=1)
    pool_grad, passage_grad = join_gradients(own_grad, taken_grad, pool_rows)
    own_line, pool_grad = lax.optimization_barrier((own_line, pool_grad))
    query_grad = own_line.astype(f32)
    for x in arrived:
        query_grad = query_grad + x.astype(f32)
    return (query_grad.astype(bf16), passage_grad, pool_grad)


def solution(mesh):
    placed = (
        P("dp", None),
        P(("tower", "dp"), None),
        P(("tower", "dp"), None),
        P(),
        P(),
        P("dp", None),
    )
    return jax.shard_map(
        shards,
        mesh=mesh,
        in_specs=placed,
        out_specs=(P(("dp", "tower"), None), P(("tower", "dp"), None), P(("tower", "dp"), None)),
        check_vma=False,
    )
```

```python
import functools

import jax
import jax.numpy as jnp
from jax import lax
from jax.experimental import pallas as pl
from jax.experimental.pallas import tpu as pltpu
from jax.sharding import PartitionSpec as P

logit_scale = 50.0
axes = ("tower", "dp")
rank_order = [14, 10, 8, 15, 9, 4, 13, 11, 12, 1, 0, 3, 2, 6, 5, 7]
group = 4
f32 = jnp.float32
bf16 = jnp.bfloat16
last_last = (((1,), (1,)), ((), ()))
first_first = (((0,), (0,)), ((), ()))


def block_step(blocks):
    return pl.program_id(0) if blocks > 1 else 0


def grid_of(blocks, in_specs, out_specs):
    if blocks == 1:
        return {}
    return {"grid": (blocks,), "in_specs": in_specs, "out_specs": out_specs}


def params(mib):
    return pltpu.CompilerParams(vmem_limit_bytes=int(mib * 2**20))


def normalized(projected):
    squares = jnp.sum(projected * projected, axis=1, keepdims=True)
    return (projected * lax.rsqrt(squares + 1e-06)).astype(bf16)


def digits_of(ids):
    rows = ids.shape[1]
    full = rows // 128 * 128
    assert rows - full == 64 and full == 128
    high = ((ids >> 8) - 256).astype(f32)
    low = (ids & 255).astype(f32)
    last = jnp.concatenate([high[:, full:], low[:, full:]], axis=1)
    return jnp.concatenate([high[:, :full], low[:, :full], last], axis=0).astype(bf16)


def ids_of(digits):
    digits = digits.astype(f32).astype(jnp.int32)
    count = digits.shape[0] // 3
    last = digits[2 * count :]
    high = jnp.concatenate([digits[:count], last[:, :64]], axis=1)
    low = jnp.concatenate([digits[count : 2 * count], last[:, 64:]], axis=1)
    return ((high + 256) << 8) + low


def query_kernel(steps, part_rows, hidden_ref, weight_ref, ids_ref, unit_ref, part_ref, head_ref, rest_ref, hidden, weight, ids_near, sems, ids_sem):
    depth = weight.shape[0] // steps
    copies = []
    for k in range(steps):
        span = pl.ds(k * depth, depth)
        copies.append(
            (
                pltpu.make_async_copy(hidden_ref.at[:, span], hidden.at[:, span], sems.at[0, k]),
                pltpu.make_async_copy(weight_ref.at[span, :], weight.at[span, :], sems.at[1, k]),
            )
        )
    ids_copy = pltpu.make_async_copy(ids_ref, ids_near, ids_sem)
    ids_copy.start()
    for pair in copies:
        for copy in pair:
            copy.start()
    ids_copy.wait()
    digits = digits_of(ids_near[...])
    slabs = weight.shape[1] // 128
    part_ref[slabs * part_rows :, :] = digits
    head_rows = unit_ref.shape[0] - rest_ref.shape[0]
    head_ref[slabs * head_rows :, :] = digits
    total = None
    for k, pair in enumerate(copies):
        for copy in pair:
            copy.wait()
        span = slice(k * depth, (k + 1) * depth)
        product = jnp.dot(hidden[:, span], weight[span, :], preferred_element_type=f32)
        total = product if total is None else total + product
    unit_ref[...] = normalized(total)
    start = pl.multiple_of(lax.axis_index("tower") * part_rows, 16)
    rest_ref[...] = unit_ref[head_rows:, :]
    for k in range(slabs):
        head_ref[k * head_rows : (k + 1) * head_rows, :] = unit_ref[
            :head_rows, k * 128 : (k + 1) * 128
        ]
        part_ref[k * part_rows : (k + 1) * part_rows, :] = unit_ref[
            pl.ds(start, part_rows), k * 128 : (k + 1) * 128
        ]


def project_queries(hidden, weight, ids, part_rows):
    rows, depth = hidden.shape
    width = weight.shape[1]
    steps = 3
    extra = 3 * ids.shape[0]
    head = 1 * part_rows
    far = pl.BlockSpec(memory_space=pltpu.HBM)
    near = pl.BlockSpec(memory_space=pltpu.VMEM)
    return pl.pallas_call(
        functools.partial(query_kernel, steps, part_rows),
        in_specs=[far, far, far],
        out_specs=[near, near, near, near],
        out_shape=[
            jax.ShapeDtypeStruct((rows, width), bf16),
            jax.ShapeDtypeStruct((part_rows * width // 128 + extra, 128), bf16),
            jax.ShapeDtypeStruct((head * width // 128 + extra, 128), bf16),
            jax.ShapeDtypeStruct((rows - head, width), bf16),
        ],
        scratch_shapes=[
            pltpu.VMEM((rows, depth), bf16),
            pltpu.VMEM((depth, width), bf16),
            pltpu.VMEM(ids.shape, jnp.int32),
            pltpu.SemaphoreType.DMA((2, steps)),
            pltpu.SemaphoreType.DMA,
        ],
        compiler_params=params(24),
        cost_estimate=pl.CostEstimate(
            flops=16 * rows * depth * width,
            bytes_accessed=12 * depth * (rows + width),
            transcendentals=0,
        ),
        name="query_units",
    )(
        pltpu.with_memory_space_constraint(hidden, pltpu.HBM),
        pltpu.with_memory_space_constraint(weight, pltpu.HBM),
        pltpu.with_memory_space_constraint(ids, pltpu.HBM),
    )


def item_kernel(pool_ref, passage_ref, weight_ref, unit_ref):
    hidden = jnp.concatenate([pool_ref[...], passage_ref[...]], axis=0)
    unit_ref[...] = normalized(
        jnp.dot(hidden, weight_ref[...], preferred_element_type=f32)
    )


def project_items(pool, passage, weight):
    depth, width = weight.shape
    rows = pool.shape[0] + passage.shape[0]
    return pl.pallas_call(
        item_kernel,
        out_shape=jax.ShapeDtypeStruct((rows, width), bf16),
        compiler_params=params(24),
        cost_estimate=pl.CostEstimate(
            flops=2 * rows * depth * width,
            bytes_accessed=2 * depth * (rows + width),
            transcendentals=0,
        ),
        name="item_units",
    )(pool, passage, weight)


def count_kernel(pool_rows, extra, *refs):
    ids_ref, *digit_refs, count_ref = refs
    own = lax.axis_index("tower") * lax.axis_size("dp") + lax.axis_index("dp")
    ids = [ids_ref[...]]
    for ref in digit_refs:
        ids.append(ids_of(ref[-extra:, :]))
    ids = jnp.concatenate(ids, axis=1)
    neg_count, queries = ids.shape
    chunk = 64

    for half in range(2):
        base = (own ^ half) * pool_rows
        local = ids - base

        @pl.loop(0, pool_rows // chunk)
        def _(step):
            rows = lax.broadcasted_iota(jnp.int32, (chunk, queries), 0) + step * chunk
            count = jnp.zeros((chunk, queries), f32)
            for k in range(neg_count):
                count += jnp.where(rows == local[k : k + 1, :], 1.0, 0.0)
            start = pl.multiple_of(half * pool_rows + step * chunk, chunk)
            count_ref[pl.ds(start, chunk), :] = count.astype(bf16)


def count_names(pieces, pool_rows, block):
    neg_count, queries = pieces[0].shape
    if len(pieces) == 1:
        specs = [pl.BlockSpec((neg_count, block), lambda g: (0, g))]
    else:
        queries *= len(pieces)
        specs = [pl.BlockSpec(x.shape, lambda g: (0, 0)) for x in pieces]
    return pl.pallas_call(
        functools.partial(count_kernel, pool_rows, 3 * neg_count),
        out_shape=jax.ShapeDtypeStruct((2 * pool_rows, queries), bf16),
        **grid_of(
            queries // block, specs, pl.BlockSpec((2 * pool_rows, block), lambda g: (0, g))
        ),
        compiler_params=params(16),
        cost_estimate=pl.CostEstimate(
            flops=6 * queries * neg_count * pool_rows,
            bytes_accessed=4 * pool_rows * queries,
            transcendentals=0,
        ),
        name="name_counts",
    )(*pieces)


def positive_mask(query_rows, own_rows, half, first_lane, block, blocks):
    dp_size = lax.axis_size("dp")
    tower, dp = lax.axis_index("tower"), lax.axis_index("dp")
    lane = lax.broadcasted_iota(jnp.int32, (1, block), 1) + first_lane
    query = jnp.zeros((1, block), jnp.int32)
    for k in range(group):
        step = block_step(blocks) * group + k
        start = (((dp // 2) ^ step) * 2 + dp % 2) * query_rows
        query = jnp.where(
            (lane >= k * query_rows) & (lane < (k + 1) * query_rows),
            start + lane - k * query_rows,
            query,
        )
    first = (tower * dp_size + (dp ^ half)) * own_rows
    passage = lax.broadcasted_iota(jnp.int32, (own_rows, block), 0) + first
    return passage == query


def placed_totals(totals, query_rows):
    place = (lax.axis_index("dp") // 2) % group
    out = totals
    for k in range(1, group):
        turned = jnp.concatenate(
            [
                totals[:, (j ^ k) * query_rows : ((j ^ k) + 1) * query_rows]
                for j in range(group)
            ],
            axis=1,
        )
        out = jnp.where(place == k, turned, out)
    return out


def score_tile(
    items_refs, queries, count_ref, exp_ref, start, offset, query_rows, pool_rows, blocks
):
    chunk = queries.shape[0]
    own_rows = items_refs[0].shape[0] - pool_rows
    lanes = slice(start, start + chunk)
    hard = jnp.zeros((1, chunk), f32)
    batch = jnp.zeros((1, chunk), f32)
    for half, items_ref in enumerate(items_refs):
        scores = lax.dot_general(items_ref[...], queries, last_last, preferred_element_type=f32)
        exps = jnp.exp(logit_scale * scores)
        rows = slice(half * pool_rows, (half + 1) * pool_rows)
        named = exps[:pool_rows] * count_ref[
            rows, offset + start : offset + start + chunk
        ].astype(f32)
        hard += jnp.sum(named, axis=0, keepdims=True)
        exp_ref[rows, lanes] = named.astype(bf16)
        mask = positive_mask(query_rows, own_rows, half, offset + start, chunk, blocks)
        hard += jnp.sum(jnp.where(mask, exps[pool_rows:], 0.0), axis=0, keepdims=True)
        batch += jnp.sum(exps[pool_rows:], axis=0, keepdims=True)
        row = 2 * pool_rows + half * own_rows
        exp_ref[row : row + own_rows, lanes] = exps[pool_rows:].astype(bf16)
    return jnp.concatenate([batch, hard], axis=0)


def score_tiles(
    items_refs, queries_ref, count_ref, exp_ref, offset, query_rows, pool_rows, blocks
):
    block = queries_ref.shape[0]
    chunk = 256 if block % 256 == 0 else block
    sums = []
    for start in range(0, block, chunk):
        queries = queries_ref[start : start + chunk, :]
        sums.append(
            score_tile(
                items_refs,
                queries,
                count_ref,
                exp_ref,
                start,
                offset,
                query_rows,
                pool_rows,
                blocks,
            )
        )
    return jnp.concatenate(sums, axis=1)


def joined_kernel(blocks, copies, query_rows, pool_rows, queries_ref, own_ref, other_ref, count_ref, *outs):
    exp_ref, totals_ref = outs
    totals = score_tiles(
        (own_ref, other_ref), queries_ref, count_ref, exp_ref, 0, query_rows, pool_rows, blocks
    )
    totals = placed_totals(totals, query_rows)
    for k in range(copies):
        totals_ref[k] = totals


def far_kernel(copies, query_rows, pool_rows, part_rows, towers, *refs):
    far_refs, refs = refs[:towers], refs[towers:]
    own_ref, other_ref, count_ref, near_ref, exp_ref, totals_ref, queries_ref = refs
    tower = lax.axis_index("tower")
    slabs = queries_ref.shape[1] // 128
    for d in range(towers):
        for s in range(queries_ref.shape[0] // query_rows):
            start = pl.multiple_of(s * query_rows + (tower ^ d) * part_rows, 16)
            for k in range(slabs):
                queries_ref[pl.ds(start, part_rows), k * 128 : (k + 1) * 128] = far_refs[d][
                    (s * slabs + k) * part_rows : (s * slabs + k + 1) * part_rows, :
                ]
    items = (own_ref, other_ref)
    totals = score_tiles(
        items, queries_ref, count_ref, exp_ref, 2 * query_rows, query_rows, pool_rows, 1
    )
    totals = placed_totals(jnp.concatenate([near_ref[...], totals], axis=1), query_rows)
    for k in range(copies):
        totals_ref[k] = totals


def near_kernel(query_rows, pool_rows, *refs):
    unit_ref, head_ref, rest_ref, own_ref, other_ref, count_ref, exp_ref, totals_ref, queries = refs
    queries[:query_rows, :] = unit_ref[...]
    head_rows = query_rows - rest_ref.shape[0]
    for k in range(queries.shape[1] // 128):
        queries[query_rows : query_rows + head_rows, k * 128 : (k + 1) * 128] = head_ref[
            k * head_rows : (k + 1) * head_rows, :
        ]
    queries[query_rows + head_rows :, :] = rest_ref[...]
    totals_ref[...] = score_tiles(
        (own_ref, other_ref), queries, count_ref, exp_ref, 0, query_rows, pool_rows, 1
    )


def score_cost(rows, queries, width):
    return pl.CostEstimate(
        flops=2 * rows * queries * width,
        bytes_accessed=4 * rows * queries,
        transcendentals=rows * queries,
    )


def score_joined(queries, items, other, count, query_rows, pool_rows, copies):
    total, width = queries.shape
    block = group * query_rows
    rows = 2 * items.shape[0]
    whole = lambda x: pl.BlockSpec(x.shape, lambda g: (0, 0))
    return pl.pallas_call(
        functools.partial(joined_kernel, total // block, copies, query_rows, pool_rows),
        grid=(total // block,),
        in_specs=[
            pl.BlockSpec((block, width), lambda g: (g, 0)),
            whole(items),
            whole(other),
            pl.BlockSpec((2 * pool_rows, block), lambda g: (0, g)),
        ],
        out_specs=[
            pl.BlockSpec((rows, block), lambda g: (0, g)),
            pl.BlockSpec((copies, 2, block), lambda g: (0, 0, g)),
        ],
        out_shape=[
            jax.ShapeDtypeStruct((rows, total), bf16),
            jax.ShapeDtypeStruct((copies, 2, total), f32),
        ],
        compiler_params=params(40),
        cost_estimate=score_cost(rows, total, width),
        name="scores",
    )(queries, items, other, count)


def score_far(spread, items, other, count, near, query_rows, pool_rows, part_rows, copies):
    rows, width = 2 * items.shape[0], items.shape[1]
    queries = (group - 2) * query_rows
    return pl.pallas_call(
        functools.partial(far_kernel, copies, query_rows, pool_rows, part_rows, len(spread)),
        out_shape=[
            jax.ShapeDtypeStruct((rows, queries), bf16),
            jax.ShapeDtypeStruct((copies, 2, group * query_rows), f32),
            jax.ShapeDtypeStruct((queries, width), bf16),
        ],
        compiler_params=params(32),
        cost_estimate=score_cost(rows, queries, width),
        name="far_scores",
    )(*spread, items, other, count, near)


def score_near(unit, head, rest, items, other, count, query_rows, pool_rows):
    rows, width = 2 * items.shape[0], items.shape[1]
    queries = 2 * query_rows
    return pl.pallas_call(
        functools.partial(near_kernel, query_rows, pool_rows),
        out_shape=[
            jax.ShapeDtypeStruct((rows, queries), bf16),
            jax.ShapeDtypeStruct((2, queries), f32),
            jax.ShapeDtypeStruct((queries, width), bf16),
        ],
        compiler_params=params(32),
        cost_estimate=score_cost(rows, queries, width),
        name="near_scores",
    )(unit, head, rest, items, other, count)


def weight_kernel(blocks, exp_count, query_rows, pool_rows, own_rows, part_rows, towers, *refs):
    totals_ref, refs = refs[0], refs[1:]
    exp_refs, refs = refs[:exp_count], refs[exp_count:]
    own_ref, other_ref, weight_ref, *grad_refs = refs
    totals = placed_totals(jnp.sum(totals_ref[...], axis=0), query_rows)
    scale = logit_scale / totals
    pools = 2 * pool_rows
    first = 0
    for exp_ref in exp_refs:
        block = exp_ref.shape[1]
        lanes = slice(first, first + block)
        batch, hard = scale[0:1, lanes], scale[1:2, lanes]
        weight_ref[:pools, lanes] = (exp_ref[:pools, :].astype(f32) * hard).astype(bf16)
        for half in range(2):
            row = pools + half * own_rows
            exps = exp_ref[row : row + own_rows, :].astype(f32)
            mask = positive_mask(query_rows, own_rows, half, first, block, blocks)
            weight_ref[row : row + own_rows, lanes] = (
                exps * batch + jnp.where(mask, exps * hard - 2.0 * logit_scale, 0.0)
            ).astype(bf16)
        first += block
    tower = lax.axis_index("tower")
    items = jnp.concatenate(
        [
            own_ref[:pool_rows, :],
            other_ref[:pool_rows, :],
            own_ref[pool_rows:, :],
            other_ref[pool_rows:, :],
        ],
        axis=0,
    )
    grad = lax.dot_general(
        weight_ref[...], items, first_first, preferred_element_type=f32
    ).astype(bf16)
    if exp_count == 2:
        near_ref, next_ref, *grad_refs = grad_refs
        near_ref[...] = grad[:query_rows]
        next_ref[...] = grad[query_rows : 2 * query_rows]
        grad = grad[2 * query_rows :]
    grad = grad.reshape(-1, towers, part_rows, grad.shape[1])
    for t in range(towers):
        for d in range(towers):

            @pl.when((tower ^ d) == t)
            def _(t=t, d=d):
                grad_refs[d][...] = grad[:, t]


def weigh(totals, exps, items, other, query_rows, pool_rows, part_rows, towers):
    rows, width = items.shape
    queries = sum(x.shape[1] for x in exps)
    block = group * query_rows
    whole = lambda x: pl.BlockSpec(x.shape, lambda g: (0, 0))
    tall = pl.BlockSpec((2 * rows, block), lambda g: (0, g))
    near = pl.BlockSpec((query_rows, width), lambda g: (0, 0))
    if len(exps) == 1:
        exp_specs, out_specs, out_shape, sent = [tall], [], [], group
    else:
        exp_specs = [whole(x) for x in exps]
        out_specs = [near, near]
        out_shape = [jax.ShapeDtypeStruct((query_rows, width), bf16)] * 2
        sent = group - 2
    blocks = queries // block
    return pl.pallas_call(
        functools.partial(
            weight_kernel,
            blocks,
            len(exps),
            query_rows,
            pool_rows,
            rows - pool_rows,
            part_rows,
            towers,
        ),
        **grid_of(
            blocks,
            [pl.BlockSpec((totals.shape[0], 2, block), lambda g: (0, 0, g))]
            + exp_specs
            + [whole(items), whole(other)],
            [tall]
            + out_specs
            + [pl.BlockSpec((sent, part_rows, width), lambda g: (g, 0, 0))] * towers,
        ),
        out_shape=[jax.ShapeDtypeStruct((2 * rows, queries), bf16)]
        + out_shape
        + [jax.ShapeDtypeStruct((sent * blocks, part_rows, width), bf16)] * towers,
        compiler_params=params(40),
        cost_estimate=pl.CostEstimate(
            flops=4 * rows * queries * width,
            bytes_accessed=8 * rows * queries,
            transcendentals=0,
        ),
        name="weights",
    )(totals, *exps, items, other)


def gradient_kernel(steps, query_count, pool_rows, own_rows, weight_ref, *refs):
    query_refs, refs = refs[:query_count], refs[query_count:]
    own_ref, sent_ref, *scratch = refs
    step = block_step(steps)
    if len(query_refs) == 1:
        queries = query_refs[0][...]
    else:
        queries = jnp.concatenate([ref[...] for ref in query_refs], axis=0)
    product = jnp.dot(weight_ref[...], queries, preferred_element_type=f32)

    def finish(total):
        pools = 2 * pool_rows
        own_ref[:pool_rows, :] = total[:pool_rows, :]
        own_ref[pool_rows:, :] = total[pools : pools + own_rows, :]
        sent_ref[:pool_rows, :] = total[pool_rows:pools, :].astype(bf16)
        sent_ref[pool_rows:, :] = total[pools + own_rows :, :].astype(bf16)

    if steps == 1:
        finish(product)
        return
    (total,) = scratch

    @pl.when(step == 0)
    def _():
        total[...] = product

    @pl.when(step > 0)
    def _():
        total[...] += product

    @pl.when(step == steps - 1)
    def _():
        finish(total[...])


def item_gradients(weights, queries, query_rows, pool_rows):
    rows, total = weights.shape
    half = rows // 2
    width = queries[0].shape[1]
    block = group * query_rows
    blocks = total // block
    fixed = pl.BlockSpec((half, width), lambda g: (0, 0))
    if len(queries) == 1:
        query_specs = [pl.BlockSpec((block, width), lambda g: (g, 0))]
    else:
        query_specs = [pl.BlockSpec(x.shape, lambda g: (0, 0)) for x in queries]
    return pl.pallas_call(
        functools.partial(
            gradient_kernel, blocks, len(queries), pool_rows, half - pool_rows
        ),
        **grid_of(
            blocks,
            [pl.BlockSpec((rows, block), lambda g: (0, g))] + query_specs,
            [fixed, fixed],
        ),
        out_shape=[
            jax.ShapeDtypeStruct((half, width), f32),
            jax.ShapeDtypeStruct((half, width), bf16),
        ],
        scratch_shapes=[pltpu.VMEM((rows, width), f32)] if blocks > 1 else [],
        compiler_params=params(40),
        cost_estimate=pl.CostEstimate(
            flops=2 * rows * total * width, bytes_accessed=6 * rows * width, transcendentals=0
        ),
        name="item_gradients",
    )(weights, *queries)


def join_kernel(pool_rows, own_ref, taken_ref, pool_ref, passage_ref):
    grad = (own_ref[...] + taken_ref[...].astype(f32)).astype(bf16)
    pool_ref[...] = grad[:pool_rows]
    passage_ref[...] = grad[pool_rows:]


def join_gradients(own, taken, pool_rows):
    rows, width = own.shape
    return pl.pallas_call(
        functools.partial(join_kernel, pool_rows),
        out_shape=[
            jax.ShapeDtypeStruct((pool_rows, width), bf16),
            jax.ShapeDtypeStruct((rows - pool_rows, width), bf16),
        ],
        compiler_params=params(16),
        cost_estimate=pl.CostEstimate(
            flops=rows * width, bytes_accessed=8 * rows * width, transcendentals=0
        ),
        name="join_item_gradients",
    )(own, taken)


def line_kernel(towers, part_rows, near_far, *refs):
    ins, refs = refs[:towers], refs[towers:]
    if near_far:
        near_ref, arrived_ref, *refs = refs
        plane_refs, refs = refs[:towers], refs[towers:]
        tower = lax.axis_index("tower")
        for d, out_ref in enumerate(plane_refs):
            rows = pl.ds(pl.multiple_of((tower ^ d) * part_rows, 16), part_rows)
            total = near_ref[rows, :].astype(f32) + arrived_ref[rows, :].astype(f32)
            out_ref[...] = total.astype(bf16)
    for s, out_ref in enumerate(refs):
        total = ins[0][s].astype(f32)
        for ref in ins[1:]:
            total += ref[s].astype(f32)
        out_ref[...] = total.astype(bf16)


def sum_lines(pieces, near=()):
    chips, rows, width = pieces[0].shape
    towers = len(pieces)
    outs = chips + (towers if near else 0)
    out = pl.pallas_call(
        functools.partial(line_kernel, towers, rows, len(near) > 0),
        out_shape=[jax.ShapeDtypeStruct((rows, width), bf16)] * outs,
        compiler_params=params(32),
        cost_estimate=pl.CostEstimate(
            flops=4 * outs * rows * width,
            bytes_accessed=10 * outs * rows * width,
            transcendentals=0,
        ),
        name="partial_sums",
    )(*pieces, *near)
    return (out[:towers], out[towers:]) if near else out


def shards(query_hidden, passage_hidden, pool_hidden, query_proj, passage_proj, negative_ids):
    towers = lax.axis_size("tower")
    dp_size = lax.axis_size("dp")
    chips = dp_size // 2
    query_rows = query_hidden.shape[0]
    part_rows = query_rows // towers
    pool_rows = pool_hidden.shape[0]
    width = query_proj.shape[1]

    def moved(x, tower_step=0, place_step=0, core_step=0):
        pairs = []
        for source in range(towers * dp_size):
            t, d = divmod(source, dp_size)
            target = ((d // 2) ^ place_step) * 2 + ((d % 2) ^ core_step)
            pairs.append((source, (t ^ tower_step) * dp_size + target))
        return lax.ppermute(x, axes, pairs)

    ids = jnp.transpose(negative_ids)
    near_far = chips == group
    copies = towers * chips
    query_unit, part, head, rest = project_queries(query_hidden, query_proj, ids, part_rows)
    if near_far:
        parts = {s: moved(part, place_step=s) for s in [2, 3]}
        parts = [parts[s] for s in range(2, chips)]
    else:
        parts = [moved(part, place_step=s) for s in range(1, chips)]
    slabs = width // 128
    far = jnp.concatenate([x[: slabs * part_rows] for x in parts], axis=0)
    if near_far:
        next_head = moved(head, place_step=1)
        far, next_head = lax.optimization_barrier((far, next_head))
    spread = {d: moved(far, tower_step=d) for d in [1, 2, 3]}
    spread = [far] + [spread[d] for d in range(1, towers)]
    pool_hidden, part = lax.optimization_barrier((pool_hidden, part))
    items = project_items(pool_hidden, passage_hidden, passage_proj)
    sent_items, _ = lax.optimization_barrier((items, far))
    other = moved(sent_items, core_step=1)
    if near_far:
        sent_rest, _ = lax.optimization_barrier((rest, far))
        next_rest = moved(sent_rest, place_step=1)
        count = count_names([ids, next_head] + parts, pool_rows, group * query_rows)
        exps, near_totals, near_queries = score_near(
            query_unit, next_head, next_rest, items, other, count, query_rows, pool_rows
        )
        far_exps, totals, far_queries = score_far(
            spread, items, other, count, near_totals, query_rows, pool_rows, part_rows, copies
        )
        exps = [exps, far_exps]
        queries = [near_queries, far_queries]
    else:
        ids = [ids] + [ids_of(x[slabs * part_rows :]) for x in parts]
        count = count_names([jnp.concatenate(ids, axis=1)], pool_rows, group * query_rows)
        tower = lax.axis_index("tower")
        near = query_unit.reshape(1, towers, part_rows, width)
        blocks = jnp.stack(
            [
                jnp.moveaxis(x.reshape(chips - 1, slabs, part_rows, 128), 1, 2).reshape(
                    chips - 1, part_rows, width
                )
                for x in spread
            ],
            axis=1,
        )
        blocks = jnp.take(blocks, tower ^ jnp.arange(towers), axis=1)
        queries = jnp.concatenate([near, blocks], axis=0).reshape(-1, width)
        exps, totals = score_joined(
            queries, items, other, count, query_rows, pool_rows, copies
        )
        exps = [exps]
        queries = [queries]
        shift = lax.axis_index("dp") // 2 // group
        turned = shift ^ jnp.arange(chips // group)
        totals = totals.reshape(copies, 2, chips // group, -1)
        totals = jnp.take(totals, turned, axis=2).reshape(copies, 2, -1)
    ranks = list(reversed(range(copies)))
    if copies == len(rank_order):
        ranks = rank_order
    same_core = [
        [rank // chips * dp_size + 2 * (rank % chips) + c for rank in ranks] for c in range(2)
    ]
    totals = lax.all_to_all(totals, axes, 0, 0, axis_index_groups=same_core)
    if not near_far:
        totals = totals.reshape(copies, 2, chips // group, -1)
        totals = jnp.take(totals, turned, axis=2).reshape(copies, 2, -1)
    weights, *grads = weigh(
        totals, exps, items, other, query_rows, pool_rows, part_rows, towers
    )
    own_grad, sent_grad = item_gradients(weights, queries, query_rows, pool_rows)
    if near_far:
        near_grad, next_grad, *grads = grads
    far_sums = [moved(grads[d], tower_step=d) for d in [3, 2, 1]]
    sums = [grads[0]] + far_sums
    if near_far:
        plane, line = sum_lines(sums, (near_grad, moved(next_grad, place_step=1)))
        arrived = [moved(line[s - 2], place_step=s) for s in [3, 2]]
        arrived += [moved(plane[d], tower_step=d) for d in [3, 2, 1]]
        own_line = plane[0]
    else:
        line = sum_lines(sums)
        arrived = [moved(line[s], place_step=s) for s in range(1, chips)]
        own_line = line[0]
    sent_grad, own_line = lax.optimization_barrier((sent_grad, own_line))
    taken_grad = moved(sent_grad, core_step=1)
    pool_grad, passage_grad = join_gradients(own_grad, taken_grad, pool_rows)
    own_line, pool_grad = lax.optimization_barrier((own_line, pool_grad))
    query_grad = own_line.astype(f32)
    for x in arrived:
        query_grad = query_grad + x.astype(f32)
    return (query_grad.astype(bf16), passage_grad, pool_grad)


def solution(mesh):
    placed = (
        P("dp", None),
        P(("tower", "dp"), None),
        P(("tower", "dp"), None),
        P(),
        P(),
        P("dp", None),
    )
    return jax.shard_map(
        shards,
        mesh=mesh,
        in_specs=placed,
        out_specs=(P(("dp", "tower"), None), P(("tower", "dp"), None), P(("tower", "dp"), None)),
        check_vma=False,
    )
```

```python
import functools

import jax
import jax.numpy as jnp
from jax import lax
from jax.experimental import pallas as pl
from jax.experimental.pallas import tpu as pltpu
from jax.sharding import PartitionSpec as P

logit_scale = 50.0
axes = ("tower", "dp")
rank_order = [14, 10, 8, 15, 9, 4, 13, 11, 12, 1, 0, 3, 2, 6, 5, 7]
group = 4
f32 = jnp.float32
bf16 = jnp.bfloat16
last_last = (((1,), (1,)), ((), ()))
first_first = (((0,), (0,)), ((), ()))


def block_step(blocks):
    return pl.program_id(0) if blocks > 1 else 0


def grid_of(blocks, in_specs, out_specs):
    if blocks == 1:
        return {}
    return {"grid": (blocks,), "in_specs": in_specs, "out_specs": out_specs}


def params(mib):
    return pltpu.CompilerParams(vmem_limit_bytes=int(mib * 2**20))


def normalized(projected):
    squares = jnp.sum(projected * projected, axis=1, keepdims=True)
    return (projected * lax.rsqrt(squares + 1e-06)).astype(bf16)


def digits_of(ids):
    rows = ids.shape[1]
    full = rows // 128 * 128
    assert rows - full == 64 and full == 128
    high = ((ids >> 8) - 256).astype(f32)
    low = (ids & 255).astype(f32)
    last = jnp.concatenate([high[:, full:], low[:, full:]], axis=1)
    return jnp.concatenate([high[:, :full], low[:, :full], last], axis=0).astype(bf16)


def ids_of(digits):
    digits = digits.astype(f32).astype(jnp.int32)
    count = digits.shape[0] // 3
    last = digits[2 * count :]
    high = jnp.concatenate([digits[:count], last[:, :64]], axis=1)
    low = jnp.concatenate([digits[count : 2 * count], last[:, 64:]], axis=1)
    return ((high + 256) << 8) + low


def query_kernel(steps, part_rows, hidden_ref, weight_ref, ids_ref, unit_ref, part_ref, head_ref, rest_ref, hidden, weight, ids_near, sems, ids_sem):
    depth = weight.shape[0] // steps
    copies = []
    for k in range(steps):
        span = pl.ds(k * depth, depth)
        copies.append(
            (
                pltpu.make_async_copy(hidden_ref.at[:, span], hidden.at[:, span], sems.at[0, k]),
                pltpu.make_async_copy(weight_ref.at[span, :], weight.at[span, :], sems.at[1, k]),
            )
        )
    ids_copy = pltpu.make_async_copy(ids_ref, ids_near, ids_sem)
    ids_copy.start()
    for pair in copies:
        for copy in pair:
            copy.start()
    ids_copy.wait()
    digits = digits_of(ids_near[...])
    slabs = weight.shape[1] // 128
    part_ref[slabs * part_rows :, :] = digits
    head_rows = unit_ref.shape[0] - rest_ref.shape[0]
    head_ref[slabs * head_rows :, :] = digits
    total = None
    for k, pair in enumerate(copies):
        for copy in pair:
            copy.wait()
        span = slice(k * depth, (k + 1) * depth)
        product = jnp.dot(hidden[:, span], weight[span, :], preferred_element_type=f32)
        total = product if total is None else total + product
    unit_ref[...] = normalized(total)
    start = pl.multiple_of(lax.axis_index("tower") * part_rows, 16)
    rest_ref[...] = unit_ref[head_rows:, :]
    for k in range(slabs):
        head_ref[k * head_rows : (k + 1) * head_rows, :] = unit_ref[
            :head_rows, k * 128 : (k + 1) * 128
        ]
        part_ref[k * part_rows : (k + 1) * part_rows, :] = unit_ref[
            pl.ds(start, part_rows), k * 128 : (k + 1) * 128
        ]


def project_queries(hidden, weight, ids, part_rows):
    rows, depth = hidden.shape
    width = weight.shape[1]
    steps = 3
    extra = 3 * ids.shape[0]
    head = 1 * part_rows
    far = pl.BlockSpec(memory_space=pltpu.HBM)
    near = pl.BlockSpec(memory_space=pltpu.VMEM)
    return pl.pallas_call(
        functools.partial(query_kernel, steps, part_rows),
        in_specs=[far, far, far],
        out_specs=[near, near, near, near],
        out_shape=[
            jax.ShapeDtypeStruct((rows, width), bf16),
            jax.ShapeDtypeStruct((part_rows * width // 128 + extra, 128), bf16),
            jax.ShapeDtypeStruct((head * width // 128 + extra, 128), bf16),
            jax.ShapeDtypeStruct((rows - head, width), bf16),
        ],
        scratch_shapes=[
            pltpu.VMEM((rows, depth), bf16),
            pltpu.VMEM((depth, width), bf16),
            pltpu.VMEM(ids.shape, jnp.int32),
            pltpu.SemaphoreType.DMA((2, steps)),
            pltpu.SemaphoreType.DMA,
        ],
        compiler_params=params(24),
        cost_estimate=pl.CostEstimate(
            flops=16 * rows * depth * width,
            bytes_accessed=12 * depth * (rows + width),
            transcendentals=0,
        ),
        name="query_units",
    )(
        pltpu.with_memory_space_constraint(hidden, pltpu.HBM),
        pltpu.with_memory_space_constraint(weight, pltpu.HBM),
        pltpu.with_memory_space_constraint(ids, pltpu.HBM),
    )


def item_kernel(pool_ref, passage_ref, weight_ref, unit_ref):
    hidden = jnp.concatenate([pool_ref[...], passage_ref[...]], axis=0)
    unit_ref[...] = normalized(
        jnp.dot(hidden, weight_ref[...], preferred_element_type=f32)
    )


def project_items(pool, passage, weight):
    depth, width = weight.shape
    rows = pool.shape[0] + passage.shape[0]
    return pl.pallas_call(
        item_kernel,
        out_shape=jax.ShapeDtypeStruct((rows, width), bf16),
        compiler_params=params(24),
        cost_estimate=pl.CostEstimate(
            flops=2 * rows * depth * width,
            bytes_accessed=2 * depth * (rows + width),
            transcendentals=0,
        ),
        name="item_units",
    )(pool, passage, weight)


def count_kernel(pool_rows, extra, *refs):
    ids_ref, *digit_refs, count_ref = refs
    own = lax.axis_index("tower") * lax.axis_size("dp") + lax.axis_index("dp")
    ids = [ids_ref[...]]
    for ref in digit_refs:
        ids.append(ids_of(ref[-extra:, :]))
    ids = jnp.concatenate(ids, axis=1)
    neg_count, queries = ids.shape
    chunk = 64

    for half in range(2):
        base = (own ^ half) * pool_rows
        local = ids - base

        @pl.loop(0, pool_rows // chunk)
        def _(step):
            rows = lax.broadcasted_iota(jnp.int32, (chunk, queries), 0) + step * chunk
            count = jnp.zeros((chunk, queries), f32)
            for k in range(neg_count):
                count += jnp.where(rows == local[k : k + 1, :], 1.0, 0.0)
            start = pl.multiple_of(half * pool_rows + step * chunk, chunk)
            count_ref[pl.ds(start, chunk), :] = count.astype(bf16)


def count_names(pieces, pool_rows, block):
    neg_count, queries = pieces[0].shape
    if len(pieces) == 1:
        specs = [pl.BlockSpec((neg_count, block), lambda g: (0, g))]
    else:
        queries *= len(pieces)
        specs = [pl.BlockSpec(x.shape, lambda g: (0, 0)) for x in pieces]
    return pl.pallas_call(
        functools.partial(count_kernel, pool_rows, 3 * neg_count),
        out_shape=jax.ShapeDtypeStruct((2 * pool_rows, queries), bf16),
        **grid_of(
            queries // block, specs, pl.BlockSpec((2 * pool_rows, block), lambda g: (0, g))
        ),
        compiler_params=params(16),
        cost_estimate=pl.CostEstimate(
            flops=6 * queries * neg_count * pool_rows,
            bytes_accessed=4 * pool_rows * queries,
            transcendentals=0,
        ),
        name="name_counts",
    )(*pieces)


def positive_mask(query_rows, own_rows, half, first_lane, block, blocks):
    dp_size = lax.axis_size("dp")
    tower, dp = lax.axis_index("tower"), lax.axis_index("dp")
    lane = lax.broadcasted_iota(jnp.int32, (1, block), 1) + first_lane
    query = jnp.zeros((1, block), jnp.int32)
    for k in range(group):
        step = block_step(blocks) * group + k
        start = (((dp // 2) ^ step) * 2 + dp % 2) * query_rows
        query = jnp.where(
            (lane >= k * query_rows) & (lane < (k + 1) * query_rows),
            start + lane - k * query_rows,
            query,
        )
    first = (tower * dp_size + (dp ^ half)) * own_rows
    passage = lax.broadcasted_iota(jnp.int32, (own_rows, block), 0) + first
    return passage == query


def placed_totals(totals, query_rows):
    place = (lax.axis_index("dp") // 2) % group
    out = totals
    for k in range(1, group):
        turned = jnp.concatenate(
            [
                totals[:, (j ^ k) * query_rows : ((j ^ k) + 1) * query_rows]
                for j in range(group)
            ],
            axis=1,
        )
        out = jnp.where(place == k, turned, out)
    return out


def score_tile(
    items_refs, queries, count_ref, exp_ref, start, offset, query_rows, pool_rows, blocks
):
    chunk = queries.shape[0]
    own_rows = items_refs[0].shape[0] - pool_rows
    lanes = slice(start, start + chunk)
    hard = jnp.zeros((1, chunk), f32)
    batch = jnp.zeros((1, chunk), f32)
    for half, items_ref in enumerate(items_refs):
        scores = lax.dot_general(items_ref[...], queries, last_last, preferred_element_type=f32)
        exps = jnp.exp(logit_scale * scores)
        rows = slice(half * pool_rows, (half + 1) * pool_rows)
        named = exps[:pool_rows] * count_ref[
            rows, offset + start : offset + start + chunk
        ].astype(f32)
        hard += jnp.sum(named, axis=0, keepdims=True)
        exp_ref[rows, lanes] = named.astype(bf16)
        mask = positive_mask(query_rows, own_rows, half, offset + start, chunk, blocks)
        hard += jnp.sum(jnp.where(mask, exps[pool_rows:], 0.0), axis=0, keepdims=True)
        batch += jnp.sum(exps[pool_rows:], axis=0, keepdims=True)
        row = 2 * pool_rows + half * own_rows
        exp_ref[row : row + own_rows, lanes] = exps[pool_rows:].astype(bf16)
    return jnp.concatenate([batch, hard], axis=0)


def score_tiles(
    items_refs, queries_ref, count_ref, exp_ref, offset, query_rows, pool_rows, blocks
):
    block = queries_ref.shape[0]
    chunk = 256 if block % 256 == 0 else block
    sums = []
    for start in range(0, block, chunk):
        queries = queries_ref[start : start + chunk, :]
        sums.append(
            score_tile(
                items_refs,
                queries,
                count_ref,
                exp_ref,
                start,
                offset,
                query_rows,
                pool_rows,
                blocks,
            )
        )
    return jnp.concatenate(sums, axis=1)


def joined_kernel(blocks, copies, query_rows, pool_rows, queries_ref, own_ref, other_ref, count_ref, *outs):
    exp_ref, totals_ref = outs
    totals = score_tiles(
        (own_ref, other_ref), queries_ref, count_ref, exp_ref, 0, query_rows, pool_rows, blocks
    )
    totals = placed_totals(totals, query_rows)
    for k in range(copies):
        totals_ref[k] = totals


def far_kernel(copies, query_rows, pool_rows, part_rows, towers, *refs):
    far_refs, refs = refs[:towers], refs[towers:]
    own_ref, other_ref, count_ref, near_ref, exp_ref, totals_ref, queries_ref = refs
    tower = lax.axis_index("tower")
    slabs = queries_ref.shape[1] // 128
    for d in range(towers):
        for s in range(queries_ref.shape[0] // query_rows):
            start = pl.multiple_of(s * query_rows + (tower ^ d) * part_rows, 16)
            for k in range(slabs):
                queries_ref[pl.ds(start, part_rows), k * 128 : (k + 1) * 128] = far_refs[d][
                    (s * slabs + k) * part_rows : (s * slabs + k + 1) * part_rows, :
                ]
    items = (own_ref, other_ref)
    totals = score_tiles(
        items, queries_ref, count_ref, exp_ref, 2 * query_rows, query_rows, pool_rows, 1
    )
    totals = placed_totals(jnp.concatenate([near_ref[...], totals], axis=1), query_rows)
    for k in range(copies):
        totals_ref[k] = totals


def near_kernel(query_rows, pool_rows, *refs):
    unit_ref, head_ref, rest_ref, own_ref, other_ref, count_ref, exp_ref, totals_ref, queries = refs
    queries[:query_rows, :] = unit_ref[...]
    head_rows = query_rows - rest_ref.shape[0]
    for k in range(queries.shape[1] // 128):
        queries[query_rows : query_rows + head_rows, k * 128 : (k + 1) * 128] = head_ref[
            k * head_rows : (k + 1) * head_rows, :
        ]
    queries[query_rows + head_rows :, :] = rest_ref[...]
    totals_ref[...] = score_tiles(
        (own_ref, other_ref), queries, count_ref, exp_ref, 0, query_rows, pool_rows, 1
    )


def score_cost(rows, queries, width):
    return pl.CostEstimate(
        flops=2 * rows * queries * width,
        bytes_accessed=4 * rows * queries,
        transcendentals=rows * queries,
    )


def score_joined(queries, items, other, count, query_rows, pool_rows, copies):
    total, width = queries.shape
    block = group * query_rows
    rows = 2 * items.shape[0]
    whole = lambda x: pl.BlockSpec(x.shape, lambda g: (0, 0))
    return pl.pallas_call(
        functools.partial(joined_kernel, total // block, copies, query_rows, pool_rows),
        grid=(total // block,),
        in_specs=[
            pl.BlockSpec((block, width), lambda g: (g, 0)),
            whole(items),
            whole(other),
            pl.BlockSpec((2 * pool_rows, block), lambda g: (0, g)),
        ],
        out_specs=[
            pl.BlockSpec((rows, block), lambda g: (0, g)),
            pl.BlockSpec((copies, 2, block), lambda g: (0, 0, g)),
        ],
        out_shape=[
            jax.ShapeDtypeStruct((rows, total), bf16),
            jax.ShapeDtypeStruct((copies, 2, total), f32),
        ],
        compiler_params=params(40),
        cost_estimate=score_cost(rows, total, width),
        name="scores",
    )(queries, items, other, count)


def score_far(spread, items, other, count, near, query_rows, pool_rows, part_rows, copies):
    rows, width = 2 * items.shape[0], items.shape[1]
    queries = (group - 2) * query_rows
    return pl.pallas_call(
        functools.partial(far_kernel, copies, query_rows, pool_rows, part_rows, len(spread)),
        out_shape=[
            jax.ShapeDtypeStruct((rows, queries), bf16),
            jax.ShapeDtypeStruct((copies, 2, group * query_rows), f32),
            jax.ShapeDtypeStruct((queries, width), bf16),
        ],
        compiler_params=params(32),
        cost_estimate=score_cost(rows, queries, width),
        name="far_scores",
    )(*spread, items, other, count, near)


def score_near(unit, head, rest, items, other, count, query_rows, pool_rows):
    rows, width = 2 * items.shape[0], items.shape[1]
    queries = 2 * query_rows
    return pl.pallas_call(
        functools.partial(near_kernel, query_rows, pool_rows),
        out_shape=[
            jax.ShapeDtypeStruct((rows, queries), bf16),
            jax.ShapeDtypeStruct((2, queries), f32),
            jax.ShapeDtypeStruct((queries, width), bf16),
        ],
        compiler_params=params(32),
        cost_estimate=score_cost(rows, queries, width),
        name="near_scores",
    )(unit, head, rest, items, other, count)


def weight_kernel(blocks, exp_count, query_rows, pool_rows, own_rows, part_rows, towers, *refs):
    totals_ref, refs = refs[0], refs[1:]
    exp_refs, refs = refs[:exp_count], refs[exp_count:]
    own_ref, other_ref, weight_ref, *grad_refs = refs
    totals = placed_totals(jnp.sum(totals_ref[...], axis=0), query_rows)
    scale = logit_scale / totals
    pools = 2 * pool_rows
    first = 0
    for exp_ref in exp_refs:
        block = exp_ref.shape[1]
        lanes = slice(first, first + block)
        batch, hard = scale[0:1, lanes], scale[1:2, lanes]
        weight_ref[:pools, lanes] = (exp_ref[:pools, :].astype(f32) * hard).astype(bf16)
        for half in range(2):
            row = pools + half * own_rows
            exps = exp_ref[row : row + own_rows, :].astype(f32)
            mask = positive_mask(query_rows, own_rows, half, first, block, blocks)
            weight_ref[row : row + own_rows, lanes] = (
                exps * batch + jnp.where(mask, exps * hard - 2.0 * logit_scale, 0.0)
            ).astype(bf16)
        first += block
    tower = lax.axis_index("tower")
    items = jnp.concatenate(
        [
            own_ref[:pool_rows, :],
            other_ref[:pool_rows, :],
            own_ref[pool_rows:, :],
            other_ref[pool_rows:, :],
        ],
        axis=0,
    )
    grad = lax.dot_general(
        weight_ref[...], items, first_first, preferred_element_type=f32
    ).astype(bf16)
    if exp_count == 2:
        near_ref, next_ref, *grad_refs = grad_refs
        near_ref[...] = grad[:query_rows]
        next_ref[...] = grad[query_rows : 2 * query_rows]
        grad = grad[2 * query_rows :]
    grad = grad.reshape(-1, towers, part_rows, grad.shape[1])
    for t in range(towers):
        for d in range(towers):

            @pl.when((tower ^ d) == t)
            def _(t=t, d=d):
                grad_refs[d][...] = grad[:, t]


def weigh(totals, exps, items, other, query_rows, pool_rows, part_rows, towers):
    rows, width = items.shape
    queries = sum(x.shape[1] for x in exps)
    block = group * query_rows
    whole = lambda x: pl.BlockSpec(x.shape, lambda g: (0, 0))
    tall = pl.BlockSpec((2 * rows, block), lambda g: (0, g))
    near = pl.BlockSpec((query_rows, width), lambda g: (0, 0))
    if len(exps) == 1:
        exp_specs, out_specs, out_shape, sent = [tall], [], [], group
    else:
        exp_specs = [whole(x) for x in exps]
        out_specs = [near, near]
        out_shape = [jax.ShapeDtypeStruct((query_rows, width), bf16)] * 2
        sent = group - 2
    blocks = queries // block
    return pl.pallas_call(
        functools.partial(
            weight_kernel,
            blocks,
            len(exps),
            query_rows,
            pool_rows,
            rows - pool_rows,
            part_rows,
            towers,
        ),
        **grid_of(
            blocks,
            [pl.BlockSpec((totals.shape[0], 2, block), lambda g: (0, 0, g))]
            + exp_specs
            + [whole(items), whole(other)],
            [tall]
            + out_specs
            + [pl.BlockSpec((sent, part_rows, width), lambda g: (g, 0, 0))] * towers,
        ),
        out_shape=[jax.ShapeDtypeStruct((2 * rows, queries), bf16)]
        + out_shape
        + [jax.ShapeDtypeStruct((sent * blocks, part_rows, width), bf16)] * towers,
        compiler_params=params(40),
        cost_estimate=pl.CostEstimate(
            flops=4 * rows * queries * width,
            bytes_accessed=8 * rows * queries,
            transcendentals=0,
        ),
        name="weights",
    )(totals, *exps, items, other)


def gradient_kernel(steps, query_count, pool_rows, own_rows, weight_ref, *refs):
    query_refs, refs = refs[:query_count], refs[query_count:]
    own_ref, sent_ref, *scratch = refs
    step = block_step(steps)
    if len(query_refs) == 1:
        queries = query_refs[0][...]
    else:
        queries = jnp.concatenate([ref[...] for ref in query_refs], axis=0)
    product = jnp.dot(weight_ref[...], queries, preferred_element_type=f32)

    def finish(total):
        pools = 2 * pool_rows
        own_ref[:pool_rows, :] = total[:pool_rows, :]
        own_ref[pool_rows:, :] = total[pools : pools + own_rows, :]
        sent_ref[:pool_rows, :] = total[pool_rows:pools, :].astype(bf16)
        sent_ref[pool_rows:, :] = total[pools + own_rows :, :].astype(bf16)

    if steps == 1:
        finish(product)
        return
    (total,) = scratch

    @pl.when(step == 0)
    def _():
        total[...] = product

    @pl.when(step > 0)
    def _():
        total[...] += product

    @pl.when(step == steps - 1)
    def _():
        finish(total[...])


def item_gradients(weights, queries, query_rows, pool_rows):
    rows, total = weights.shape
    half = rows // 2
    width = queries[0].shape[1]
    block = group * query_rows
    blocks = total // block
    fixed = pl.BlockSpec((half, width), lambda g: (0, 0))
    if len(queries) == 1:
        query_specs = [pl.BlockSpec((block, width), lambda g: (g, 0))]
    else:
        query_specs = [pl.BlockSpec(x.shape, lambda g: (0, 0)) for x in queries]
    return pl.pallas_call(
        functools.partial(
            gradient_kernel, blocks, len(queries), pool_rows, half - pool_rows
        ),
        **grid_of(
            blocks,
            [pl.BlockSpec((rows, block), lambda g: (0, g))] + query_specs,
            [fixed, fixed],
        ),
        out_shape=[
            jax.ShapeDtypeStruct((half, width), f32),
            jax.ShapeDtypeStruct((half, width), bf16),
        ],
        scratch_shapes=[pltpu.VMEM((rows, width), f32)] if blocks > 1 else [],
        compiler_params=params(40),
        cost_estimate=pl.CostEstimate(
            flops=2 * rows * total * width, bytes_accessed=6 * rows * width, transcendentals=0
        ),
        name="item_gradients",
    )(weights, *queries)


def join_kernel(pool_rows, own_ref, taken_ref, pool_ref, passage_ref):
    grad = (own_ref[...] + taken_ref[...].astype(f32)).astype(bf16)
    pool_ref[...] = grad[:pool_rows]
    passage_ref[...] = grad[pool_rows:]


def join_gradients(own, taken, pool_rows):
    rows, width = own.shape
    return pl.pallas_call(
        functools.partial(join_kernel, pool_rows),
        out_shape=[
            jax.ShapeDtypeStruct((pool_rows, width), bf16),
            jax.ShapeDtypeStruct((rows - pool_rows, width), bf16),
        ],
        compiler_params=params(16),
        cost_estimate=pl.CostEstimate(
            flops=rows * width, bytes_accessed=8 * rows * width, transcendentals=0
        ),
        name="join_item_gradients",
    )(own, taken)


def line_kernel(towers, part_rows, near_far, *refs):
    ins, refs = refs[:towers], refs[towers:]
    if near_far:
        near_ref, arrived_ref, *refs = refs
        plane_refs, refs = refs[:towers], refs[towers:]
        tower = lax.axis_index("tower")
        for d, out_ref in enumerate(plane_refs):
            rows = pl.ds(pl.multiple_of((tower ^ d) * part_rows, 16), part_rows)
            total = near_ref[rows, :].astype(f32) + arrived_ref[rows, :].astype(f32)
            out_ref[...] = total.astype(bf16)
    for s, out_ref in enumerate(refs):
        total = ins[0][s].astype(f32)
        for ref in ins[1:]:
            total += ref[s].astype(f32)
        out_ref[...] = total.astype(bf16)


def sum_lines(pieces, near=()):
    chips, rows, width = pieces[0].shape
    towers = len(pieces)
    outs = chips + (towers if near else 0)
    out = pl.pallas_call(
        functools.partial(line_kernel, towers, rows, len(near) > 0),
        out_shape=[jax.ShapeDtypeStruct((rows, width), bf16)] * outs,
        compiler_params=params(32),
        cost_estimate=pl.CostEstimate(
            flops=4 * outs * rows * width,
            bytes_accessed=10 * outs * rows * width,
            transcendentals=0,
        ),
        name="partial_sums",
    )(*pieces, *near)
    return (out[:towers], out[towers:]) if near else out


def shards(query_hidden, passage_hidden, pool_hidden, query_proj, passage_proj, negative_ids):
    towers = lax.axis_size("tower")
    dp_size = lax.axis_size("dp")
    chips = dp_size // 2
    query_rows = query_hidden.shape[0]
    part_rows = query_rows // towers
    pool_rows = pool_hidden.shape[0]
    width = query_proj.shape[1]

    def moved(x, tower_step=0, place_step=0, core_step=0):
        pairs = []
        for source in range(towers * dp_size):
            t, d = divmod(source, dp_size)
            target = ((d // 2) ^ place_step) * 2 + ((d % 2) ^ core_step)
            pairs.append((source, (t ^ tower_step) * dp_size + target))
        return lax.ppermute(x, axes, pairs)

    ids = jnp.transpose(negative_ids)
    near_far = chips == group
    copies = towers * chips
    query_unit, part, head, rest = project_queries(query_hidden, query_proj, ids, part_rows)
    if near_far:
        parts = {s: moved(part, place_step=s) for s in [2, 3]}
        parts = [parts[s] for s in range(2, chips)]
    else:
        parts = [moved(part, place_step=s) for s in range(1, chips)]
    slabs = width // 128
    far = jnp.concatenate([x[: slabs * part_rows] for x in parts], axis=0)
    if near_far:
        next_head = moved(head, place_step=1)
        far, next_head = lax.optimization_barrier((far, next_head))
    spread = {d: moved(far, tower_step=d) for d in [2, 1, 3]}
    spread = [far] + [spread[d] for d in range(1, towers)]
    pool_hidden, part = lax.optimization_barrier((pool_hidden, part))
    items = project_items(pool_hidden, passage_hidden, passage_proj)
    sent_items, _ = lax.optimization_barrier((items, far))
    other = moved(sent_items, core_step=1)
    if near_far:
        sent_rest, _ = lax.optimization_barrier((rest, far))
        next_rest = moved(sent_rest, place_step=1)
        count = count_names([ids, next_head] + parts, pool_rows, group * query_rows)
        exps, near_totals, near_queries = score_near(
            query_unit, next_head, next_rest, items, other, count, query_rows, pool_rows
        )
        far_exps, totals, far_queries = score_far(
            spread, items, other, count, near_totals, query_rows, pool_rows, part_rows, copies
        )
        exps = [exps, far_exps]
        queries = [near_queries, far_queries]
    else:
        ids = [ids] + [ids_of(x[slabs * part_rows :]) for x in parts]
        count = count_names([jnp.concatenate(ids, axis=1)], pool_rows, group * query_rows)
        tower = lax.axis_index("tower")
        near = query_unit.reshape(1, towers, part_rows, width)
        blocks = jnp.stack(
            [
                jnp.moveaxis(x.reshape(chips - 1, slabs, part_rows, 128), 1, 2).reshape(
                    chips - 1, part_rows, width
                )
                for x in spread
            ],
            axis=1,
        )
        blocks = jnp.take(blocks, tower ^ jnp.arange(towers), axis=1)
        queries = jnp.concatenate([near, blocks], axis=0).reshape(-1, width)
        exps, totals = score_joined(
            queries, items, other, count, query_rows, pool_rows, copies
        )
        exps = [exps]
        queries = [queries]
        shift = lax.axis_index("dp") // 2 // group
        turned = shift ^ jnp.arange(chips // group)
        totals = totals.reshape(copies, 2, chips // group, -1)
        totals = jnp.take(totals, turned, axis=2).reshape(copies, 2, -1)
    ranks = list(reversed(range(copies)))
    if copies == len(rank_order):
        ranks = rank_order
    same_core = [
        [rank // chips * dp_size + 2 * (rank % chips) + c for rank in ranks] for c in range(2)
    ]
    totals = lax.all_to_all(totals, axes, 0, 0, axis_index_groups=same_core)
    if not near_far:
        totals = totals.reshape(copies, 2, chips // group, -1)
        totals = jnp.take(totals, turned, axis=2).reshape(copies, 2, -1)
    weights, *grads = weigh(
        totals, exps, items, other, query_rows, pool_rows, part_rows, towers
    )
    own_grad, sent_grad = item_gradients(weights, queries, query_rows, pool_rows)
    if near_far:
        near_grad, next_grad, *grads = grads
    far_sums = [moved(grads[d], tower_step=d) for d in [3, 2, 1]]
    sums = [grads[0]] + far_sums
    if near_far:
        plane, line = sum_lines(sums, (near_grad, moved(next_grad, place_step=1)))
        arrived = [moved(line[s - 2], place_step=s) for s in [3, 2]]
        arrived += [moved(plane[d], tower_step=d) for d in [3, 2, 1]]
        own_line = plane[0]
    else:
        line = sum_lines(sums)
        arrived = [moved(line[s], place_step=s) for s in range(1, chips)]
        own_line = line[0]
    sent_grad, own_line = lax.optimization_barrier((sent_grad, own_line))
    taken_grad = moved(sent_grad, core_step=1)
    pool_grad, passage_grad = join_gradients(own_grad, taken_grad, pool_rows)
    own_line, pool_grad = lax.optimization_barrier((own_line, pool_grad))
    query_grad = own_line.astype(f32)
    for x in arrived:
        query_grad = query_grad + x.astype(f32)
    return (query_grad.astype(bf16), passage_grad, pool_grad)


def solution(mesh):
    placed = (
        P("dp", None),
        P(("tower", "dp"), None),
        P(("tower", "dp"), None),
        P(),
        P(),
        P("dp", None),
    )
    return jax.shard_map(
        shards,
        mesh=mesh,
        in_specs=placed,
        out_specs=(P(("dp", "tower"), None), P(("tower", "dp"), None), P(("tower", "dp"), None)),
        check_vma=False,
    )
```

```python
import functools

import jax
import jax.numpy as jnp
from jax import lax
from jax.experimental import pallas as pl
from jax.experimental.pallas import tpu as pltpu
from jax.sharding import PartitionSpec as P

logit_scale = 50.0
axes = ("tower", "dp")
rank_order = [14, 4, 6, 0, 8, 7, 5, 1, 10, 11, 15, 3, 2, 9, 13, 12]
group = 4
f32 = jnp.float32
bf16 = jnp.bfloat16
last_last = (((1,), (1,)), ((), ()))
first_first = (((0,), (0,)), ((), ()))


def block_step(blocks):
    return pl.program_id(0) if blocks > 1 else 0


def grid_of(blocks, in_specs, out_specs):
    if blocks == 1:
        return {}
    return {"grid": (blocks,), "in_specs": in_specs, "out_specs": out_specs}


def params(mib):
    return pltpu.CompilerParams(vmem_limit_bytes=int(mib * 2**20))


def normalized(projected):
    squares = jnp.sum(projected * projected, axis=1, keepdims=True)
    return (projected * lax.rsqrt(squares + 1e-06)).astype(bf16)


def digits_of(ids):
    rows = ids.shape[1]
    full = rows // 128 * 128
    assert rows - full == 64 and full == 128
    high = ((ids >> 8) - 256).astype(f32)
    low = (ids & 255).astype(f32)
    last = jnp.concatenate([high[:, full:], low[:, full:]], axis=1)
    return jnp.concatenate([high[:, :full], low[:, :full], last], axis=0).astype(bf16)


def ids_of(digits):
    digits = digits.astype(f32).astype(jnp.int32)
    count = digits.shape[0] // 3
    last = digits[2 * count :]
    high = jnp.concatenate([digits[:count], last[:, :64]], axis=1)
    low = jnp.concatenate([digits[count : 2 * count], last[:, 64:]], axis=1)
    return ((high + 256) << 8) + low


def query_kernel(steps, part_rows, hidden_ref, weight_ref, ids_ref, unit_ref, part_ref, head_ref, rest_ref, hidden, weight, ids_near, sems, ids_sem):
    depth = weight.shape[0] // steps
    copies = []
    for k in range(steps):
        span = pl.ds(k * depth, depth)
        copies.append(
            (
                pltpu.make_async_copy(hidden_ref.at[:, span], hidden.at[:, span], sems.at[0, k]),
                pltpu.make_async_copy(weight_ref.at[span, :], weight.at[span, :], sems.at[1, k]),
            )
        )
    ids_copy = pltpu.make_async_copy(ids_ref, ids_near, ids_sem)
    ids_copy.start()
    for pair in copies:
        for copy in pair:
            copy.start()
    ids_copy.wait()
    digits = digits_of(ids_near[...])
    slabs = weight.shape[1] // 128
    part_ref[slabs * part_rows :, :] = digits
    head_rows = unit_ref.shape[0] - rest_ref.shape[0]
    head_ref[slabs * head_rows :, :] = digits
    total = None
    for k, pair in enumerate(copies):
        for copy in pair:
            copy.wait()
        span = slice(k * depth, (k + 1) * depth)
        product = jnp.dot(hidden[:, span], weight[span, :], preferred_element_type=f32)
        total = product if total is None else total + product
    unit_ref[...] = normalized(total)
    start = pl.multiple_of(lax.axis_index("tower") * part_rows, 16)
    rest_ref[...] = unit_ref[head_rows:, :]
    for k in range(slabs):
        head_ref[k * head_rows : (k + 1) * head_rows, :] = unit_ref[
            :head_rows, k * 128 : (k + 1) * 128
        ]
        part_ref[k * part_rows : (k + 1) * part_rows, :] = unit_ref[
            pl.ds(start, part_rows), k * 128 : (k + 1) * 128
        ]


def project_queries(hidden, weight, ids, part_rows):
    rows, depth = hidden.shape
    width = weight.shape[1]
    steps = 3
    extra = 3 * ids.shape[0]
    head = 1 * part_rows
    far = pl.BlockSpec(memory_space=pltpu.HBM)
    near = pl.BlockSpec(memory_space=pltpu.VMEM)
    return pl.pallas_call(
        functools.partial(query_kernel, steps, part_rows),
        in_specs=[far, far, far],
        out_specs=[near, near, near, near],
        out_shape=[
            jax.ShapeDtypeStruct((rows, width), bf16),
            jax.ShapeDtypeStruct((part_rows * width // 128 + extra, 128), bf16),
            jax.ShapeDtypeStruct((head * width // 128 + extra, 128), bf16),
            jax.ShapeDtypeStruct((rows - head, width), bf16),
        ],
        scratch_shapes=[
            pltpu.VMEM((rows, depth), bf16),
            pltpu.VMEM((depth, width), bf16),
            pltpu.VMEM(ids.shape, jnp.int32),
            pltpu.SemaphoreType.DMA((2, steps)),
            pltpu.SemaphoreType.DMA,
        ],
        compiler_params=params(24),
        cost_estimate=pl.CostEstimate(
            flops=16 * rows * depth * width,
            bytes_accessed=12 * depth * (rows + width),
            transcendentals=0,
        ),
        name="query_units",
    )(
        pltpu.with_memory_space_constraint(hidden, pltpu.HBM),
        pltpu.with_memory_space_constraint(weight, pltpu.HBM),
        pltpu.with_memory_space_constraint(ids, pltpu.HBM),
    )


def item_kernel(pool_ref, passage_ref, weight_ref, unit_ref):
    hidden = jnp.concatenate([pool_ref[...], passage_ref[...]], axis=0)
    unit_ref[...] = normalized(
        jnp.dot(hidden, weight_ref[...], preferred_element_type=f32)
    )


def project_items(pool, passage, weight):
    depth, width = weight.shape
    rows = pool.shape[0] + passage.shape[0]
    return pl.pallas_call(
        item_kernel,
        out_shape=jax.ShapeDtypeStruct((rows, width), bf16),
        compiler_params=params(24),
        cost_estimate=pl.CostEstimate(
            flops=2 * rows * depth * width,
            bytes_accessed=2 * depth * (rows + width),
            transcendentals=0,
        ),
        name="item_units",
    )(pool, passage, weight)


def count_kernel(pool_rows, extra, *refs):
    ids_ref, *digit_refs, count_ref = refs
    own = lax.axis_index("tower") * lax.axis_size("dp") + lax.axis_index("dp")
    ids = [ids_ref[...]]
    for ref in digit_refs:
        ids.append(ids_of(ref[-extra:, :]))
    ids = jnp.concatenate(ids, axis=1)
    neg_count, queries = ids.shape
    chunk = 64

    for half in range(2):
        base = (own ^ half) * pool_rows
        local = ids - base

        @pl.loop(0, pool_rows // chunk)
        def _(step):
            rows = lax.broadcasted_iota(jnp.int32, (chunk, queries), 0) + step * chunk
            count = jnp.zeros((chunk, queries), f32)
            for k in range(neg_count):
                count += jnp.where(rows == local[k : k + 1, :], 1.0, 0.0)
            start = pl.multiple_of(half * pool_rows + step * chunk, chunk)
            count_ref[pl.ds(start, chunk), :] = count.astype(bf16)


def count_names(pieces, pool_rows, block):
    neg_count, queries = pieces[0].shape
    if len(pieces) == 1:
        specs = [pl.BlockSpec((neg_count, block), lambda g: (0, g))]
    else:
        queries *= len(pieces)
        specs = [pl.BlockSpec(x.shape, lambda g: (0, 0)) for x in pieces]
    return pl.pallas_call(
        functools.partial(count_kernel, pool_rows, 3 * neg_count),
        out_shape=jax.ShapeDtypeStruct((2 * pool_rows, queries), bf16),
        **grid_of(
            queries // block, specs, pl.BlockSpec((2 * pool_rows, block), lambda g: (0, g))
        ),
        compiler_params=params(16),
        cost_estimate=pl.CostEstimate(
            flops=6 * queries * neg_count * pool_rows,
            bytes_accessed=4 * pool_rows * queries,
            transcendentals=0,
        ),
        name="name_counts",
    )(*pieces)


def positive_mask(query_rows, own_rows, half, first_lane, block, blocks):
    dp_size = lax.axis_size("dp")
    tower, dp = lax.axis_index("tower"), lax.axis_index("dp")
    lane = lax.broadcasted_iota(jnp.int32, (1, block), 1) + first_lane
    query = jnp.zeros((1, block), jnp.int32)
    for k in range(group):
        step = block_step(blocks) * group + k
        start = (((dp // 2) ^ step) * 2 + dp % 2) * query_rows
        query = jnp.where(
            (lane >= k * query_rows) & (lane < (k + 1) * query_rows),
            start + lane - k * query_rows,
            query,
        )
    first = (tower * dp_size + (dp ^ half)) * own_rows
    passage = lax.broadcasted_iota(jnp.int32, (own_rows, block), 0) + first
    return passage == query


def placed_totals(totals, query_rows):
    place = (lax.axis_index("dp") // 2) % group
    out = totals
    for k in range(1, group):
        turned = jnp.concatenate(
            [
                totals[:, (j ^ k) * query_rows : ((j ^ k) + 1) * query_rows]
                for j in range(group)
            ],
            axis=1,
        )
        out = jnp.where(place == k, turned, out)
    return out


def score_tile(
    items_refs, queries, count_ref, exp_ref, start, offset, query_rows, pool_rows, blocks
):
    chunk = queries.shape[0]
    own_rows = items_refs[0].shape[0] - pool_rows
    lanes = slice(start, start + chunk)
    hard = jnp.zeros((1, chunk), f32)
    batch = jnp.zeros((1, chunk), f32)
    for half, items_ref in enumerate(items_refs):
        scores = lax.dot_general(items_ref[...], queries, last_last, preferred_element_type=f32)
        exps = jnp.exp(logit_scale * scores)
        rows = slice(half * pool_rows, (half + 1) * pool_rows)
        named = exps[:pool_rows] * count_ref[
            rows, offset + start : offset + start + chunk
        ].astype(f32)
        hard += jnp.sum(named, axis=0, keepdims=True)
        exp_ref[rows, lanes] = named.astype(bf16)
        mask = positive_mask(query_rows, own_rows, half, offset + start, chunk, blocks)
        hard += jnp.sum(jnp.where(mask, exps[pool_rows:], 0.0), axis=0, keepdims=True)
        batch += jnp.sum(exps[pool_rows:], axis=0, keepdims=True)
        row = 2 * pool_rows + half * own_rows
        exp_ref[row : row + own_rows, lanes] = exps[pool_rows:].astype(bf16)
    return jnp.concatenate([batch, hard], axis=0)


def score_tiles(
    items_refs, queries_ref, count_ref, exp_ref, offset, query_rows, pool_rows, blocks
):
    block = queries_ref.shape[0]
    chunk = 256 if block % 256 == 0 else block
    sums = []
    for start in range(0, block, chunk):
        queries = queries_ref[start : start + chunk, :]
        sums.append(
            score_tile(
                items_refs,
                queries,
                count_ref,
                exp_ref,
                start,
                offset,
                query_rows,
                pool_rows,
                blocks,
            )
        )
    return jnp.concatenate(sums, axis=1)


def joined_kernel(blocks, copies, query_rows, pool_rows, queries_ref, own_ref, other_ref, count_ref, *outs):
    exp_ref, totals_ref = outs
    totals = score_tiles(
        (own_ref, other_ref), queries_ref, count_ref, exp_ref, 0, query_rows, pool_rows, blocks
    )
    totals = placed_totals(totals, query_rows)
    for k in range(copies):
        totals_ref[k] = totals


def far_kernel(copies, query_rows, pool_rows, part_rows, towers, *refs):
    far_refs, refs = refs[:towers], refs[towers:]
    own_ref, other_ref, count_ref, near_ref, exp_ref, totals_ref, queries_ref = refs
    tower = lax.axis_index("tower")
    slabs = queries_ref.shape[1] // 128
    for d in range(towers):
        for s in range(queries_ref.shape[0] // query_rows):
            start = pl.multiple_of(s * query_rows + (tower ^ d) * part_rows, 16)
            for k in range(slabs):
                queries_ref[pl.ds(start, part_rows), k * 128 : (k + 1) * 128] = far_refs[d][
                    (s * slabs + k) * part_rows : (s * slabs + k + 1) * part_rows, :
                ]
    items = (own_ref, other_ref)
    totals = score_tiles(
        items, queries_ref, count_ref, exp_ref, 2 * query_rows, query_rows, pool_rows, 1
    )
    totals = placed_totals(jnp.concatenate([near_ref[...], totals], axis=1), query_rows)
    for k in range(copies):
        totals_ref[k] = totals


def near_kernel(query_rows, pool_rows, *refs):
    unit_ref, head_ref, rest_ref, own_ref, other_ref, count_ref, exp_ref, totals_ref, queries = refs
    queries[:query_rows, :] = unit_ref[...]
    head_rows = query_rows - rest_ref.shape[0]
    for k in range(queries.shape[1] // 128):
        queries[query_rows : query_rows + head_rows, k * 128 : (k + 1) * 128] = head_ref[
            k * head_rows : (k + 1) * head_rows, :
        ]
    queries[query_rows + head_rows :, :] = rest_ref[...]
    totals_ref[...] = score_tiles(
        (own_ref, other_ref), queries, count_ref, exp_ref, 0, query_rows, pool_rows, 1
    )


def score_cost(rows, queries, width):
    return pl.CostEstimate(
        flops=2 * rows * queries * width,
        bytes_accessed=4 * rows * queries,
        transcendentals=rows * queries,
    )


def score_joined(queries, items, other, count, query_rows, pool_rows, copies):
    total, width = queries.shape
    block = group * query_rows
    rows = 2 * items.shape[0]
    whole = lambda x: pl.BlockSpec(x.shape, lambda g: (0, 0))
    return pl.pallas_call(
        functools.partial(joined_kernel, total // block, copies, query_rows, pool_rows),
        grid=(total // block,),
        in_specs=[
            pl.BlockSpec((block, width), lambda g: (g, 0)),
            whole(items),
            whole(other),
            pl.BlockSpec((2 * pool_rows, block), lambda g: (0, g)),
        ],
        out_specs=[
            pl.BlockSpec((rows, block), lambda g: (0, g)),
            pl.BlockSpec((copies, 2, block), lambda g: (0, 0, g)),
        ],
        out_shape=[
            jax.ShapeDtypeStruct((rows, total), bf16),
            jax.ShapeDtypeStruct((copies, 2, total), f32),
        ],
        compiler_params=params(40),
        cost_estimate=score_cost(rows, total, width),
        name="scores",
    )(queries, items, other, count)


def score_far(spread, items, other, count, near, query_rows, pool_rows, part_rows, copies):
    rows, width = 2 * items.shape[0], items.shape[1]
    queries = (group - 2) * query_rows
    return pl.pallas_call(
        functools.partial(far_kernel, copies, query_rows, pool_rows, part_rows, len(spread)),
        out_shape=[
            jax.ShapeDtypeStruct((rows, queries), bf16),
            jax.ShapeDtypeStruct((copies, 2, group * query_rows), f32),
            jax.ShapeDtypeStruct((queries, width), bf16),
        ],
        compiler_params=params(32),
        cost_estimate=score_cost(rows, queries, width),
        name="far_scores",
    )(*spread, items, other, count, near)


def score_near(unit, head, rest, items, other, count, query_rows, pool_rows):
    rows, width = 2 * items.shape[0], items.shape[1]
    queries = 2 * query_rows
    return pl.pallas_call(
        functools.partial(near_kernel, query_rows, pool_rows),
        out_shape=[
            jax.ShapeDtypeStruct((rows, queries), bf16),
            jax.ShapeDtypeStruct((2, queries), f32),
            jax.ShapeDtypeStruct((queries, width), bf16),
        ],
        compiler_params=params(32),
        cost_estimate=score_cost(rows, queries, width),
        name="near_scores",
    )(unit, head, rest, items, other, count)


def weight_kernel(blocks, exp_count, query_rows, pool_rows, own_rows, part_rows, towers, *refs):
    totals_ref, refs = refs[0], refs[1:]
    exp_refs, refs = refs[:exp_count], refs[exp_count:]
    own_ref, other_ref, weight_ref, *grad_refs = refs
    totals = placed_totals(jnp.sum(totals_ref[...], axis=0), query_rows)
    scale = logit_scale / totals
    pools = 2 * pool_rows
    first = 0
    for exp_ref in exp_refs:
        block = exp_ref.shape[1]
        lanes = slice(first, first + block)
        batch, hard = scale[0:1, lanes], scale[1:2, lanes]
        weight_ref[:pools, lanes] = (exp_ref[:pools, :].astype(f32) * hard).astype(bf16)
        for half in range(2):
            row = pools + half * own_rows
            exps = exp_ref[row : row + own_rows, :].astype(f32)
            mask = positive_mask(query_rows, own_rows, half, first, block, blocks)
            weight_ref[row : row + own_rows, lanes] = (
                exps * batch + jnp.where(mask, exps * hard - 2.0 * logit_scale, 0.0)
            ).astype(bf16)
        first += block
    tower = lax.axis_index("tower")
    items = jnp.concatenate(
        [
            own_ref[:pool_rows, :],
            other_ref[:pool_rows, :],
            own_ref[pool_rows:, :],
            other_ref[pool_rows:, :],
        ],
        axis=0,
    )
    grad = lax.dot_general(
        weight_ref[...], items, first_first, preferred_element_type=f32
    ).astype(bf16)
    if exp_count == 2:
        near_ref, next_ref, *grad_refs = grad_refs
        near_ref[...] = grad[:query_rows]
        next_ref[...] = grad[query_rows : 2 * query_rows]
        grad = grad[2 * query_rows :]
    grad = grad.reshape(-1, towers, part_rows, grad.shape[1])
    for t in range(towers):
        for d in range(towers):

            @pl.when((tower ^ d) == t)
            def _(t=t, d=d):
                grad_refs[d][...] = grad[:, t]


def weigh(totals, exps, items, other, query_rows, pool_rows, part_rows, towers):
    rows, width = items.shape
    queries = sum(x.shape[1] for x in exps)
    block = group * query_rows
    whole = lambda x: pl.BlockSpec(x.shape, lambda g: (0, 0))
    tall = pl.BlockSpec((2 * rows, block), lambda g: (0, g))
    near = pl.BlockSpec((query_rows, width), lambda g: (0, 0))
    if len(exps) == 1:
        exp_specs, out_specs, out_shape, sent = [tall], [], [], group
    else:
        exp_specs = [whole(x) for x in exps]
        out_specs = [near, near]
        out_shape = [jax.ShapeDtypeStruct((query_rows, width), bf16)] * 2
        sent = group - 2
    blocks = queries // block
    return pl.pallas_call(
        functools.partial(
            weight_kernel,
            blocks,
            len(exps),
            query_rows,
            pool_rows,
            rows - pool_rows,
            part_rows,
            towers,
        ),
        **grid_of(
            blocks,
            [pl.BlockSpec((totals.shape[0], 2, block), lambda g: (0, 0, g))]
            + exp_specs
            + [whole(items), whole(other)],
            [tall]
            + out_specs
            + [pl.BlockSpec((sent, part_rows, width), lambda g: (g, 0, 0))] * towers,
        ),
        out_shape=[jax.ShapeDtypeStruct((2 * rows, queries), bf16)]
        + out_shape
        + [jax.ShapeDtypeStruct((sent * blocks, part_rows, width), bf16)] * towers,
        compiler_params=params(40),
        cost_estimate=pl.CostEstimate(
            flops=4 * rows * queries * width,
            bytes_accessed=8 * rows * queries,
            transcendentals=0,
        ),
        name="weights",
    )(totals, *exps, items, other)


def gradient_kernel(steps, query_count, pool_rows, own_rows, weight_ref, *refs):
    query_refs, refs = refs[:query_count], refs[query_count:]
    own_ref, sent_ref, *scratch = refs
    step = block_step(steps)
    if len(query_refs) == 1:
        queries = query_refs[0][...]
    else:
        queries = jnp.concatenate([ref[...] for ref in query_refs], axis=0)
    product = jnp.dot(weight_ref[...], queries, preferred_element_type=f32)

    def finish(total):
        pools = 2 * pool_rows
        own_ref[:pool_rows, :] = total[:pool_rows, :]
        own_ref[pool_rows:, :] = total[pools : pools + own_rows, :]
        sent_ref[:pool_rows, :] = total[pool_rows:pools, :].astype(bf16)
        sent_ref[pool_rows:, :] = total[pools + own_rows :, :].astype(bf16)

    if steps == 1:
        finish(product)
        return
    (total,) = scratch

    @pl.when(step == 0)
    def _():
        total[...] = product

    @pl.when(step > 0)
    def _():
        total[...] += product

    @pl.when(step == steps - 1)
    def _():
        finish(total[...])


def item_gradients(weights, queries, query_rows, pool_rows):
    rows, total = weights.shape
    half = rows // 2
    width = queries[0].shape[1]
    block = group * query_rows
    blocks = total // block
    fixed = pl.BlockSpec((half, width), lambda g: (0, 0))
    if len(queries) == 1:
        query_specs = [pl.BlockSpec((block, width), lambda g: (g, 0))]
    else:
        query_specs = [pl.BlockSpec(x.shape, lambda g: (0, 0)) for x in queries]
    return pl.pallas_call(
        functools.partial(
            gradient_kernel, blocks, len(queries), pool_rows, half - pool_rows
        ),
        **grid_of(
            blocks,
            [pl.BlockSpec((rows, block), lambda g: (0, g))] + query_specs,
            [fixed, fixed],
        ),
        out_shape=[
            jax.ShapeDtypeStruct((half, width), f32),
            jax.ShapeDtypeStruct((half, width), bf16),
        ],
        scratch_shapes=[pltpu.VMEM((rows, width), f32)] if blocks > 1 else [],
        compiler_params=params(40),
        cost_estimate=pl.CostEstimate(
            flops=2 * rows * total * width, bytes_accessed=6 * rows * width, transcendentals=0
        ),
        name="item_gradients",
    )(weights, *queries)


def join_kernel(pool_rows, own_ref, taken_ref, pool_ref, passage_ref):
    grad = (own_ref[...] + taken_ref[...].astype(f32)).astype(bf16)
    pool_ref[...] = grad[:pool_rows]
    passage_ref[...] = grad[pool_rows:]


def join_gradients(own, taken, pool_rows):
    rows, width = own.shape
    return pl.pallas_call(
        functools.partial(join_kernel, pool_rows),
        out_shape=[
            jax.ShapeDtypeStruct((pool_rows, width), bf16),
            jax.ShapeDtypeStruct((rows - pool_rows, width), bf16),
        ],
        compiler_params=params(16),
        cost_estimate=pl.CostEstimate(
            flops=rows * width, bytes_accessed=8 * rows * width, transcendentals=0
        ),
        name="join_item_gradients",
    )(own, taken)


def line_kernel(towers, part_rows, near_far, *refs):
    ins, refs = refs[:towers], refs[towers:]
    if near_far:
        near_ref, arrived_ref, *refs = refs
        plane_refs, refs = refs[:towers], refs[towers:]
        tower = lax.axis_index("tower")
        for d, out_ref in enumerate(plane_refs):
            rows = pl.ds(pl.multiple_of((tower ^ d) * part_rows, 16), part_rows)
            total = near_ref[rows, :].astype(f32) + arrived_ref[rows, :].astype(f32)
            out_ref[...] = total.astype(bf16)
    for s, out_ref in enumerate(refs):
        total = ins[0][s].astype(f32)
        for ref in ins[1:]:
            total += ref[s].astype(f32)
        out_ref[...] = total.astype(bf16)


def sum_lines(pieces, near=()):
    chips, rows, width = pieces[0].shape
    towers = len(pieces)
    outs = chips + (towers if near else 0)
    out = pl.pallas_call(
        functools.partial(line_kernel, towers, rows, len(near) > 0),
        out_shape=[jax.ShapeDtypeStruct((rows, width), bf16)] * outs,
        compiler_params=params(32),
        cost_estimate=pl.CostEstimate(
            flops=4 * outs * rows * width,
            bytes_accessed=10 * outs * rows * width,
            transcendentals=0,
        ),
        name="partial_sums",
    )(*pieces, *near)
    return (out[:towers], out[towers:]) if near else out


def shards(query_hidden, passage_hidden, pool_hidden, query_proj, passage_proj, negative_ids):
    towers = lax.axis_size("tower")
    dp_size = lax.axis_size("dp")
    chips = dp_size // 2
    query_rows = query_hidden.shape[0]
    part_rows = query_rows // towers
    pool_rows = pool_hidden.shape[0]
    width = query_proj.shape[1]

    def moved(x, tower_step=0, place_step=0, core_step=0):
        pairs = []
        for source in range(towers * dp_size):
            t, d = divmod(source, dp_size)
            target = ((d // 2) ^ place_step) * 2 + ((d % 2) ^ core_step)
            pairs.append((source, (t ^ tower_step) * dp_size + target))
        return lax.ppermute(x, axes, pairs)

    ids = jnp.transpose(negative_ids)
    near_far = chips == group
    copies = towers * chips
    query_unit, part, head, rest = project_queries(query_hidden, query_proj, ids, part_rows)
    if near_far:
        parts = {s: moved(part, place_step=s) for s in [2, 3]}
        parts = [parts[s] for s in range(2, chips)]
    else:
        parts = [moved(part, place_step=s) for s in range(1, chips)]
    slabs = width // 128
    far = jnp.concatenate([x[: slabs * part_rows] for x in parts], axis=0)
    if near_far:
        next_head = moved(head, place_step=1)
        far, next_head = lax.optimization_barrier((far, next_head))
    spread = {d: moved(far, tower_step=d) for d in [1, 2, 3]}
    spread = [far] + [spread[d] for d in range(1, towers)]
    pool_hidden, part = lax.optimization_barrier((pool_hidden, part))
    items = project_items(pool_hidden, passage_hidden, passage_proj)
    sent_items, _ = lax.optimization_barrier((items, far))
    other = moved(sent_items, core_step=1)
    if near_far:
        sent_rest, _ = lax.optimization_barrier((rest, far))
        next_rest = moved(sent_rest, place_step=1)
        count = count_names([ids, next_head] + parts, pool_rows, group * query_rows)
        exps, near_totals, near_queries = score_near(
            query_unit, next_head, next_rest, items, other, count, query_rows, pool_rows
        )
        far_exps, totals, far_queries = score_far(
            spread, items, other, count, near_totals, query_rows, pool_rows, part_rows, copies
        )
        exps = [exps, far_exps]
        queries = [near_queries, far_queries]
    else:
        ids = [ids] + [ids_of(x[slabs * part_rows :]) for x in parts]
        count = count_names([jnp.concatenate(ids, axis=1)], pool_rows, group * query_rows)
        tower = lax.axis_index("tower")
        near = query_unit.reshape(1, towers, part_rows, width)
        blocks = jnp.stack(
            [
                jnp.moveaxis(x.reshape(chips - 1, slabs, part_rows, 128), 1, 2).reshape(
                    chips - 1, part_rows, width
                )
                for x in spread
            ],
            axis=1,
        )
        blocks = jnp.take(blocks, tower ^ jnp.arange(towers), axis=1)
        queries = jnp.concatenate([near, blocks], axis=0).reshape(-1, width)
        exps, totals = score_joined(
            queries, items, other, count, query_rows, pool_rows, copies
        )
        exps = [exps]
        queries = [queries]
        shift = lax.axis_index("dp") // 2 // group
        turned = shift ^ jnp.arange(chips // group)
        totals = totals.reshape(copies, 2, chips // group, -1)
        totals = jnp.take(totals, turned, axis=2).reshape(copies, 2, -1)
    ranks = list(reversed(range(copies)))
    if copies == len(rank_order):
        ranks = rank_order
    same_core = [
        [rank // chips * dp_size + 2 * (rank % chips) + c for rank in ranks] for c in range(2)
    ]
    totals = lax.all_to_all(totals, axes, 0, 0, axis_index_groups=same_core)
    if not near_far:
        totals = totals.reshape(copies, 2, chips // group, -1)
        totals = jnp.take(totals, turned, axis=2).reshape(copies, 2, -1)
    weights, *grads = weigh(
        totals, exps, items, other, query_rows, pool_rows, part_rows, towers
    )
    own_grad, sent_grad = item_gradients(weights, queries, query_rows, pool_rows)
    if near_far:
        near_grad, next_grad, *grads = grads
    far_sums = [moved(grads[d], tower_step=d) for d in [3, 2, 1]]
    sums = [grads[0]] + far_sums
    if near_far:
        plane, line = sum_lines(sums, (near_grad, moved(next_grad, place_step=1)))
        arrived = [moved(line[s - 2], place_step=s) for s in [3, 2]]
        arrived += [moved(plane[d], tower_step=d) for d in [3, 2, 1]]
        own_line = plane[0]
    else:
        line = sum_lines(sums)
        arrived = [moved(line[s], place_step=s) for s in range(1, chips)]
        own_line = line[0]
    sent_grad, own_line = lax.optimization_barrier((sent_grad, own_line))
    taken_grad = moved(sent_grad, core_step=1)
    pool_grad, passage_grad = join_gradients(own_grad, taken_grad, pool_rows)
    own_line, pool_grad = lax.optimization_barrier((own_line, pool_grad))
    query_grad = own_line.astype(f32)
    for x in arrived:
        query_grad = query_grad + x.astype(f32)
    return (query_grad.astype(bf16), passage_grad, pool_grad)


def solution(mesh):
    placed = (
        P("dp", None),
        P(("tower", "dp"), None),
        P(("tower", "dp"), None),
        P(),
        P(),
        P("dp", None),
    )
    return jax.shard_map(
        shards,
        mesh=mesh,
        in_specs=placed,
        out_specs=(P(("dp", "tower"), None), P(("tower", "dp"), None), P(("tower", "dp"), None)),
        check_vma=False,
    )
```
